32 devices in a mesh: expert: 8 (over z, core), tensor: 4 (over y, x).
Axes of the slice: x: 2, y: 2, z: 4, core: 2. Of those that a mesh axis runs over, the one named last changes fastest.
Arguments:
- inputs: bfloat16 [12288, 1024], P(('expert', 'tensor')), may hold values from -6 to 6
- attn_gain: bfloat16 [1024], replicated, may hold values from 0.25 to 1.75
- w_query: bfloat16 [1024, 1024], replicated, may hold values from -0.1875 to 0.1875
- w_key: bfloat16 [1024, 1024], replicated, may hold values from -0.1875 to 0.1875
- w_value: bfloat16 [1024, 1024], replicated, may hold values from -0.1875 to 0.1875
- w_proj: bfloat16 [1024, 1024], replicated, may hold values from -1 to 1
- rel_bias: bfloat16 [32, 16], replicated, may hold values from -4 to 4
- moe_gain: bfloat16 [1024], replicated, may hold values from 0.25 to 1.75
- w_router: bfloat16 [1024, 16], replicated, may hold values from -0.119628906 to 0.119628906
- w_gate: bfloat16 [16, 1024, 2816], P('expert', None, 'tensor'), may hold values from -0.1875 to 0.1875
- w_up: bfloat16 [16, 1024, 2816], P('expert', None, 'tensor'), may hold values from -0.1875 to 0.1875
- w_down: bfloat16 [16, 2816, 1024], P('expert', 'tensor'), may hold values from -2.5 to 2.5
- routes: int32 [12288, 2], P(('expert', 'tensor')), may hold values from 0 to 15, all different within a row
- long_buckets: int32 [2047], replicated, may hold values from 0 to 31
- short_buckets: int32 [255], replicated, may hold values from 0 to 31
- long_lens: int32 [8], P('expert'), may hold values from 769 to 1024, as said below
- short_lens: int32 [32], P(('expert', 'tensor')), may hold values from 64 to 128, as said below
- cotangent: bfloat16 [12288, 1024], P(('expert', 'tensor')), may hold values from -6 to 6
Outputs:
- outputs: bfloat16 [12288, 1024], P(('expert', 'tensor'))
- inputs_grad: float32 [12288, 1024], P(('expert', 'tensor'))
- attn_gain_grad: float32 [1024], replicated
- w_query_grad: float32 [1024, 1024], replicated
- w_key_grad: float32 [1024, 1024], replicated
- w_value_grad: float32 [1024, 1024], replicated
- w_proj_grad: float32 [1024, 1024], replicated
- rel_bias_grad: float32 [32, 16], replicated
- moe_gain_grad: float32 [1024], replicated
- w_router_grad: float32 [1024, 16], replicated
- w_gate_grad: float32 [16, 1024, 2816], P('expert', None, 'tensor')
- w_up_grad: float32 [16, 1024, 2816], P('expert', None, 'tensor')
- w_down_grad: float32 [16, 2816, 1024], P('expert', 'tensor')
The draws below stay inside these ranges and needn't reach their ends.
Inputs may be any that keep to these rules, and one draw needn't show every extreme that they name: `routes`: the two experts of a token differ. `long_lens`: some long sequence has all 1024 tokens valid. `short_lens`: some short sequence has all 128 tokens valid.
All inputs are finite; a program needn't handle non-finite values.
Results may differ from the reference program's by a relative error of at most 0.019.
Values may be sent and summed in bfloat16 or wider, within the bound.
No kernel may reach another device: no remote copies, remote signals or barrier semaphores. Data moves between devices by JAX's collectives and lax.ppermute only.
A program may use at most 448 MiB of HBM per device.

```python
import math
import jax
import jax.numpy as jnp
from jax import lax

D = 1024
HEADS = 16
HEAD_DIM = 64
FF = 2816
BUCKETS = 32
TOPK = 2
SHORT = 128
SHORT_SEQS = 1
EXPERTS = 16
LONG = 1024
LONG_DEV = 256
TOK_DEV = 384
TOKENS = 12288
LONG_SEQS = 8
SHORT_TOTAL = 32
CAP = 60
N_TENSOR = 4
DEVICES = 32


def draw_long_lens(key, part):
    key = jax.random.fold_in(key, 11)
    first, second = jax.random.split(key)
    lengths = jax.random.randint(first, (LONG_SEQS,), LONG - LONG_DEV + 1, LONG + 1)
    chosen = jax.random.randint(second, (), 0, LONG_SEQS)
    return jnp.where(jnp.arange(LONG_SEQS) == chosen, LONG, lengths).astype(jnp.int32)


def draw_short_lens(key, part):
    key = jax.random.fold_in(key, 12)
    first, second = jax.random.split(key)
    lengths = jax.random.randint(first, (SHORT_TOTAL,), SHORT // 2, SHORT + 1)
    chosen = jax.random.randint(second, (), 0, SHORT_TOTAL)
    return jnp.where(jnp.arange(SHORT_TOTAL) == chosen, SHORT, lengths).astype(jnp.int32)


def plant(values, stream_key, least, high):
    place = [jax.random.randint(jax.random.fold_in(stream_key, axis), (), 0, length) for axis, length in enumerate(values.shape)]
    widest = values.shape.index(max(values.shape))
    next_to = place[:widest] + [(place[widest] + 1) % values.shape[widest]] + place[widest + 1:]
    return values.at[tuple(place)].set(least).at[tuple(next_to)].set(high)


def block_scale(key, shape, shards, least, largest):
    level, own = 1.0, jax.random.fold_in(key, 6)
    for dim, blocks in shards:
        steps = jnp.exp(jax.random.uniform(jax.random.fold_in(own, dim), (blocks,), jnp.float32, least / len(shards), largest / len(shards)))
        level = level * jnp.repeat(steps, shape[dim] // blocks).reshape([-1 if axis == dim else 1 for axis in range(len(shape))])
    return level


def distinct(rng, rows, count, top, lift):
    sequence = jax.random.permutation(jax.random.fold_in(rng, 1), count)
    pull = sequence
    for power in range(3):
        pull = pull * pull // count
    pull = pull * lift // count
    tickets = jax.random.randint(jax.random.fold_in(rng, 2), (rows, count), 0, 4096) + pull
    fixed_rows = jax.random.permutation(jax.random.fold_in(rng, 3), rows)[jnp.arange(count) % rows]
    tickets = jnp.where(jnp.arange(rows)[:, None] == fixed_rows[None, :], 1 << 14, tickets)
    merit = tickets * count + jnp.arange(count)
    return lax.top_k(merit.astype(jnp.int32), top)[1].astype(jnp.int32)


def centred(stream_key, dims, scale, limit, pieces=(), kind=jnp.bfloat16):
    values = scale * jax.random.normal(stream_key, dims, jnp.float32)
    if pieces:
        values = values * block_scale(stream_key, dims, pieces, -0.22, 0.18)
    return jnp.clip(values, -limit, limit).astype(kind)


def setup_inputs(seed: int = 0) -> dict:
    arg_keys = jax.random.split(jax.random.key(seed), 19)
    return {
        "inputs": centred(arg_keys[0], (TOKENS, D), 1.0, 6.0, ((0, 32),)),
        "attn_gain": jnp.clip(1.0 + 0.15 * jax.random.normal(arg_keys[1], (D,), jnp.float32), 0.25, 1.75).astype(jnp.bfloat16),
        "w_query": centred(arg_keys[2], (D, D), D ** -0.5, 0.1875),
        "w_key": centred(arg_keys[3], (D, D), D ** -0.5, 0.1875),
        "w_value": centred(arg_keys[4], (D, D), D ** -0.5, 0.1875),
        "w_proj": centred(arg_keys[5], (D, D), (D // 32) ** -0.5, 1.0),
        "rel_bias": centred(arg_keys[6], (BUCKETS, HEADS), 1.0, 4.0),
        "moe_gain": jnp.clip(1.0 + 0.15 * jax.random.normal(arg_keys[7], (D,), jnp.float32), 0.25, 1.75).astype(jnp.bfloat16),
        "w_router": centred(arg_keys[8], (D, EXPERTS), 0.02, 0.119628906),
        "w_gate": centred(arg_keys[9], (EXPERTS, D, FF), D ** -0.5, 0.1875, ((0, 8), (2, 4))),
        "w_up": centred(arg_keys[10], (EXPERTS, D, FF), D ** -0.5, 0.1875, ((0, 8), (2, 4))),
        "w_down": centred(arg_keys[11], (EXPERTS, FF, D), (max(FF // 512, 2)) ** -0.5, 2.5, ((0, 8), (1, 4))),
        "routes": distinct(arg_keys[12], TOKENS, EXPERTS, TOPK, 1024),
        "long_buckets": plant(jax.random.randint(arg_keys[13], (2 * LONG - 1,), 0, BUCKETS), jax.random.fold_in(arg_keys[13], 1), 0, BUCKETS - 1).astype(jnp.int32),
        "short_buckets": plant(jax.random.randint(arg_keys[14], (2 * SHORT - 1,), 0, BUCKETS), jax.random.fold_in(arg_keys[14], 1), 0, BUCKETS - 1).astype(jnp.int32),
        "long_lens": draw_long_lens(jax.random.fold_in(arg_keys[18], 71), 0),
        "short_lens": draw_short_lens(jax.random.fold_in(arg_keys[18], 71), 0),
        "cotangent": centred(arg_keys[17], (TOKENS, D), 1.0, 6.0, ((0, 32),)),
    }


precise = lax.Precision.HIGHEST

@jax.custom_vjp
def low(v):
    return lax.optimization_barrier(v.astype(jnp.bfloat16)).astype(jnp.float32)

@jax.custom_vjp
def low_back(v):
    return v

def low_keep(v):
    return (low(v), None)

def low_pass(kept, grad):
    return (grad,)

def back_keep(v):
    return (v, None)

def back_low(kept, grad):
    return (low(grad),)
low.defvjp(low_keep, low_pass)
low_back.defvjp(back_keep, back_low)

def rms_scale(rows):
    return rows * lax.rsqrt(lax.optimization_barrier(jnp.mean(rows * rows, axis=-1, keepdims=True)) + 1e-06)

def matmul(left, right):
    return jnp.dot(left, right, precision=precise, preferred_element_type=jnp.float32)

def one_sequence(query, keys, values, length, table, rel_table):
    count = query.shape[0]
    heads_query = query.reshape(count, HEADS, HEAD_DIM)
    heads_keys = keys.reshape(count, HEADS, HEAD_DIM)
    heads_values = values.reshape(count, HEADS, HEAD_DIM)
    product = jnp.einsum('ihd,jhd->hij', heads_query, heads_keys, precision=precise) * (1.0 / math.sqrt(HEAD_DIM))
    places = jnp.arange(count, dtype=jnp.int32)
    offsets = places[None, :] - places[:, None] + (count - 1)
    bias = jnp.transpose(rel_table[table[offsets]], (2, 0, 1))
    scores = low_back(product) + bias
    scores = jnp.where((places < length)[None, None, :], scores, -1e+30)
    attend = jax.nn.softmax(scores, axis=-1)
    mixed = jnp.einsum('hij,jhd->ihd', low(attend), heads_values, precision=precise)
    return low_back(low(mixed.reshape(count, HEADS * HEAD_DIM)))

def split_rows(rows):
    view = rows.reshape(LONG_SEQS, N_TENSOR, TOK_DEV, D)
    long_rows = view[:, :, :LONG_DEV].reshape(LONG_SEQS, LONG, D)
    short_rows = view[:, :, LONG_DEV:].reshape(SHORT_TOTAL, SHORT, D)
    return (long_rows, short_rows)

def join_rows(long_rows, short_rows):
    long_view = long_rows.reshape(LONG_SEQS, N_TENSOR, LONG_DEV, D)
    short_view = short_rows.reshape(LONG_SEQS, N_TENSOR, SHORT_SEQS * SHORT, D)
    return jnp.concatenate([long_view, short_view], axis=2).reshape(TOKENS, D)

def placement(routes):
    pairs = routes.reshape(DEVICES, TOK_DEV * TOPK)
    hot = (pairs[:, :, None] == jnp.arange(EXPERTS, dtype=jnp.int32)).astype(jnp.int32)
    before = jnp.cumsum(hot, axis=1) - hot
    position = lax.optimization_barrier(jnp.sum(before * hot, axis=-1))
    kept = position < CAP
    slot_index = pairs * CAP + position
    chosen = (slot_index[:, :, None] == jnp.arange(EXPERTS * CAP, dtype=jnp.int32)) & kept[:, :, None]
    return chosen.astype(jnp.float32)

def expert_step(item):
    rows, gate_weight, up_weight, down_weight = item
    gate_pre = low_back(matmul(rows, gate_weight))
    up_pre = low_back(matmul(rows, up_weight))
    hidden = low(jax.nn.gelu(gate_pre, approximate=True) * up_pre)
    return low_back(low(matmul(hidden, down_weight)))

def reference(inputs, attn_gain, w_query, w_key, w_value, w_proj, rel_bias, moe_gain, w_router, w_gate, w_up, w_down, routes, long_buckets, short_buckets, long_lens, short_lens, cotangent):
    pair_hot = placement(routes)
    token_hot = lax.optimization_barrier(jnp.sum(pair_hot.reshape(DEVICES, TOK_DEV, TOPK, EXPERTS * CAP), axis=2))
    group = math.gcd(SHORT_TOTAL, 32)

    def forward(inputs, attn_gain, w_query, w_key, w_value, w_proj, rel_bias, moe_gain, w_router, w_gate, w_up, w_down):
        normed = low(rms_scale(inputs) * attn_gain)
        query = low_back(low(matmul(normed, w_query)))
        keys = low_back(low(matmul(normed, w_key)))
        values = low_back(low(matmul(normed, w_value)))
        long_query, short_query = split_rows(query)
        long_keys, short_keys = split_rows(keys)
        long_values, short_values = split_rows(values)

        def long_step(item):
            return one_sequence(item[0], item[1], item[2], item[3], long_buckets, rel_bias)

        def short_one(query_rows, key_rows, value_rows, length):
            return one_sequence(query_rows, key_rows, value_rows, length, short_buckets, rel_bias)

        def short_step(item):
            return jax.vmap(short_one)(item[0], item[1], item[2], item[3])
        long_mixed = lax.map(jax.checkpoint(long_step), (long_query, long_keys, long_values, long_lens))
        batches = SHORT_TOTAL // group
        short_mixed = lax.map(jax.checkpoint(short_step), (short_query.reshape(batches, group, SHORT, D), short_keys.reshape(batches, group, SHORT, D), short_values.reshape(batches, group, SHORT, D), short_lens.reshape(batches, group)))
        mixed = join_rows(long_mixed, short_mixed.reshape(SHORT_TOTAL, SHORT, D))
        resid = inputs + low_back(matmul(mixed, w_proj))
        normed_moe = low(rms_scale(resid) * moe_gain)
        logits = low_back(matmul(normed_moe, w_router))
        gates = jnp.take_along_axis(jax.nn.softmax(logits, axis=-1), routes, axis=1)
        grouped = normed_moe.reshape(DEVICES, TOK_DEV, D)
        slots = low_back(low(jnp.einsum('nts,ntd->nsd', token_hot, grouped, precision=precise)))
        per_expert = slots.reshape(DEVICES, EXPERTS, CAP, D).transpose(1, 0, 2, 3).reshape(EXPERTS, DEVICES * CAP, D)
        expert_out = lax.map(jax.checkpoint(expert_step), (per_expert, w_gate, w_up, w_down))
        back = expert_out.reshape(EXPERTS, DEVICES, CAP, D).transpose(1, 0, 2, 3).reshape(DEVICES, EXPERTS * CAP, D)
        pair_values = jnp.einsum('nps,nsd->npd', pair_hot, back, precision=precise).reshape(TOKENS, TOPK, D)
        return resid + lax.optimization_barrier(jnp.sum(gates[:, :, None] * pair_values, axis=1))
    floats = (inputs.astype(jnp.float32), attn_gain.astype(jnp.float32), w_query.astype(jnp.float32), w_key.astype(jnp.float32), w_value.astype(jnp.float32), w_proj.astype(jnp.float32), rel_bias.astype(jnp.float32), moe_gain.astype(jnp.float32), w_router.astype(jnp.float32), w_gate.astype(jnp.float32), w_up.astype(jnp.float32), w_down.astype(jnp.float32))
    result, pullback = jax.vjp(forward, floats[0], floats[1], floats[2], floats[3], floats[4], floats[5], floats[6], floats[7], floats[8], floats[9], floats[10], floats[11])
    grads = pullback(cotangent.astype(jnp.float32))
    return (result.astype(jnp.bfloat16), grads[0], grads[1], grads[2], grads[3], grads[4], grads[5], grads[6], grads[7], grads[8], grads[9], grads[10], grads[11])
```

```python
from functools import partial
import math

import jax
import jax.numpy as jnp
from jax import lax
from jax.experimental import pallas as pl
from jax.experimental.pallas import tpu as pltpu
from jax.sharding import PartitionSpec as P

precise = lax.Precision.HIGHEST
bf16 = jnp.bfloat16
f32 = jnp.float32
NT = (((1,), (1,)), ((), ()))
NN = (((1,), (0,)), ((), ()))
TN = (((0,), (0,)), ((), ()))
VMEM_BYTES = 56 * 1024 * 1024


def mm(left, right, dims=NN):
    return lax.dot_general(left, right, dims, preferred_element_type=f32)


def params():
    return pltpu.CompilerParams(
        dimension_semantics=("arbitrary",), vmem_limit_bytes=VMEM_BYTES
    )


def cost(flops, moved):
    return pl.CostEstimate(flops=int(flops), bytes_accessed=int(moved), transcendentals=0)


def rms_scale(rows):
    return rows * lax.rsqrt(jnp.mean(rows * rows, axis=-1, keepdims=True) + 1e-06)


def norm_apply(rows, gain):
    return rms_scale(rows) * gain


def gate_values(logit_rows, route_hot):
    return jnp.sum(route_hot * jax.nn.softmax(logit_rows, axis=-1)[:, None, :], axis=-1)


def table_hot(table, count):
    return (table[:, None] == jnp.arange(count, dtype=jnp.int32)[None, :]).astype(f32)


def swap(rows, axis, mask):
    count = lax.axis_size(axis)
    return lax.ppermute(rows, axis, [(i, i ^ mask) for i in range(count)])


def gather_parts(rows):
    count = lax.axis_size("tensor")
    if count != 4:
        return [rows] + [swap(rows, "tensor", r) for r in range(1, count)]
    half = rows.shape[0] // 2
    by_x = swap(rows, "tensor", 1)
    by_y = swap(rows, "tensor", 2)
    return [rows, by_x, by_y, swap(by_x[:half], "tensor", 2), swap(by_y[half:], "tensor", 1)]


def sum_parts(parts):
    count = lax.axis_size("tensor")
    if count != 4:
        arrived = [swap(parts[r], "tensor", r) for r in range(1, count)]
        return sum([part.astype(f32) for part in arrived], parts[0].astype(f32))
    half = parts[3].shape[0]
    left = swap(parts[3], "tensor", 1)
    right = swap(parts[4], "tensor", 2)
    to_y = jnp.concatenate(
        [(parts[2][:half].astype(f32) + left.astype(f32)).astype(bf16), parts[2][half:]], axis=0
    )
    to_x = jnp.concatenate(
        [parts[1][:half], (parts[1][half:].astype(f32) + right.astype(f32)).astype(bf16)], axis=0
    )
    from_x = swap(to_x, "tensor", 1)
    from_y = swap(to_y, "tensor", 2)
    return parts[0].astype(f32) + from_x.astype(f32) + from_y.astype(f32)


def part_rows(count, rows):
    return [rows, rows, rows, rows // 2, rows // 2] if count == 4 else [rows] * count


def over_experts(rows):
    experts_axis = lax.axis_size("expert")
    blocks = rows.reshape(experts_axis, rows.shape[0] // experts_axis, rows.shape[1])
    return lax.all_to_all(blocks, "expert", 0, 0, tiled=True).reshape(rows.shape)


def piece(rows, index, size):
    return lax.dynamic_slice_in_dim(rows, index * size, size, 0)


def total(rows):
    experts_axis = lax.axis_size("expert")
    tensor_axis = lax.axis_size("tensor")
    size = rows.shape[0]
    if experts_axis != 8 or tensor_axis != 4 or size % 256:
        return lax.psum(rows, ("expert", "tensor"))
    here = lax.axis_index("expert")
    core = here % 2
    depth = here // 2
    place = lax.axis_index("tensor")
    levels = (
        (core, 2, lambda a, r: swap(a, "expert", r)),
        (place, 4, lambda a, r: swap(a, "tensor", r)),
        (depth, 4, lambda a, r: swap(a, "expert", 2 * r)),
    )
    part = rows
    for index, count, move in levels:
        size = size // count
        arrived = [move(piece(part, index ^ r, size).astype(bf16), r) for r in range(1, count)]
        part = piece(part, index, size).astype(f32)
        for other in arrived:
            part = part + other.astype(f32)
    part = part.astype(bf16)
    for index, count, move in levels[::-1]:
        blocks = jnp.stack([part] + [move(part, r) for r in range(1, count)])
        part = jnp.concatenate(
            [lax.dynamic_index_in_dim(blocks, index ^ i, 0, keepdims=False) for i in range(count)],
            axis=0,
        )
    return part.astype(f32)


def project_kernel(long_local, inputs, gain, w_query, w_key, w_value, normed, query, pair, near, held):
    @pl.when(pl.program_id(0) == 0)
    def _():
        rows = inputs[...].astype(f32)
        scale = lax.rsqrt(jnp.mean(rows * rows, axis=-1, keepdims=True) + 1e-06)
        held[...] = (rows * scale * gain[...].astype(f32)).astype(bf16)
        normed[...] = held[...]

    rows = held[...]
    query[...] = mm(rows, w_query[...]).astype(bf16)
    keys = mm(rows, w_key[...]).astype(bf16)
    values = mm(rows, w_value[...]).astype(bf16)
    pair[:long_local] = keys[:long_local]
    pair[long_local:] = values[:long_local]
    short = keys.shape[0] - long_local
    near[:short] = keys[long_local:]
    near[short:] = values[long_local:]


def project(inputs, gain, w_query, w_key, w_value, long_local):
    rows, width = inputs.shape
    short = rows - long_local
    step = 256
    whole = lambda count: pl.BlockSpec((count, width), lambda i: (0, 0))
    cut = lambda count: pl.BlockSpec((count, step), lambda i: (0, i))
    return pl.pallas_call(
        partial(project_kernel, long_local),
        grid=(width // step,),
        in_specs=[whole(rows), whole(1), cut(width), cut(width), cut(width)],
        out_specs=[whole(rows), cut(rows), cut(2 * long_local), cut(2 * short)],
        out_shape=[
            jax.ShapeDtypeStruct((rows, width), bf16),
            jax.ShapeDtypeStruct((rows, width), bf16),
            jax.ShapeDtypeStruct((2 * long_local, width), bf16),
            jax.ShapeDtypeStruct((2 * short, width), bf16),
        ],
        scratch_shapes=[pltpu.VMEM((rows, width), bf16)],
        compiler_params=params(),
        cost_estimate=cost(6 * rows * width * width, 6 * width * width + 10 * rows * width),
        name="project",
    )(inputs, gain.reshape(1, width), w_query, w_key, w_value)


def key_value_views(parts, count, rows):
    views = []
    for r in range(count):
        if count == 4 and r == 3:
            views.append((parts[3], slice(0, rows), parts[4], slice(0, rows)))
        else:
            views.append((parts[r], slice(0, rows), parts[r], slice(rows, 2 * rows)))
    return views


def forward_kernel(count, rows, dim, facts, query, *refs):
    kinds = len(part_rows(count, rows))
    parts = refs[:kinds]
    near, far_bias, near_bias, mixed, far_attend, near_attend, window = refs[kinds:]
    place, far_len, near_len = facts[0], facts[1], facts[2]
    scale = 1.0 / math.sqrt(dim)
    views = key_value_views(parts, count, rows)
    short = near.shape[0] // 2
    reach = far_bias.shape[-1]
    for head in range(2):
        lanes = slice(head * dim, (head + 1) * dim)
        low = (query[:, lanes].astype(f32) * scale).astype(bf16)
        table = jnp.broadcast_to(far_bias[0, head : head + 1, :], (rows, reach))
        window[...] = pltpu.roll(table, reach - (rows - 1), 1, stride=1, stride_axis=0)
        scores = []
        for r in range(count):
            source = place ^ r
            start = pl.multiple_of(source * rows, rows)
            keys = views[r][0][views[r][1], lanes]
            part = mm(low[:rows], keys, NT) + window[:, pl.ds(start, rows)]
            spot = source * rows + lax.broadcasted_iota(jnp.int32, (1, rows), 1)
            scores.append(jnp.where(spot < far_len, part, -1e30))
        highest = scores[0]
        for part in scores[1:]:
            highest = jnp.maximum(highest, part)
        highest = jnp.max(highest, axis=-1, keepdims=True)
        grown = [jnp.exp(part - highest) for part in scores]
        whole = grown[0]
        for part in grown[1:]:
            whole = whole + part
        inverse = 1.0 / jnp.sum(whole, axis=-1, keepdims=True)
        out = jnp.zeros((rows, dim), f32)
        for r in range(count):
            attend = (grown[r] * inverse).astype(bf16)
            far_attend[head, :, r * rows : (r + 1) * rows] = attend
            out = out + mm(attend, views[r][2][views[r][3], lanes])
        mixed[:rows, lanes] = out.astype(bf16)

        table = jnp.broadcast_to(near_bias[0, head : head + 1, :], (short, 2 * short))
        bias = pltpu.roll(table, short + 1, 1, stride=1, stride_axis=0)[:, :short]
        part = mm(low[rows:], near[:short, lanes], NT) + bias
        spot = lax.broadcasted_iota(jnp.int32, (1, short), 1)
        part = jnp.where(spot < near_len, part, -1e30)
        part = jnp.exp(part - jnp.max(part, axis=-1, keepdims=True))
        attend = (part * (1.0 / jnp.sum(part, axis=-1, keepdims=True))).astype(bf16)
        near_attend[head] = attend
        mixed[rows:, lanes] = mm(attend, near[short:, lanes]).astype(bf16)


def attention_specs(count, rows, short, reach, tokens):
    cut = lambda size: pl.BlockSpec((size, 128), lambda i, *_: (0, i))
    parts = [cut(size) for size in part_rows(count, 2 * rows)]
    table = lambda size: pl.BlockSpec((1, 2, size), lambda i, *_: (i, 0, 0))
    weights = lambda size, span: pl.BlockSpec((2, size, span), lambda i, *_: (i, 0, 0))
    return (
        cut(tokens),
        parts,
        cut(2 * short),
        [table(reach), table(2 * short)],
        [weights(rows, count * rows), weights(short, short)],
    )


def attend_forward(facts, query, parts, near, far_bias, near_bias, count, rows, dim):
    tokens, width = query.shape
    heads = width // dim
    short = near.shape[0] // 2
    reach = far_bias.shape[-1]
    cut, part_specs, near_spec, tables, weights = attention_specs(count, rows, short, reach, tokens)
    return pl.pallas_call(
        partial(forward_kernel, count, rows, dim),
        grid_spec=pltpu.PrefetchScalarGridSpec(
            num_scalar_prefetch=1,
            grid=(heads // 2,),
            in_specs=[cut] + part_specs + [near_spec] + tables,
            out_specs=[cut] + weights,
            scratch_shapes=[pltpu.VMEM((rows, reach), f32)],
        ),
        out_shape=[
            jax.ShapeDtypeStruct((tokens, width), bf16),
            jax.ShapeDtypeStruct((heads, rows, count * rows), bf16),
            jax.ShapeDtypeStruct((heads, short, short), bf16),
        ],
        compiler_params=params(),
        cost_estimate=cost(40 * heads * rows * rows * count * dim, 12 * width * rows * count),
        name="attend_forward",
    )(facts, query, *parts, near, far_bias, near_bias)


def backward_kernel(count, rows, dim, facts, query, grad, *refs):
    kinds = len(part_rows(count, rows))
    parts = refs[:kinds]
    near, far_attend, near_attend = refs[kinds : kinds + 3]
    grad_query = refs[kinds + 3]
    grad_parts = refs[kinds + 4 : 2 * kinds + 4]
    grad_near, far_sums, near_sums, window, near_window = refs[2 * kinds + 4 :]
    place = facts[0]
    scale = 1.0 / math.sqrt(dim)
    views = key_value_views(parts, count, rows)
    grad_views = key_value_views(grad_parts, count, rows)
    short = near.shape[0] // 2
    reach = window.shape[1]

    @pl.when(pl.program_id(0) == 0)
    def _():
        window[...] = jnp.zeros_like(window)
        near_window[...] = jnp.zeros_like(near_window)

    def reversal(size):
        up = lax.broadcasted_iota(jnp.int32, (size, size), 0)
        across = lax.broadcasted_iota(jnp.int32, (size, size), 1)
        return (up + across == size - 1).astype(bf16)

    far_turn = reversal(rows)
    near_turn = far_turn if short == rows else reversal(short)
    for head in range(2):
        lanes = slice(head * dim, (head + 1) * dim)
        low = query[:, lanes]
        grad_low = grad[:, lanes]
        turned = jnp.transpose((low.astype(f32) * scale), (1, 0)).astype(bf16)
        grad_turned = jnp.transpose(grad_low.astype(f32), (1, 0)).astype(bf16)
        attends, grads = [], []
        inner = jnp.zeros((rows, 1), f32)
        for r in range(count):
            attend = far_attend[head, :, r * rows : (r + 1) * rows]
            part = mm(grad_low[:rows], views[r][2][views[r][3], lanes], NT)
            inner = inner + jnp.sum(attend.astype(f32) * part, axis=-1, keepdims=True)
            attends.append(attend)
            grads.append(part)
        out = jnp.zeros((rows, dim), f32)
        for r in range(count):
            start = pl.multiple_of((place ^ r) * rows, rows)
            scores = (attends[r].astype(f32) * (grads[r] - inner)).astype(bf16)
            window[:, pl.ds(start, rows)] = mm(far_turn, scores)
            out = out + mm(scores, views[r][0][views[r][1], lanes])
            grad_keys = mm(turned[:, :rows], scores)
            grad_values = mm(grad_turned[:, :rows], attends[r])
            view = grad_views[r]
            view[0][view[1], lanes] = jnp.transpose(grad_keys, (1, 0)).astype(bf16)
            view[2][view[3], lanes] = jnp.transpose(grad_values, (1, 0)).astype(bf16)
        grad_query[:rows, lanes] = (out * scale).astype(bf16)
        rolled = pltpu.roll(window[...], 0, 1, stride=1, stride_axis=0)
        far_sums[0, head : head + 1, :] = jnp.sum(rolled, axis=0, keepdims=True)

        attend = near_attend[head]
        part = mm(grad_low[rows:], near[short:, lanes], NT)
        wide = attend.astype(f32)
        part = wide * (part - jnp.sum(wide * part, axis=-1, keepdims=True))
        scores = part.astype(bf16)
        near_window[:, :short] = mm(near_turn, scores)
        rolled = pltpu.roll(near_window[...], 0, 1, stride=1, stride_axis=0)
        near_sums[0, head : head + 1, :] = jnp.sum(rolled, axis=0, keepdims=True)
        grad_query[rows:, lanes] = (mm(scores, near[:short, lanes]) * scale).astype(bf16)
        grad_keys = mm(turned[:, rows:], scores)
        grad_values = mm(grad_turned[:, rows:], attend)
        grad_near[:short, lanes] = jnp.transpose(grad_keys, (1, 0)).astype(bf16)
        grad_near[short:, lanes] = jnp.transpose(grad_values, (1, 0)).astype(bf16)


def attend_backward(facts, query, grad, parts, near, weights, reach, count, rows, dim):
    tokens, width = query.shape
    heads = width // dim
    short = near.shape[0] // 2
    cut, part_specs, near_spec, tables, weight_specs = attention_specs(count, rows, short, reach, tokens)
    sizes = part_rows(count, 2 * rows)
    outs = pl.pallas_call(
        partial(backward_kernel, count, rows, dim),
        grid_spec=pltpu.PrefetchScalarGridSpec(
            num_scalar_prefetch=1,
            grid=(heads // 2,),
            in_specs=[cut, cut] + part_specs + [near_spec] + weight_specs,
            out_specs=[cut] + part_specs + [near_spec] + tables,
            scratch_shapes=[pltpu.VMEM((rows, reach), f32), pltpu.VMEM((short, 2 * short), f32)],
        ),
        out_shape=[jax.ShapeDtypeStruct((tokens, width), bf16)]
        + [jax.ShapeDtypeStruct((size, width), bf16) for size in sizes]
        + [jax.ShapeDtypeStruct((2 * short, width), bf16)]
        + [
            jax.ShapeDtypeStruct((heads // 2, 2, reach), f32),
            jax.ShapeDtypeStruct((heads // 2, 2, 2 * short), f32),
        ],
        compiler_params=params(),
        cost_estimate=cost(100 * heads * rows * rows * count * dim, 16 * width * rows * count),
        name="attend_backward",
    )(facts, query, grad, *parts, near, *weights)
    kinds = len(sizes)
    return outs[0], outs[1 : kinds + 1], outs[kinds + 1], outs[kinds + 2], outs[kinds + 3]


def part_copies(count, parts, index, buffer, sem, out=False):
    if count == 4 and index == 3:
        half = parts[3].shape[0]
        pairs = [(parts[3], buffer.at[pl.ds(0, half)]), (parts[4], buffer.at[pl.ds(half, half)])]
    else:
        pairs = [(parts[index], buffer)]
    return [
        pltpu.make_async_copy(b, a, sem) if out else pltpu.make_async_copy(a, b, sem)
        for a, b in pairs
    ]


def expert_kernel(count, capacity, padded, facts, *refs):
    kinds = len(part_rows(count, 2))
    slots, grads = refs[:kinds], refs[kinds : 2 * kinds]
    w_gate, w_up, w_down = refs[2 * kinds : 2 * kinds + 3]
    rest = refs[2 * kinds + 3 :]
    hidden_out, gate_out, up_out = rest[:3]
    outs, grad_outs = rest[3 : 3 + kinds], rest[3 + kinds : 3 + 2 * kinds]
    slot_rows, grad_rows, out_rows, grad_out_rows, in_sem, out_sem = rest[3 + 2 * kinds :]
    step = pl.program_id(0)
    slot = step % 2
    rows, width = slot_rows.shape[1:]
    groups = rows // padded
    place = facts[0]

    def fetch(index, side):
        for r in range(count):

            @pl.when(index == r)
            def _():
                for source, buffer, lane in ((slots, slot_rows, 0), (grads, grad_rows, 1)):
                    for copy in part_copies(count, source, r, buffer.at[side], in_sem.at[side, lane]):
                        copy.start()

    @pl.when(step == 0)
    def _():
        fetch(step, slot)

    @pl.when(step + 1 < count)
    def _():
        fetch(step + 1, 1 - slot)

    for buffer, source, lane in ((slot_rows, slots, 0), (grad_rows, grads, 1)):
        pltpu.make_async_copy(source[0], buffer.at[slot], in_sem.at[slot, lane]).wait()

    def wait_out(side):
        for buffer, target, lane in ((out_rows, outs, 0), (grad_out_rows, grad_outs, 1)):
            pltpu.make_async_copy(buffer.at[side], target[0], out_sem.at[side, lane]).wait()

    @pl.when(step >= 2)
    def _():
        wait_out(slot)

    rows_in = slot_rows[slot]
    grads_in = grad_rows[slot]
    lanes = lax.broadcasted_iota(jnp.int32, (padded, 128), 1)
    match = lax.broadcasted_iota(jnp.int32, (padded, 128), 0) == lanes
    columns = []
    for g in range(groups):
        tail = slot_rows[slot, pl.ds((g + 1) * padded - 16, 16), :128].astype(f32)
        spare = 16 - (padded - capacity)
        line = tail[spare : spare + 1] + tail[spare + 1 : spare + 2]
        columns.append(jnp.sum(jnp.where(match, line, 0.0), axis=-1, keepdims=True))
    gate_column = jnp.concatenate(columns, axis=0)

    gate_pre = mm(rows_in, w_gate[0], NT)
    up_pre = mm(rows_in, w_up[0], NT)
    grad_hidden = mm(grads_in, w_down[0], NT) * gate_column
    slope = math.sqrt(2.0 / math.pi)
    square = gate_pre * gate_pre
    curve = jnp.tanh(slope * gate_pre * (1.0 + 0.044715 * square))
    side = 0.5 * (1.0 + curve)
    bent = gate_pre * side
    hidden = bent * up_pre
    bent_slope = side + 0.5 * slope * gate_pre * (1.0 - curve * curve) * (
        1.0 + 3.0 * 0.044715 * square
    )
    gate_low = (grad_hidden * up_pre * bent_slope).astype(bf16)
    up_low = (grad_hidden * bent).astype(bf16)
    hidden_out[...] = (hidden * gate_column).astype(bf16)
    gate_out[...] = gate_low
    up_out[...] = up_low
    out = mm(hidden.astype(bf16), w_down[0])
    out_rows[slot] = out.astype(bf16)
    grad_gate = jnp.sum(out * grads_in.astype(f32), axis=-1, keepdims=True)
    grad_out = mm(gate_low, w_gate[0]) + mm(up_low, w_up[0])
    grad_out_rows[slot] = grad_out.astype(bf16)

    span = count * padded
    lanes = lax.broadcasted_iota(jnp.int32, (padded, span), 1)
    match = lax.broadcasted_iota(jnp.int32, (padded, span), 0) + place * padded == lanes
    row = lax.broadcasted_iota(jnp.int32, (16, span), 0)
    spare = 16 - (padded - capacity)
    for g in range(groups):
        values = jnp.where(match, grad_gate[g * padded : (g + 1) * padded], 0.0)
        line = jnp.sum(values, axis=0, keepdims=True)
        high = line.astype(bf16).astype(f32)
        tail = grad_out[(g + 1) * padded - 16 : (g + 1) * padded, :span]
        tail = jnp.where(row == spare, high, jnp.where(row == spare + 1, line - high, tail))
        grad_out_rows[slot, pl.ds((g + 1) * padded - 16, 16), :span] = tail.astype(bf16)

    for r in range(count):

        @pl.when(step == r)
        def _():
            for target, buffer, lane in ((outs, out_rows, 0), (grad_outs, grad_out_rows, 1)):
                for copy in part_copies(count, target, r, buffer.at[slot], out_sem.at[slot, lane], True):
                    copy.start()

    @pl.when(step == count - 1)
    def _():
        wait_out(slot)
        if count > 1:
            wait_out(1 - slot)


def expert_pass(facts, slots, grads, w_gate, w_up, w_down, which, capacity, padded):
    count = lax.axis_size("tensor")
    rows, width = slots[0].shape
    units = w_gate.shape[1]
    sizes = part_rows(count, rows)
    kinds = len(sizes)
    anywhere = pl.BlockSpec(memory_space=pl.ANY)
    weight = pl.BlockSpec((1, units, width), lambda i, *_: (which, 0, 0))
    middle = pl.BlockSpec((rows, units), lambda i, *_: (i, 0))
    outs = pl.pallas_call(
        partial(expert_kernel, count, capacity, padded),
        grid_spec=pltpu.PrefetchScalarGridSpec(
            num_scalar_prefetch=1,
            grid=(count,),
            in_specs=[anywhere] * (2 * kinds) + [weight] * 3,
            out_specs=[middle] * 3 + [anywhere] * (2 * kinds),
            scratch_shapes=[pltpu.VMEM((2, rows, width), bf16)] * 4
            + [pltpu.SemaphoreType.DMA((2, 2))] * 2,
        ),
        out_shape=[jax.ShapeDtypeStruct((count * rows, units), bf16)] * 3
        + [jax.ShapeDtypeStruct((size, width), bf16) for size in sizes] * 2,
        compiler_params=params(),
        cost_estimate=cost(12 * count * rows * units * width, 8 * count * rows * width),
        name="expert_pass",
    )(facts, *slots, *grads, w_gate, w_up, w_down)
    return outs[:3], outs[3 : 3 + kinds], outs[3 + kinds :]


def weight_kernel(count, *refs):
    kinds = len(part_rows(count, 2))
    slots, grads = refs[:kinds], refs[kinds : 2 * kinds]
    hidden, gate_low, up_low = refs[2 * kinds : 2 * kinds + 3]
    gate_out, up_out, down_out, slot_rows, grad_rows, in_sem = refs[-6:]
    step = pl.program_id(0)
    slot = step % 2

    def fetch(index, side):
        for r in range(count):

            @pl.when(index == r)
            def _():
                for source, buffer, lane in ((slots, slot_rows, 0), (grads, grad_rows, 1)):
                    for copy in part_copies(count, source, r, buffer.at[side], in_sem.at[side, lane]):
                        copy.start()

    @pl.when(step == 0)
    def _():
        fetch(step, slot)

    @pl.when(step + 1 < count)
    def _():
        fetch(step + 1, 1 - slot)

    for buffer, source, lane in ((slot_rows, slots, 0), (grad_rows, grads, 1)):
        pltpu.make_async_copy(source[0], buffer.at[slot], in_sem.at[slot, lane]).wait()

    @pl.when(step == 0)
    def _():
        for out in (gate_out, up_out, down_out):
            out[...] = jnp.zeros_like(out)

    rows_in = slot_rows[slot]
    gate_out[0] += mm(gate_low[...], rows_in, TN)
    up_out[0] += mm(up_low[...], rows_in, TN)
    down_out[0] += mm(hidden[...], grad_rows[slot], TN)


def weight_pass(slots, grads, middles, before, which, local):
    count = lax.axis_size("tensor")
    rows, width = slots[0].shape
    units = middles[0].shape[1]
    kinds = len(slots)
    anywhere = pl.BlockSpec(memory_space=pl.ANY)
    middle = pl.BlockSpec((rows, units), lambda i: (i, 0))
    outs = pl.BlockSpec((1, units, width), lambda i: (which, 0, 0))
    aliases = {2 * kinds + 3 + i: i for i in range(len(before))}
    return pl.pallas_call(
        partial(weight_kernel, count),
        grid=(count,),
        in_specs=[anywhere] * (2 * kinds) + [middle] * 3 + [anywhere] * len(before),
        out_specs=[outs] * 3,
        out_shape=[jax.ShapeDtypeStruct((local, units, width), f32)] * 3,
        scratch_shapes=[pltpu.VMEM((2, rows, width), bf16)] * 2 + [pltpu.SemaphoreType.DMA((2, 2))],
        input_output_aliases=aliases,
        compiler_params=params(),
        cost_estimate=cost(6 * count * rows * units * width, 8 * count * rows * width),
        name="weight_pass",
    )(*slots, *grads, *middles, *before)


def per_device(
    inputs,
    attn_gain,
    w_query,
    w_key,
    w_value,
    w_proj,
    rel_bias,
    moe_gain,
    w_router,
    w_gate,
    w_up,
    w_down,
    routes,
    long_buckets,
    short_buckets,
    long_lens,
    short_lens,
    cotangent,
):
    experts_axis = lax.axis_size("expert")
    tensor_axis = lax.axis_size("tensor")
    place = lax.axis_index("tensor")
    tok_count, width = inputs.shape
    top_count = routes.shape[1]
    short_len = (short_buckets.shape[0] + 1) // 2
    long_span = (long_buckets.shape[0] + 1) // 2
    long_local = tok_count - short_len
    bucket_count, heads = rel_bias.shape
    head_dim = width // heads
    experts = w_router.shape[1]
    local = experts // experts_axis
    capacity = (5 * tok_count * top_count + 4 * experts - 1) // (4 * experts)
    padded = (capacity + 2 + 15) // 16 * 16
    block = experts_axis * padded
    rel_table = rel_bias.astype(f32)
    facts = jnp.stack([place.astype(jnp.int32), long_lens[0], short_lens[0]])

    pair_routes = routes.reshape(-1)
    pair_total = pair_routes.shape[0]
    route_count = (pair_routes[:, None] == jnp.arange(experts, dtype=jnp.int32)).astype(bf16)
    pair_places = jnp.arange(pair_total, dtype=jnp.int32)
    earlier = (pair_places[None, :] < pair_places[:, None]).astype(bf16)
    before = jnp.dot(earlier, route_count, preferred_element_type=f32)
    position = jnp.sum(before * route_count.astype(f32), axis=1).astype(jnp.int32)
    slot_index = (pair_routes % local) * block + (pair_routes // local) * padded + position
    slot_index = jnp.where(position < capacity, slot_index, -1).reshape(tok_count, top_count)
    slot_places = jnp.arange(local * block, dtype=jnp.int32)
    pair_hot = (slot_index[:, :, None] == slot_places).astype(bf16)
    token_hot = jnp.sum(pair_hot, axis=1)

    grad_slots_in = mm(token_hot, cotangent, TN).astype(bf16)
    grad_parts = [
        gather_parts(over_experts(grad_slots_in[j * block : (j + 1) * block])) for j in range(local)
    ]

    normed_low, query, pair, near = project(inputs, attn_gain, w_query, w_key, w_value, long_local)
    parts = gather_parts(pair)
    reach = long_span + long_local
    first = long_span - long_local - long_local * place
    long_table = jnp.pad(long_buckets, (0, 1), constant_values=-1)
    long_hot = table_hot(lax.dynamic_slice_in_dim(long_table, first, reach, 0), bucket_count)
    short_hot = table_hot(jnp.pad(short_buckets, (0, 1), constant_values=-1), bucket_count)
    spread = lambda hot: jnp.einsum(
        "cb,bh->hc", hot, rel_table, precision=precise, preferred_element_type=f32
    ).reshape(heads // 2, 2, hot.shape[0])
    mixed, far_attend, near_attend = attend_forward(
        facts, query, parts, near, spread(long_hot), spread(short_hot), tensor_axis, long_local, head_dim
    )
    inputs_wide = inputs.astype(f32)
    resid = inputs_wide + mm(mixed, w_proj)
    normed_moe, norm_moe_back = jax.vjp(norm_apply, resid, moe_gain.astype(f32))
    moe_low = normed_moe.astype(bf16)
    logits = mm(moe_low, w_router)
    route_hot = (routes[:, :, None] == jnp.arange(experts, dtype=jnp.int32)).astype(f32)
    gates, gate_back = jax.vjp(partial(gate_values, route_hot=route_hot), logits)

    slot_gates = jnp.sum(pair_hot.astype(f32) * gates[:, :, None], axis=(0, 1))
    slot_gates = slot_gates.reshape(local * experts_axis, padded)
    gates_high = slot_gates.astype(bf16)
    gates_rest = (slot_gates - gates_high.astype(f32)).astype(bf16)
    spare_rows = jnp.pad(
        jnp.concatenate([gates_high, gates_rest], axis=0), ((0, 0), (0, width - padded))
    )
    group = jnp.arange(local * experts_axis, dtype=jnp.int32)[:, None] * padded + capacity
    spare_hot = jnp.concatenate([group == slot_places, group + 1 == slot_places], axis=0).astype(bf16)
    slots_in = (mm(token_hot, moe_low, TN) + mm(spare_hot, spare_rows, TN)).astype(bf16)
    slot_parts = [
        gather_parts(over_experts(slots_in[j * block : (j + 1) * block])) for j in range(local)
    ]
    gate_turned = jnp.swapaxes(w_gate, 1, 2)
    up_turned = jnp.swapaxes(w_up, 1, 2)
    passes = [
        expert_pass(
            facts, slot_parts[j], grad_parts[j], gate_turned, up_turned, w_down, j, capacity, padded
        )
        for j in range(local)
    ]
    grad_slots = [over_experts(sum_parts(passes[j][2]).astype(bf16)) for j in range(local)]
    weight_grads = ()
    for j in range(local):
        weight_grads = weight_pass(slot_parts[j], grad_parts[j], passes[j][0], weight_grads, j, local)

    grad_out = cotangent.astype(f32)
    slot_grads = []
    for rows in grad_slots:
        lines = rows.reshape(experts_axis, padded, width)[:, capacity : capacity + 2]
        lines = lines[:, :, : tensor_axis * padded].astype(f32)
        lines = lines.reshape(experts_axis, 2, tensor_axis, padded)
        slot_grads.append(jnp.sum(lines, axis=(1, 2)).reshape(block))
    slot_grads = jnp.concatenate(slot_grads)
    grad_gates = jnp.sum(
        jnp.where(slot_index[:, :, None] == slot_places, slot_grads, 0.0), axis=-1
    )
    grad_moe = sum(
        mm(token_hot[:, j * block : (j + 1) * block], grad_slots[j]) for j in range(local)
    )
    logits_low = gate_back(grad_gates)[0].astype(bf16)
    router_grad = mm(logits_low, moe_low, TN)
    grad_moe = grad_moe + mm(logits_low, w_router, NT)
    grad_resid_part, moe_gain_grad = norm_moe_back(grad_moe)
    grad_resid = grad_out + grad_resid_part
    grad_branch = grad_resid.astype(bf16)
    proj_grad = total(mm(mixed, grad_branch, TN))
    grad_mixed = mm(grad_branch, w_proj, NT).astype(bf16)

    grad_query, grad_pairs, grad_near, far_sums, near_sums = attend_backward(
        facts, query, grad_mixed, parts, near, (far_attend, near_attend), reach, tensor_axis, long_local, head_dim
    )
    pair_sums = sum_parts(grad_pairs).astype(bf16)
    query_grad = total(mm(normed_low, grad_query, TN))
    grad_keys = jnp.concatenate([pair_sums[:long_local], grad_near[:short_len]], axis=0)
    grad_values = jnp.concatenate([pair_sums[long_local:], grad_near[short_len:]], axis=0)
    collect = lambda sums, hot: jnp.einsum(
        "hc,cb->bh",
        sums.reshape(heads, hot.shape[0]),
        hot,
        precision=precise,
        preferred_element_type=f32,
    )
    rel_grad = collect(far_sums, long_hot) + collect(near_sums, short_hot)
    key_grad = total(mm(normed_low, grad_keys, TN))
    value_grad = mm(normed_low, grad_values, TN)
    grad_normed = mm(grad_query, w_query, NT) + mm(grad_keys, w_key, NT) + mm(grad_values, w_value, NT)
    norm_attn_back = jax.vjp(norm_apply, inputs_wide, attn_gain.astype(f32))[1]
    grad_inputs_part, attn_gain_grad = norm_attn_back(grad_normed)
    inputs_grad = grad_resid + grad_inputs_part
    rel_row = jnp.pad(rel_grad.reshape(1, -1), ((0, 0), (0, width - rel_grad.size)))
    small = jnp.concatenate([attn_gain_grad[None], moe_gain_grad[None], rel_row, router_grad], axis=0)
    small_rows = small.shape[0]
    small = jnp.pad(small, ((0, 256 - small_rows), (0, 0)))
    last = total(jnp.concatenate([value_grad, small], axis=0))

    outs_back = [over_experts(sum_parts(passes[j][1]).astype(bf16)) for j in range(local)]
    pair_values = sum(
        mm(pair_hot[:, :, j * block : (j + 1) * block].reshape(pair_total, block), outs_back[j])
        for j in range(local)
    ).reshape(tok_count, top_count, width)
    outputs = (resid + jnp.sum(gates[:, :, None] * pair_values, axis=1)).astype(bf16)
    return (
        outputs,
        inputs_grad,
        last[width],
        query_grad,
        key_grad,
        last[:width],
        proj_grad,
        last[width + 2, : rel_grad.size].reshape(rel_grad.shape),
        last[width + 1],
        jnp.transpose(last[width + 3 : width + small_rows]),
        jnp.swapaxes(weight_grads[0], 1, 2),
        jnp.swapaxes(weight_grads[1], 1, 2),
        weight_grads[2],
    )


def solution(mesh):
    return jax.shard_map(
        per_device,
        mesh=mesh,
        in_specs=(
            P(("expert", "tensor"), None),
            P(),
            P(),
            P(),
            P(),
            P(),
            P(),
            P(),
            P(),
            P("expert", None, "tensor"),
            P("expert", None, "tensor"),
            P("expert", "tensor", None),
            P(("expert", "tensor"), None),
            P(),
            P(),
            P("expert"),
            P(("expert", "tensor")),
            P(("expert", "tensor"), None),
        ),
        out_specs=(
            P(("expert", "tensor"), None),
            P(("expert", "tensor"), None),
            P(),
            P(),
            P(),
            P(),
            P(),
            P(),
            P(),
            P(),
            P("expert", None, "tensor"),
            P("expert", None, "tensor"),
            P("expert", "tensor", None),
        ),
        check_vma=False,
    )
```

```python
from functools import partial
import math

import jax
import jax.numpy as jnp
from jax import lax
from jax.experimental import pallas as pl
from jax.experimental.pallas import tpu as pltpu
from jax.sharding import PartitionSpec as P

precise = lax.Precision.HIGHEST
bf16 = jnp.bfloat16
f32 = jnp.float32
NT = (((1,), (1,)), ((), ()))
NN = (((1,), (0,)), ((), ()))
TN = (((0,), (0,)), ((), ()))
VMEM_BYTES = 56 * 1024 * 1024


def mm(left, right, dims=NN):
    return lax.dot_general(left, right, dims, preferred_element_type=f32)


def params():
    return pltpu.CompilerParams(
        dimension_semantics=("arbitrary",), vmem_limit_bytes=VMEM_BYTES
    )


def cost(flops, moved):
    return pl.CostEstimate(flops=int(flops) // 8, bytes_accessed=int(moved) // 8, transcendentals=0)


def table_hot(table, count):
    return (table[:, None] == jnp.arange(count, dtype=jnp.int32)[None, :]).astype(f32)


def swap(rows, axis, mask):
    count = lax.axis_size(axis)
    return lax.ppermute(rows, axis, [(i, i ^ mask) for i in range(count)])


def after(value, *others):
    return lax.optimization_barrier((value,) + tuple(jax.tree.leaves(others)))[0]


def after_all(values, *others):
    leaves = tuple(jax.tree.leaves(others))
    return lax.optimization_barrier(tuple(values) + leaves)[: len(values)]


def ring_gather(rows, move):
    half = rows.shape[0] // 2
    first, second = move(rows, 0), move(rows, 1)
    return [rows, first, second, move(first[:half], 1), move(second[half:], 0)]


def ring_sum(parts, move):
    half = parts[3].shape[0]
    left = move(parts[3], 0)
    right = move(parts[4], 1)
    to_second = jnp.concatenate(
        [(parts[2][:half].astype(f32) + left.astype(f32)).astype(bf16), parts[2][half:]], axis=0
    )
    to_first = jnp.concatenate(
        [parts[1][:half], (parts[1][half:].astype(f32) + right.astype(f32)).astype(bf16)], axis=0
    )
    first = move(to_first, 0)
    second = move(to_second, 1)
    return parts[0].astype(f32) + first.astype(f32) + second.astype(f32)


def in_plane(rows, way):
    return swap(rows, "tensor", 1 + way)


def gather_parts(rows):
    count = lax.axis_size("tensor")
    if count == 4:
        return ring_gather(rows, in_plane)
    return [rows] + [swap(rows, "tensor", r) for r in range(1, count)]


def sum_parts(parts):
    count = lax.axis_size("tensor")
    if count == 4:
        return ring_sum(parts, in_plane)
    arrived = [swap(parts[r], "tensor", r) for r in range(1, count)]
    return sum([part.astype(f32) for part in arrived], parts[0].astype(f32))


def over_experts(rows):
    experts_axis = lax.axis_size("expert")
    blocks = rows.reshape(experts_axis, rows.shape[0] // experts_axis, rows.shape[1])
    return lax.all_to_all(blocks, "expert", 0, 0, tiled=True).reshape(rows.shape)


def add_low(left, right):
    return (left.astype(f32) + right.astype(f32)).astype(bf16)


def total_blocks(near, far):
    rest = add_low(near, swap(far, "expert", 1))
    rest = ring_sum([rest[0:4], rest[4:8], rest[8:12], rest[12:14], rest[14:16]], in_plane).astype(bf16)
    own = rest[0].astype(f32)
    for m in range(1, 4):
        own = own + swap(rest[m], "expert", 2 * m).astype(f32)
    own = own.astype(bf16)
    rest = jnp.stack([own] + [swap(own, "expert", 2 * m) for m in range(1, 4)])
    near = jnp.concatenate(ring_gather(rest, in_plane), axis=0)
    return near, swap(near, "expert", 1)


def project_kernel(long_local, inputs, gain, w_query, w_key, w_value, normed, query, pair, near, held):
    @pl.when(pl.program_id(0) == 0)
    def _():
        rows = inputs[...].astype(f32)
        scale = lax.rsqrt(jnp.mean(rows * rows, axis=-1, keepdims=True) + 1e-06)
        held[...] = (rows * scale * gain[...].astype(f32)).astype(bf16)
        normed[...] = held[...]

    rows = held[...]
    query[...] = mm(rows, w_query[...]).astype(bf16)
    keys = mm(rows, w_key[...]).astype(bf16)
    values = mm(rows, w_value[...]).astype(bf16)
    pair[:long_local] = keys[:long_local]
    pair[long_local:] = values[:long_local]
    short = keys.shape[0] - long_local
    near[:short] = keys[long_local:]
    near[short:] = values[long_local:]


def project(inputs, gain, w_query, w_key, w_value, long_local):
    rows, width = inputs.shape
    short = rows - long_local
    step = 256
    whole = lambda count: pl.BlockSpec((count, width), lambda i: (0, 0))
    cut = lambda count: pl.BlockSpec((count, step), lambda i: (0, i))
    return pl.pallas_call(
        partial(project_kernel, long_local),
        grid=(width // step,),
        in_specs=[whole(rows), whole(1), cut(width), cut(width), cut(width)],
        out_specs=[whole(rows), cut(rows), cut(2 * long_local), cut(2 * short)],
        out_shape=[
            jax.ShapeDtypeStruct((rows, width), bf16),
            jax.ShapeDtypeStruct((rows, width), bf16),
            jax.ShapeDtypeStruct((2 * long_local, width), bf16),
            jax.ShapeDtypeStruct((2 * short, width), bf16),
        ],
        scratch_shapes=[pltpu.VMEM((rows, width), bf16)],
        compiler_params=params(),
        cost_estimate=cost(6 * rows * width * width, 6 * width * width + 10 * rows * width),
        name="project",
    )(inputs, gain.reshape(1, width), w_query, w_key, w_value)


def project_others_kernel(local, gain, w_key, w_value, *refs):
    sources, (normed, pairs, held) = refs[:-3], refs[-3:]

    @pl.when(pl.program_id(0) == 0)
    def _():
        rows = jnp.concatenate([source[...] for source in sources], axis=0).astype(f32)
        scale = lax.rsqrt(jnp.mean(rows * rows, axis=-1, keepdims=True) + 1e-06)
        held[...] = (rows * scale * gain[...].astype(f32)).astype(bf16)
        normed[...] = held[...]

    keys = mm(held[...], w_key[...]).astype(bf16)
    values = mm(held[...], w_value[...]).astype(bf16)
    for r in range(keys.shape[0] // local):
        pairs[2 * r * local : (2 * r + 1) * local] = keys[r * local : (r + 1) * local]
        pairs[(2 * r + 1) * local : (2 * r + 2) * local] = values[r * local : (r + 1) * local]


def project_others(sources, gain, w_key, w_value, local):
    rows = sum(source.shape[0] for source in sources)
    width = gain.shape[0]
    step = 256
    whole = lambda count: pl.BlockSpec((count, width), lambda i: (0, 0))
    cut = lambda count: pl.BlockSpec((count, step), lambda i: (0, i))
    return pl.pallas_call(
        partial(project_others_kernel, local),
        grid=(width // step,),
        in_specs=[whole(1), cut(width), cut(width)] + [whole(source.shape[0]) for source in sources],
        out_specs=[whole(rows), cut(2 * rows)],
        out_shape=[
            jax.ShapeDtypeStruct((rows, width), bf16),
            jax.ShapeDtypeStruct((2 * rows, width), bf16),
        ],
        scratch_shapes=[pltpu.VMEM((rows, width), bf16)],
        compiler_params=params(),
        cost_estimate=cost(4 * rows * width * width, 4 * width * width + 8 * rows * width),
        name="project_others",
    )(gain.reshape(1, width), w_key, w_value, *sources)


def key_value_views(pair, others, count, rows):
    views = [(pair, slice(0, rows), pair, slice(rows, 2 * rows))]
    for r in range(count - 1):
        at = 2 * r * rows
        views.append((others, slice(at, at + rows), others, slice(at + rows, at + 2 * rows)))
    return views


def forward_kernel(
    count, rows, dim, facts, query, pair, others, near, far_bias, near_bias, mixed, far_attend, near_attend, window
):
    place, far_len, near_len = facts[0], facts[1], facts[2]
    scale = 1.0 / math.sqrt(dim)
    views = key_value_views(pair, others, count, rows)
    short = near.shape[0] // 2
    reach = far_bias.shape[-1]
    for head in range(2):
        lanes = slice(head * dim, (head + 1) * dim)
        low = (query[:, lanes].astype(f32) * scale).astype(bf16)
        table = jnp.broadcast_to(far_bias[0, head : head + 1, :], (rows, reach))
        window[...] = pltpu.roll(table, reach - (rows - 1), 1, stride=1, stride_axis=0)
        scores = []
        for r in range(count):
            source = place ^ r
            start = pl.multiple_of(source * rows, rows)
            keys = views[r][0][views[r][1], lanes]
            part = mm(low[:rows], keys, NT) + window[:, pl.ds(start, rows)]
            spot = source * rows + lax.broadcasted_iota(jnp.int32, (1, rows), 1)
            scores.append(jnp.where(spot < far_len, part, -1e30))
        highest = scores[0]
        for part in scores[1:]:
            highest = jnp.maximum(highest, part)
        highest = jnp.max(highest, axis=-1, keepdims=True)
        grown = [jnp.exp(part - highest) for part in scores]
        whole = grown[0]
        for part in grown[1:]:
            whole = whole + part
        inverse = 1.0 / jnp.sum(whole, axis=-1, keepdims=True)
        out = jnp.zeros((rows, dim), f32)
        for r in range(count):
            attend = (grown[r] * inverse).astype(bf16)
            far_attend[head, :, r * rows : (r + 1) * rows] = attend
            out = out + mm(attend, views[r][2][views[r][3], lanes])
        mixed[:rows, lanes] = out.astype(bf16)

        table = jnp.broadcast_to(near_bias[0, head : head + 1, :], (short, 2 * short))
        bias = pltpu.roll(table, short + 1, 1, stride=1, stride_axis=0)[:, :short]
        part = mm(low[rows:], near[:short, lanes], NT) + bias
        spot = lax.broadcasted_iota(jnp.int32, (1, short), 1)
        part = jnp.where(spot < near_len, part, -1e30)
        part = jnp.exp(part - jnp.max(part, axis=-1, keepdims=True))
        attend = (part * (1.0 / jnp.sum(part, axis=-1, keepdims=True))).astype(bf16)
        near_attend[head] = attend
        mixed[rows:, lanes] = mm(attend, near[short:, lanes]).astype(bf16)


def attention_specs(count, rows, short, reach, tokens, first=0):
    cut = lambda size: pl.BlockSpec((size, 128), lambda i, *_: (0, i + first))
    parts = [cut(2 * rows), cut(2 * (count - 1) * rows)]
    table = lambda size: pl.BlockSpec((1, 2, size), lambda i, *_: (i + first, 0, 0))
    weights = lambda size, span: pl.BlockSpec((2, size, span), lambda i, *_: (i + first, 0, 0))
    return (
        cut(tokens),
        parts,
        cut(2 * short),
        [table(reach), table(2 * short)],
        [weights(rows, count * rows), weights(short, short)],
    )


def attend_forward(facts, query, parts, near, far_bias, near_bias, count, rows, dim):
    tokens, width = query.shape
    heads = width // dim
    short = near.shape[0] // 2
    reach = far_bias.shape[-1]
    cut, part_specs, near_spec, tables, weights = attention_specs(count, rows, short, reach, tokens)
    return pl.pallas_call(
        partial(forward_kernel, count, rows, dim),
        grid_spec=pltpu.PrefetchScalarGridSpec(
            num_scalar_prefetch=1,
            grid=(heads // 2,),
            in_specs=[cut] + part_specs + [near_spec] + tables,
            out_specs=[cut] + weights,
            scratch_shapes=[pltpu.VMEM((rows, reach), f32)],
        ),
        out_shape=[
            jax.ShapeDtypeStruct((tokens, width), bf16),
            jax.ShapeDtypeStruct((heads, rows, count * rows), bf16),
            jax.ShapeDtypeStruct((heads, short, short), bf16),
        ],
        compiler_params=params(),
        cost_estimate=cost(40 * heads * rows * rows * count * dim, 12 * width * rows * count),
        name="attend_forward",
    )(facts, query, *parts, near, far_bias, near_bias)


def backward_kernel(
    count,
    rows,
    dim,
    facts,
    query,
    grad,
    pair,
    others,
    near,
    far_attend,
    near_attend,
    grad_query,
    grad_pair,
    grad_others,
    grad_near,
    far_sums,
    near_sums,
    window,
    near_window,
):
    place = facts[0]
    scale = 1.0 / math.sqrt(dim)
    views = key_value_views(pair, others, count, rows)
    grad_views = key_value_views(grad_pair, grad_others, count, rows)
    short = near.shape[0] // 2
    reach = window.shape[1]

    @pl.when(pl.program_id(0) == 0)
    def _():
        window[...] = jnp.zeros_like(window)
        near_window[...] = jnp.zeros_like(near_window)

    def reversal(size):
        up = lax.broadcasted_iota(jnp.int32, (size, size), 0)
        across = lax.broadcasted_iota(jnp.int32, (size, size), 1)
        return (up + across == size - 1).astype(bf16)

    far_turn = reversal(rows)
    near_turn = far_turn if short == rows else reversal(short)
    for head in range(2):
        lanes = slice(head * dim, (head + 1) * dim)
        low = query[:, lanes]
        grad_low = grad[:, lanes]
        turned = jnp.transpose((low.astype(f32) * scale), (1, 0)).astype(bf16)
        grad_turned = jnp.transpose(grad_low.astype(f32), (1, 0)).astype(bf16)
        attends, grads = [], []
        inner = jnp.zeros((rows, 1), f32)
        for r in range(count):
            attend = far_attend[head, :, r * rows : (r + 1) * rows]
            part = mm(grad_low[:rows], views[r][2][views[r][3], lanes], NT)
            inner = inner + jnp.sum(attend.astype(f32) * part, axis=-1, keepdims=True)
            attends.append(attend)
            grads.append(part)
        out = jnp.zeros((rows, dim), f32)
        for r in range(count):
            start = pl.multiple_of((place ^ r) * rows, rows)
            scores = (attends[r].astype(f32) * (grads[r] - inner)).astype(bf16)
            window[:, pl.ds(start, rows)] = mm(far_turn, scores)
            out = out + mm(scores, views[r][0][views[r][1], lanes])
            grad_keys = mm(turned[:, :rows], scores)
            grad_values = mm(grad_turned[:, :rows], attends[r])
            view = grad_views[r]
            view[0][view[1], lanes] = jnp.transpose(grad_keys, (1, 0)).astype(bf16)
            view[2][view[3], lanes] = jnp.transpose(grad_values, (1, 0)).astype(bf16)
        grad_query[:rows, lanes] = (out * scale).astype(bf16)
        rolled = pltpu.roll(window[...], 0, 1, stride=1, stride_axis=0)
        far_sums[0, head : head + 1, :] = jnp.sum(rolled, axis=0, keepdims=True)

        attend = near_attend[head]
        part = mm(grad_low[rows:], near[short:, lanes], NT)
        wide = attend.astype(f32)
        part = wide * (part - jnp.sum(wide * part, axis=-1, keepdims=True))
        scores = part.astype(bf16)
        near_window[:, :short] = mm(near_turn, scores)
        rolled = pltpu.roll(near_window[...], 0, 1, stride=1, stride_axis=0)
        near_sums[0, head : head + 1, :] = jnp.sum(rolled, axis=0, keepdims=True)
        grad_query[rows:, lanes] = (mm(scores, near[:short, lanes]) * scale).astype(bf16)
        grad_keys = mm(turned[:, rows:], scores)
        grad_values = mm(grad_turned[:, rows:], attend)
        grad_near[:short, lanes] = jnp.transpose(grad_keys, (1, 0)).astype(bf16)
        grad_near[short:, lanes] = jnp.transpose(grad_values, (1, 0)).astype(bf16)


def attend_backward(facts, query, grad, parts, near, weights, reach, count, rows, dim, half):
    tokens, width = query.shape
    pairs = width // dim // 4
    wide = width // 2
    short = near.shape[0] // 2
    cut, part_specs, near_spec, _, weight_specs = attention_specs(
        count, rows, short, reach, tokens, half * pairs
    )
    cut_out, part_outs, near_out, tables, _ = attention_specs(count, rows, short, reach, tokens)
    return pl.pallas_call(
        partial(backward_kernel, count, rows, dim),
        grid_spec=pltpu.PrefetchScalarGridSpec(
            num_scalar_prefetch=1,
            grid=(pairs,),
            in_specs=[cut, cut] + part_specs + [near_spec] + weight_specs,
            out_specs=[cut_out] + part_outs + [near_out] + tables,
            scratch_shapes=[pltpu.VMEM((rows, reach), f32), pltpu.VMEM((short, 2 * short), f32)],
        ),
        out_shape=[
            jax.ShapeDtypeStruct((size, wide), bf16)
            for size in (tokens, 2 * rows, 2 * (count - 1) * rows, 2 * short)
        ]
        + [
            jax.ShapeDtypeStruct((pairs, 2, reach), f32),
            jax.ShapeDtypeStruct((pairs, 2, 2 * short), f32),
        ],
        compiler_params=params(),
        cost_estimate=cost(50 * width // dim * rows * rows * count * dim, 8 * width * rows * count),
        name="attend_backward",
    )(facts, query, grad, *parts, near, *weights)


def normed_grads_kernel(local, count, *refs):
    grads, (w_query, w_key, w_value) = refs[:8], refs[8:11]
    own, own_short, away = refs[11:]
    half = pl.program_id(0)

    @pl.when(half == 0)
    def _():
        own[...] = jnp.zeros_like(own)
        own_short[...] = jnp.zeros_like(own_short)
        away[...] = jnp.zeros_like(away)

    for which in range(2):

        @pl.when(half == which)
        def _():
            query, pair, others, near = grads[4 * which : 4 * which + 4]
            short = near.shape[0] // 2
            full = mm(query[...], w_query[...], NT)
            own[...] += full[:local] + mm(pair[:local], w_key[...], NT) + mm(pair[local:], w_value[...], NT)
            own_short[...] += (
                full[local:] + mm(near[:short], w_key[...], NT) + mm(near[short:], w_value[...], NT)
            )
            for r in range(count - 1):
                at = 2 * r * local
                away[r * local : (r + 1) * local] += mm(
                    others[at : at + local], w_key[...], NT
                ) + mm(others[at + local : at + 2 * local], w_value[...], NT)


def normed_grads(halves, w_query, w_key, w_value, local, count):
    width = w_query.shape[0]
    wide = width // 2
    short = halves[0][3].shape[0] // 2
    arrays = [array for half in halves for array in half[:4]]
    cut = pl.BlockSpec((width, wide), lambda i: (0, i))
    return pl.pallas_call(
        partial(normed_grads_kernel, local, count),
        grid=(2,),
        in_specs=[pl.BlockSpec(array.shape, lambda i: (0, 0)) for array in arrays] + [cut] * 3,
        out_specs=[
            pl.BlockSpec((size, width), lambda i: (0, 0)) for size in (local, short, (count - 1) * local)
        ],
        out_shape=[
            jax.ShapeDtypeStruct((size, width), f32) for size in (local, short, (count - 1) * local)
        ],
        compiler_params=params(),
        cost_estimate=cost(4 * count * local * width * width, 8 * count * local * width),
        name="normed_grads",
    )(*arrays, w_query, w_key, w_value)


def expert_kernel(chunks, capacity, padded, lanes_used, facts, rows_in, grads_in, *refs):
    sources, rest = refs[: 3 * chunks], refs[3 * chunks :]
    middles, (out_ref, grad_ref) = rest[: 3 * chunks], rest[3 * chunks : 3 * chunks + 2]
    held, sems = rest[3 * chunks + 2 : 6 * chunks + 2], rest[6 * chunks + 2]
    rows = rows_in.shape[0]
    groups = rows // padded
    first = pl.program_id(0) == 0

    def copy(i):
        index = facts[4] if i < 3 else i % 3
        return pltpu.make_async_copy(sources[i].at[index], held[i], sems.at[i])

    @pl.when(first)
    def _():
        for i in range(3 * chunks):
            copy(i).start()
        for i in range(3 * chunks):
            copy(i).wait()

    slots = rows_in[...]
    grads = grads_in[...]
    spare = 16 - (padded - capacity)
    lanes = lax.broadcasted_iota(jnp.int32, (padded, 128), 1)
    match = lax.broadcasted_iota(jnp.int32, (padded, 128), 0) == lanes
    columns = []
    for g in range(groups):
        tail = rows_in[pl.ds((g + 1) * padded - 16, 16), :128].astype(f32)
        line = tail[spare : spare + 1] + tail[spare + 1 : spare + 2]
        columns.append(jnp.sum(jnp.where(match, line, 0.0), axis=-1, keepdims=True))
    gate_column = jnp.concatenate(columns, axis=0)

    lows = []
    slope = math.sqrt(2.0 / math.pi)
    for c in range(chunks):
        gate_pre = mm(slots, held[3 * c][...], NT)
        up_pre = mm(slots, held[3 * c + 1][...], NT)
        grad_hidden = mm(grads, held[3 * c + 2][...], NT) * gate_column
        square = gate_pre * gate_pre
        curve = jnp.tanh(slope * gate_pre * (1.0 + 0.044715 * square))
        side = 0.5 * (1.0 + curve)
        bent = gate_pre * side
        hidden = bent * up_pre
        bent_slope = side + 0.5 * slope * gate_pre * (1.0 - curve * curve) * (
            1.0 + 3.0 * 0.044715 * square
        )
        gate_low = (grad_hidden * up_pre * bent_slope).astype(bf16)
        up_low = (grad_hidden * bent).astype(bf16)
        middles[3 * c][...] = (hidden * gate_column).astype(bf16)
        middles[3 * c + 1][...] = gate_low
        middles[3 * c + 2][...] = up_low
        lows.append((gate_low, up_low, hidden.astype(bf16)))
    left = [jnp.concatenate([low[k] for low in lows], axis=1) for k in range(3)]
    right = [
        jnp.concatenate([held[3 * c + k][...] for c in range(chunks)], axis=0) for k in range(3)
    ]
    out = mm(left[2], right[2])
    grad_out = mm(left[0], right[0]) + mm(left[1], right[1])
    out_ref[...] = out.astype(bf16)
    grad_ref[...] = grad_out.astype(bf16)

    grad_gate = jnp.sum(out * grads.astype(f32), axis=-1, keepdims=True)
    lanes = lax.broadcasted_iota(jnp.int32, (padded, lanes_used), 1)
    up = lax.broadcasted_iota(jnp.int32, (padded, lanes_used), 0)
    match = up + facts[5] * padded == lanes
    row = lax.broadcasted_iota(jnp.int32, (16, lanes_used), 0)
    for g in range(groups):
        values = jnp.where(match, grad_gate[g * padded : (g + 1) * padded], 0.0)
        line = jnp.sum(values, axis=0, keepdims=True)
        high = line.astype(bf16).astype(f32)
        tail = grad_out[(g + 1) * padded - 16 : (g + 1) * padded, :lanes_used]
        tail = jnp.where(row == spare, high, jnp.where(row == spare + 1, line - high, tail))
        grad_ref[pl.ds((g + 1) * padded - 16, 16), :lanes_used] = tail.astype(bf16)


def expert_pass(facts, slots, grads, own, other, capacity, padded, lanes_used):
    rows, width = slots.shape
    units = own[0].shape[1]
    chunks = 1 if other is None else 2
    sources = list(own) + ([] if other is None else [other] * 3)
    tile = rows
    cut = lambda size: pl.BlockSpec((tile, size), lambda i, f: (i, 0))
    outs = pl.pallas_call(
        partial(expert_kernel, chunks, capacity, padded, lanes_used),
        grid_spec=pltpu.PrefetchScalarGridSpec(
            num_scalar_prefetch=1,
            grid=(rows // tile,),
            in_specs=[cut(width)] * 2 + [pl.BlockSpec(memory_space=pl.ANY)] * (3 * chunks),
            out_specs=[cut(units)] * (3 * chunks) + [cut(width)] * 2,
            scratch_shapes=[pltpu.VMEM((units, width), bf16)] * (3 * chunks)
            + [pltpu.SemaphoreType.DMA((3 * chunks,))],
        ),
        out_shape=[jax.ShapeDtypeStruct((rows, units), bf16)] * (3 * chunks)
        + [jax.ShapeDtypeStruct((rows, width), bf16)] * 2,
        compiler_params=params(),
        cost_estimate=cost(12 * chunks * rows * units * width, 8 * rows * width),
        name="expert_pass",
    )(facts, slots, grads, *sources)
    middles = [outs[3 * c : 3 * c + 3] for c in range(chunks)]
    return middles, outs[3 * chunks], outs[3 * chunks + 1]


def weight_body(count, packed, extra, facts, *refs):
    kinds = [refs[k * count : (k + 1) * count] for k in range(5)]
    outs = refs[5 * count + extra :]
    targets = outs[1:4] if packed else outs[:3]
    held, sems = refs[-6:-1], refs[-1]
    step = pl.program_id(0)
    slot = step % 2

    def fetch(index, side):
        for r in range(count):

            @pl.when(index == r)
            def _():
                for k in range(5):
                    pltpu.make_async_copy(kinds[k][r], held[k].at[side], sems.at[side, k]).start()

    @pl.when(step == 0)
    def _():
        fetch(step, slot)

    @pl.when(step + 1 < count)
    def _():
        fetch(step + 1, 1 - slot)

    for k in range(5):
        pltpu.make_async_copy(kinds[k][0], held[k].at[slot], sems.at[slot, k]).wait()

    @pl.when(step == 0)
    def _():
        for target in targets:
            target[...] = jnp.zeros_like(target)

    rows, grads = held[0][slot], held[1][slot]
    lefts = ((held[3], rows), (held[4], rows), (held[2], grads))
    for target, (left, right) in zip(targets, lefts):
        target[0] += mm(left[slot], right, TN)

    if packed:

        @pl.when(step == count - 1)
        def _():
            for i in range(3):
                outs[0][i] = targets[i][0].astype(bf16)


def weight_pass(facts, slots, grads, middles, before, local, packed):
    count = len(slots)
    rows, width = slots[0].shape
    units = middles[0][0].shape[1]
    anywhere = pl.BlockSpec(memory_space=pl.ANY)
    if packed:
        out_specs = [pl.BlockSpec((3, units, width), lambda i, f: (0, 0, 0))]
        out_shape = [jax.ShapeDtypeStruct((3, units, width), bf16)]
        totals = [pltpu.VMEM((1, units, width), f32)] * 3
    else:
        out_specs = [pl.BlockSpec((1, units, width), lambda i, f: (f[4], 0, 0))] * 3
        out_shape = [jax.ShapeDtypeStruct((local, units, width), f32)] * 3
        totals = []
    kinds = [list(slots), list(grads)] + [[middle[k] for middle in middles] for k in range(3)]
    body = partial(weight_body, count, packed, len(before))
    return pl.pallas_call(
        body,
        grid_spec=pltpu.PrefetchScalarGridSpec(
            num_scalar_prefetch=1,
            grid=(count,),
            in_specs=[anywhere] * (5 * count + len(before)),
            out_specs=out_specs,
            scratch_shapes=totals
            + [pltpu.VMEM((2, rows, width), bf16)] * 2
            + [pltpu.VMEM((2, rows, units), bf16)] * 3
            + [pltpu.SemaphoreType.DMA((2, 5))],
        ),
        out_shape=out_shape,
        input_output_aliases={1 + 5 * count + i: i for i in range(len(before))},
        compiler_params=params(),
        cost_estimate=cost(6 * count * rows * units * width, 8 * count * rows * width),
        name="weight_pass",
    )(facts, *[array for kind in kinds for array in kind], *before)


def fill_kernel(facts, source, *refs):
    for i in range(3):
        refs[-3 + i][0] = source[i].astype(f32)


def weight_fill(facts, source, before):
    _, units, width = source.shape
    tile = units // 4
    anywhere = pl.BlockSpec(memory_space=pl.ANY)
    return pl.pallas_call(
        fill_kernel,
        grid_spec=pltpu.PrefetchScalarGridSpec(
            num_scalar_prefetch=1,
            grid=(4,),
            in_specs=[pl.BlockSpec((3, tile, width), lambda i, f: (0, i, 0))] + [anywhere] * 3,
            out_specs=[pl.BlockSpec((1, tile, width), lambda i, f: (f[6], i, 0))] * 3,
        ),
        out_shape=[jax.ShapeDtypeStruct(array.shape, f32) for array in before],
        input_output_aliases={2 + i: i for i in range(3)},
        compiler_params=params(),
        cost_estimate=cost(0, 6 * source.size),
        name="weight_fill",
    )(facts, source, *before)


def place_kernel(capacity, padded, block, local, turns, routes, rows, slots_out, wide_out, rows_out):
    experts_axis = block // padded
    tokens = rows.shape[0]
    experts = experts_axis * local
    number = lax.broadcasted_iota(jnp.int32, (experts, tokens), 0)
    picks = [number == routes[k : k + 1] for k in range(routes.shape[0])]
    named = picks[0]
    for pick in picks[1:]:
        named = named | pick
    earlier = lax.broadcasted_iota(jnp.int32, (tokens, tokens), 0) < lax.broadcasted_iota(
        jnp.int32, (tokens, tokens), 1
    )
    before = mm(named.astype(bf16), earlier.astype(bf16))
    places = []
    for k, pick in enumerate(picks):
        route = routes[k : k + 1]
        position = jnp.sum(jnp.where(pick, before, 0.0), axis=0, keepdims=True).astype(jnp.int32)
        owner = route // local
        turn = jnp.where(owner % 2 == 0, turns[:, 0:1], turns[:, 1:2])
        which = (route % local) ^ turn
        slot = which * block + owner * padded + position
        slots_out[k : k + 1] = jnp.where(position < capacity, slot, -1)
        slot = (owner * local + which) * padded + position
        places.append(jnp.where(position < capacity, slot, -1))
        wide_out[k : k + 1] = places[k]
    spots = lax.broadcasted_iota(jnp.int32, (local * block, tokens), 0)
    hot = spots == places[0]
    for slot in places[1:]:
        hot = hot | (spots == slot)
    rows_out[...] = mm(hot.astype(bf16), rows[...]).astype(bf16)


def place_rows(turns, routes, rows, capacity, padded, block, local):
    tops, tokens = routes.shape
    width = rows.shape[1]
    return pl.pallas_call(
        partial(place_kernel, capacity, padded, block, local),
        out_shape=[
            jax.ShapeDtypeStruct((tops, tokens), jnp.int32),
            jax.ShapeDtypeStruct((tops, tokens), jnp.int32),
            jax.ShapeDtypeStruct((local * block, width), bf16),
        ],
        compiler_params=pltpu.CompilerParams(vmem_limit_bytes=VMEM_BYTES),
        cost_estimate=cost(2 * local * block * tokens * width, 4 * local * block * width),
        name="place_rows",
    )(turns, routes, rows)


def route_kernel(
    capacity, padded, mixed, w_proj, inputs, gain, router, routes, slots, resid, moe, probs, gates, out
):
    local, block, width = out.shape
    tokens = inputs.shape[0]
    sums = inputs[...].astype(f32) + mm(mixed[...], w_proj[...])
    resid[...] = sums
    scale = lax.rsqrt(jnp.mean(sums * sums, axis=-1, keepdims=True) + 1e-06)
    low = (sums * scale * gain[...].astype(f32)).astype(bf16)
    moe[...] = low
    logits = mm(router[...], low, NT)
    grown = jnp.exp(logits - jnp.max(logits, axis=0, keepdims=True))
    share = grown / jnp.sum(grown, axis=0, keepdims=True)
    probs[...] = share
    number = lax.broadcasted_iota(jnp.int32, share.shape, 0)
    spots = lax.broadcasted_iota(jnp.int32, (local * block, tokens), 0)
    row = lax.broadcasted_iota(jnp.int32, (16, tokens), 0)
    hot = None
    lines = jnp.zeros((16, local * block), f32)
    for k in range(routes.shape[0]):
        gate = jnp.sum(jnp.where(number == routes[k : k + 1], share, 0.0), axis=0, keepdims=True)
        gates[k : k + 1] = gate
        high = gate.astype(bf16).astype(f32)
        both = jnp.where(row == 0, high, jnp.where(row == 1, gate - high, 0.0)).astype(bf16)
        mine = (spots == slots[k : k + 1]).astype(bf16)
        lines = lines + mm(both, mine, NT)
        hot = mine if hot is None else hot + mine
    filled = mm(hot, low).astype(bf16)
    spare = 16 - (padded - capacity)
    row = lax.broadcasted_iota(jnp.int32, (16, padded), 0)
    for j in range(local):
        out[j] = filled[j * block : (j + 1) * block]
        for g in range(block // padded):
            at = j * block + g * padded
            tail = filled[at + padded - 16 : at + padded, :padded].astype(f32)
            line = lines[:, at : at + padded]
            tail = jnp.where(row == spare, line[0:1], jnp.where(row == spare + 1, line[1:2], tail))
            out[j, pl.ds((g + 1) * padded - 16, 16), :padded] = tail.astype(bf16)


def route_rows(mixed, w_proj, inputs, gain, router, routes, slots, capacity, padded, block, local):
    tokens, width = inputs.shape
    tops = routes.shape[0]
    return pl.pallas_call(
        partial(route_kernel, capacity, padded),
        out_shape=[
            jax.ShapeDtypeStruct((tokens, width), f32),
            jax.ShapeDtypeStruct((tokens, width), bf16),
            jax.ShapeDtypeStruct((router.shape[0], tokens), f32),
            jax.ShapeDtypeStruct((tops, tokens), f32),
            jax.ShapeDtypeStruct((local, block, width), bf16),
        ],
        compiler_params=pltpu.CompilerParams(vmem_limit_bytes=VMEM_BYTES),
        cost_estimate=cost(4 * local * block * tokens * width, 12 * local * block * width),
        name="route_rows",
    )(mixed, w_proj, inputs, gain.reshape(1, width), router, routes, slots)


def merge_kernel(
    capacity, padded, count, cotangent, resid, probs, moe, router, gain, w_proj, routes, slots, columns, *refs
):
    local = len(refs) - 5
    grads = refs[:local]
    grad_resid, grad_mixed, gain_grad, router_grad, branch_out = refs[local:]
    block = grads[0].shape[0]
    tokens = cotangent.shape[0]
    tops = routes.shape[0]
    spare = 16 - (padded - capacity)
    pieces = []
    for j in range(local):
        for g in range(block // padded):
            tail = grads[j][pl.ds((g + 1) * padded - 16, 16), : count * padded].astype(f32)
            line = tail[spare : spare + 1] + tail[spare + 1 : spare + 2]
            folded = line[:, :padded]
            for r in range(1, count):
                folded = folded + line[:, r * padded : (r + 1) * padded]
            pieces.append(folded)
    line = jnp.concatenate(pieces, axis=1)
    row = lax.broadcasted_iota(jnp.int32, (16, line.shape[1]), 0)
    high = line.astype(bf16).astype(f32)
    rest = line - high
    middle = rest.astype(bf16).astype(f32)
    stack = jnp.where(row == 0, high, jnp.where(row == 1, middle, jnp.where(row == 2, rest - middle, 0.0)))
    stack = stack.astype(bf16)
    share = probs[...]
    number = lax.broadcasted_iota(jnp.int32, share.shape, 0)
    spots = lax.broadcasted_iota(jnp.int32, (local * block, tokens), 0)
    grad_probs = jnp.zeros_like(share)
    for k in range(tops):
        picked = jnp.sum(mm(stack, (spots == slots[k : k + 1]).astype(bf16)), axis=0, keepdims=True)
        grad_probs = grad_probs + jnp.where(number == routes[k : k + 1], picked, 0.0)
    grad_logits = share * (grad_probs - jnp.sum(share * grad_probs, axis=0, keepdims=True))
    grad_logits = grad_logits.astype(bf16)
    router_grad[...] = mm(grad_logits, moe[...])
    grad_moe = mm(grad_logits, router[...], TN)
    spots = lax.broadcasted_iota(jnp.int32, (tokens, block), 1)
    for j in range(local):
        hot = None
        for k in range(tops):
            mine = spots + j * block == columns[:, k : k + 1]
            hot = mine if hot is None else hot | mine
        grad_moe = grad_moe + mm(hot.astype(bf16), grads[j][...])
    rows = resid[...]
    scale = lax.rsqrt(jnp.mean(rows * rows, axis=-1, keepdims=True) + 1e-06)
    normed = rows * scale
    gain_grad[...] = jnp.sum(grad_moe * normed, axis=0, keepdims=True)
    lifted = grad_moe * gain[...].astype(f32)
    spread = jnp.mean(lifted * normed, axis=-1, keepdims=True)
    back = cotangent[...].astype(f32) + scale * (lifted - normed * spread)
    grad_resid[...] = back
    branch = back.astype(bf16)
    grad_mixed[...] = mm(branch, w_proj[...], NT).astype(bf16)
    branch_out[...] = branch


def merge_rows(
    cotangent, resid, probs, moe, router, gain, w_proj, routes, slots, grads, capacity, padded, count
):
    tokens, width = cotangent.shape
    return pl.pallas_call(
        partial(merge_kernel, capacity, padded, count),
        out_shape=[
            jax.ShapeDtypeStruct((tokens, width), f32),
            jax.ShapeDtypeStruct((tokens, width), bf16),
            jax.ShapeDtypeStruct((1, width), f32),
            jax.ShapeDtypeStruct((router.shape[0], width), f32),
            jax.ShapeDtypeStruct((tokens, width), bf16),
        ],
        compiler_params=pltpu.CompilerParams(vmem_limit_bytes=VMEM_BYTES),
        cost_estimate=cost(6 * tokens * width * width, 20 * tokens * width),
        name="merge_rows",
    )(
        cotangent, resid, probs, moe, router, gain.reshape(1, width), w_proj, routes, slots,
        jnp.transpose(slots), *grads,
    )


def blocks_kernel(
    local, facts, normed, normed_others, mixed, grad_query, grad_pair, grad_others, grad_near, branch, small, near, far
):
    step = pl.program_id(0)
    number = facts[3]
    group = step ^ (number // 4)
    share = (near.shape[1] - 8) // 4
    short = grad_near.shape[0] // 2
    own, own_short = normed[:local], normed[local:]

    def keyed(which):
        part = mm(own, grad_pair[which * local : (which + 1) * local], TN)
        part = part + mm(own_short, grad_near[which * short : (which + 1) * short], TN)
        for r in range(normed_others.shape[0] // local):
            at = (2 * r + which) * local
            part = part + mm(normed_others[r * local : (r + 1) * local], grad_others[at : at + local], TN)
        return part

    made = [mm(normed[...], grad_query[...], TN), keyed(0), keyed(1), mm(mixed[...], branch[...], TN)]
    made = [part.astype(bf16) for part in made]
    for s in range(4):
        spot = s ^ (number % 4)
        lines = [part[s * share : (s + 1) * share] for part in made]
        extra = jnp.zeros((8, small.shape[1]), bf16)
        if s < 3:
            extra = jnp.where(group == 0, small[s * 8 : s * 8 + 8], extra)
        whole = jnp.concatenate(lines + [extra], axis=0)

        @pl.when(step < 4)
        def _():
            near[spot] = whole

        @pl.when(step >= 4)
        def _():
            far[spot] = whole


def weight_blocks(facts, lefts, rights, branch, small, local, half):
    tokens, width = lefts[0].shape
    wide = width // 2
    rows = 4 * width // 32 + 8
    cut = lambda count: pl.BlockSpec((count, width // 8), lambda i, f: (0, i ^ (f[3] // 4)))
    full = lambda count: pl.BlockSpec((count, wide), lambda i, f: (0, 0))
    out = lambda which: pl.BlockSpec((4, rows, wide), which)
    return pl.pallas_call(
        partial(blocks_kernel, local),
        grid_spec=pltpu.PrefetchScalarGridSpec(
            num_scalar_prefetch=1,
            grid=(8,),
            in_specs=[cut(left.shape[0]) for left in lefts]
            + [full(right.shape[0]) for right in rights]
            + [pl.BlockSpec((tokens, wide), lambda i, f: (0, half)), full(24)],
            out_specs=[
                out(lambda i, f: (jnp.minimum(i, 3), 0, 0)),
                out(lambda i, f: (jnp.maximum(i - 4, 0), 0, 0)),
            ],
        ),
        out_shape=[jax.ShapeDtypeStruct((16, rows, wide), bf16)] * 2,
        compiler_params=params(),
        cost_estimate=cost(8 * tokens * width * width, 4 * width * width),
        name="weight_blocks",
    )(facts, *lefts, *rights, branch, small)


def unpack_kernel(facts, near, far, w_query, w_key, w_value, gain, *refs):
    query, key, value, proj, gain_grad, small = refs[-6:]
    step = pl.program_id(0)
    number = facts[3]
    group = step ^ (number // 4)
    share = (near.shape[1] - 8) // 4

    def spread(source):
        for s in range(4):
            block = source[s ^ (number % 4)].astype(f32)
            for which, out in enumerate((query, key, value, proj)):
                out[s * share : (s + 1) * share] = block[which * share : (which + 1) * share]
            if s < 3:

                @pl.when(group == 0)
                def _():
                    small[s * 8 : s * 8 + 8] = block[4 * share :]

    @pl.when(step < 4)
    def _():
        spread(near)

    @pl.when(step >= 4)
    def _():
        spread(far)

    sums = query[...] * w_query[...].astype(f32)
    sums = sums + key[...] * w_key[...].astype(f32)
    sums = sums + value[...] * w_value[...].astype(f32)
    column = jnp.sum(sums, axis=-1, keepdims=True)
    size = column.shape[0]
    match = lax.broadcasted_iota(jnp.int32, (size, size), 0) == lax.broadcasted_iota(
        jnp.int32, (size, size), 1
    )
    line = jnp.sum(jnp.where(match, column, 0.0), axis=0, keepdims=True)
    gain_grad[...] = line / gain[...].astype(f32)


def unpack_blocks(facts, near, far, w_query, w_key, w_value, gain, before, half):
    width = w_query.shape[0]
    wide = width // 2
    rows = near.shape[1]
    step = width // 8
    line = pl.BlockSpec((1, step), lambda i, f: (0, i ^ (f[3] // 4)))
    block = pl.BlockSpec((step, wide), lambda i, f: (i ^ (f[3] // 4), half))
    return pl.pallas_call(
        unpack_kernel,
        grid_spec=pltpu.PrefetchScalarGridSpec(
            num_scalar_prefetch=1,
            grid=(8,),
            in_specs=[
                pl.BlockSpec((4, rows, wide), lambda i, f: (jnp.minimum(i, 3), 0, 0)),
                pl.BlockSpec((4, rows, wide), lambda i, f: (jnp.maximum(i - 4, 0), 0, 0)),
                block,
                block,
                block,
                line,
            ]
            + [pl.BlockSpec(memory_space=pl.ANY)] * len(before),
            out_specs=[block, block, block, block, line, pl.BlockSpec((24, wide), lambda i, f: (0, 0))],
        ),
        out_shape=[jax.ShapeDtypeStruct((width, width), f32)] * 4
        + [jax.ShapeDtypeStruct((1, width), f32), jax.ShapeDtypeStruct((24, wide), f32)],
        input_output_aliases={7 + i: i for i in range(len(before))},
        compiler_params=params(),
        cost_estimate=cost(6 * width * width, 12 * width * width),
        name="unpack_blocks",
    )(facts, near, far, w_query, w_key, w_value, gain.reshape(1, width), *before)


def per_device(
    inputs,
    attn_gain,
    w_query,
    w_key,
    w_value,
    w_proj,
    rel_bias,
    moe_gain,
    w_router,
    w_gate,
    w_up,
    w_down,
    routes,
    long_buckets,
    short_buckets,
    long_lens,
    short_lens,
    cotangent,
):
    experts_axis = lax.axis_size("expert")
    tensor_axis = lax.axis_size("tensor")
    place = lax.axis_index("tensor")
    tok_count, width = inputs.shape
    top_count = routes.shape[1]
    short_len = (short_buckets.shape[0] + 1) // 2
    long_span = (long_buckets.shape[0] + 1) // 2
    long_local = tok_count - short_len
    bucket_count, heads = rel_bias.shape
    head_dim = width // heads
    experts = w_router.shape[1]
    local = experts // experts_axis
    capacity = (5 * tok_count * top_count + 4 * experts - 1) // (4 * experts)
    padded = (capacity + 2 + 15) // 16 * 16
    block = experts_axis * padded
    rel_table = rel_bias.astype(f32)
    here = lax.axis_index("expert")
    number = (here % 2) * 16 + place * 4 + here // 2
    paired = tensor_axis == 4 and local == 2
    routes_rows = jnp.transpose(routes)
    router = jnp.transpose(w_router)
    gate_turned = jnp.swapaxes(w_gate, 1, 2)
    up_turned = jnp.swapaxes(w_up, 1, 2)
    if paired:
        turns = jnp.stack([place % 2, place // 2]).astype(jnp.int32)
        which = jnp.where(here % 2 == 0, turns[0], turns[1])
        part_of = jnp.where(here % 2 == 0, turns[1], turns[0])
        shares = 2
    else:
        turns = jnp.zeros((2,), jnp.int32)
        which, part_of, shares = jnp.int32(0), place, tensor_axis
    facts = [place, long_lens[0], short_lens[0], number, which, part_of, 1 - which]
    facts = jnp.stack([jnp.asarray(fact, jnp.int32) for fact in facts])

    def trade(rows, other):
        pairs = []
        for e in range(experts_axis):
            mask = (2 if e % 2 == 0 else 1) if other else (1 if e % 2 == 0 else 2)
            pairs += [(e * tensor_axis + t, e * tensor_axis + (t ^ mask)) for t in range(tensor_axis)]
        return lax.ppermute(rows, ("expert", "tensor"), pairs)

    sources = gather_parts(inputs[:long_local])[1:]
    normed_low, query, pair, near = project(inputs, attn_gain, w_query, w_key, w_value, long_local)
    slots, wide_slots, grad_slots_in = place_rows(
        turns.reshape(1, 2), after(routes_rows, normed_low), cotangent, capacity, padded, block, local
    )

    def by_expert(rows):
        split = rows.reshape(experts_axis, local, padded, width)
        return [split[:, j].reshape(block, width) for j in range(local)]

    def by_device(parts):
        split = [part.reshape(experts_axis, 1, padded, width) for part in parts]
        return jnp.concatenate(split, axis=1).reshape(local * block, width)

    grad_whole = over_experts(grad_slots_in)
    grad_arrived = by_expert(grad_whole)
    normed_others, others = project_others(sources, attn_gain, w_key, w_value, long_local)
    parts = (pair, others)
    if paired:
        other = jnp.stack(
            [
                lax.dynamic_index_in_dim(array, 1 - which, 0, keepdims=False)
                for array in (gate_turned, up_turned, w_down)
            ]
        )
        other = trade(after(other, sources), False)

    reach = long_span + long_local
    first = long_span - long_local - long_local * place
    long_table = jnp.pad(long_buckets, (0, 1), constant_values=-1)
    long_hot = table_hot(lax.dynamic_slice_in_dim(long_table, first, reach, 0), bucket_count)
    short_hot = table_hot(jnp.pad(short_buckets, (0, 1), constant_values=-1), bucket_count)
    spread = lambda hot: jnp.einsum(
        "cb,bh->hc", hot, rel_table, precision=precise, preferred_element_type=f32
    ).reshape(heads // 2, 2, hot.shape[0])
    mixed, far_attend, near_attend = attend_forward(
        facts, query, parts, near, spread(long_hot), spread(short_hot),
        tensor_axis, long_local, head_dim,
    )
    resid, moe_low, probs, gates, slots_in = route_rows(
        mixed, w_proj, inputs, moe_gain, router, routes_rows, slots, capacity, padded, block, local
    )

    own = (gate_turned, up_turned, w_down)
    lanes_used = shares * padded
    if paired:

        run = lambda rows, grads: expert_pass(
            facts, rows, grads, own, other, capacity, padded, lanes_used
        )
        grads_c = trade(after(grad_arrived[0], other), True)
        grads_b = trade(after(grad_arrived[1], other), False)
        grads_d = trade(grads_b, True)
        rows_a = over_experts(after(slots_in[0], grad_whole))
        rows_c = trade(after(rows_a, grads_b, grads_c), True)
        rows_b = over_experts(after(slots_in[1], rows_a, grads_b, grads_c))
        pass_a = run(rows_a, grad_arrived[0])
        rows_b = trade(after(rows_b, pass_a[1]), False)
        pass_c = run(rows_c, grads_c)
        rows_d = trade(after(rows_b, pass_c[1]), True)
        kept = add_low(pass_a[2], trade(pass_c[2], True))
        kept = over_experts(kept)
        pass_b = run(rows_b, grads_b)
        pass_d = run(after(rows_d, pass_b[1]), grads_d)
        traded = add_low(pass_b[2], trade(pass_d[2], True))
        traded = trade(traded, False)
        grad_slots = [kept, over_experts(after(traded, kept))]

        passes = [pass_a, pass_c, pass_b, pass_d]
        slot_blocks = [rows_a, rows_c, rows_b, rows_d]
        grad_blocks = [grad_arrived[0], grads_c, grads_b, grads_d]
        (sent,) = weight_pass(
            facts, slot_blocks, grad_blocks, [after_all(made[0][1], pass_d[1]) for made in passes], (), local, True
        )
        weight_grads = weight_pass(
            facts, slot_blocks, grad_blocks, [after_all(made[0][0], sent) for made in passes], (), local, False
        )
        outs_c = trade(after(pass_c[1], traded), True)
        outs_d = trade(after(pass_d[1], traded), True)
        grad_slots[0] = after(grad_slots[0], weight_grads, outs_c, outs_d)
        outs_kept = add_low(pass_a[1], outs_c)
        outs_traded = trade(add_low(pass_b[1], outs_d), False)
        held_back = outs_traded
        sent = trade(after(sent, outs_traded), False)
        send_outs = lambda: over_experts(after(by_device([outs_kept, outs_traded]), grad_slots[1]))
    else:
        grad_blocks = [gather_parts(rows) for rows in grad_arrived]
        slot_blocks = [gather_parts(over_experts(slots_in[j])) for j in range(local)]
        weight_grads, passes = (), []
        for j in range(local):
            facts_j = facts.at[4].set(j)
            passes.append(
                [
                    expert_pass(facts_j, rows, grads, own, None, capacity, padded, lanes_used)
                    for rows, grads in zip(slot_blocks[j], grad_blocks[j])
                ]
            )
            weight_grads = weight_pass(
                facts_j, slot_blocks[j], grad_blocks[j], [made[0][0] for made in passes[j]], weight_grads, local, False
            )
        send_back = lambda which: [
            over_experts(sum_parts([made[which] for made in passes[j]]).astype(bf16)) for j in range(local)
        ]
        grad_slots = send_back(2)
        send_outs = lambda: by_device(send_back(1))
        held_back = grad_slots[0]

    grad_resid, grad_mixed, moe_gain_grad, router_grad, branch = merge_rows(
        cotangent, resid, probs, moe_low, router, moe_gain, w_proj, routes_rows, slots, grad_slots,
        capacity, padded, shares,
    )
    grad_mixed = after(grad_mixed, held_back)
    collect = lambda sums, hot: jnp.einsum(
        "hc,cb->bh",
        sums.reshape(heads // 2, hot.shape[0]),
        hot,
        precision=precise,
        preferred_element_type=f32,
    )
    quick = experts_axis == 8 and tensor_axis == 4
    wide = width // 2
    halves, rel_halves, sums = [], [], []
    for half in range(2):
        made = attend_backward(
            facts, query, grad_mixed, parts, near, (far_attend, near_attend), reach, tensor_axis, long_local,
            head_dim, half,
        )
        halves.append(made[:4])
        rel_halves.append(collect(made[4], long_hot) + collect(made[5], short_hot))
        if quick:
            rel_row = jnp.pad(rel_halves[half].reshape(1, -1), ((0, 0), (0, wide - rel_halves[half].size)))
            columns = slice(half * wide, (half + 1) * wide)
            small = jnp.concatenate([rel_row, moe_gain_grad[:, columns], router_grad[:, columns]], axis=0)
            small = jnp.pad(small, ((0, 24 - small.shape[0]), (0, 0))).astype(bf16)
            blocks = weight_blocks(
                facts, (normed_low, normed_others, mixed), made[:4], branch, small, long_local, half
            )
            grad_mixed = after(grad_mixed, blocks)
            sums.append(total_blocks(*blocks))
    own_grads, near_grads, away = normed_grads(halves, w_query, w_key, w_value, long_local, tensor_axis)
    pieces = [own_grads] + [
        away[r * long_local : (r + 1) * long_local].astype(bf16) for r in range(tensor_axis - 1)
    ]
    if tensor_axis == 4:
        pieces = pieces[:3] + [pieces[3][: long_local // 2], pieces[3][long_local // 2 :]]
    grad_normed = jnp.concatenate([sum_parts(pieces), near_grads], axis=0)
    inputs_wide = inputs.astype(f32)
    scale = lax.rsqrt(jnp.mean(inputs_wide * inputs_wide, axis=-1, keepdims=True) + 1e-06)
    normed = inputs_wide * scale
    lifted = grad_normed * attn_gain.astype(f32)
    inputs_grad = grad_resid + scale * (
        lifted - normed * jnp.mean(lifted * normed, axis=-1, keepdims=True)
    )
    if quick:
        outs, smalls, gains = (), [], []
        for half in range(2):
            made = unpack_blocks(facts, *sums[half], w_query, w_key, w_value, attn_gain, outs, half)
            outs = made[:4]
            gains.append(made[4])
            smalls.append(made[5])
        query_grad, key_grad, value_grad, proj_grad = outs
        attn_gain_grad = (gains[0] + gains[1])[0]
        rel_grad = jnp.concatenate(
            [small[0, : rel.size].reshape(rel.shape) for small, rel in zip(smalls, rel_halves)], axis=1
        )
        small = jnp.concatenate(smalls, axis=1)
    else:
        whole = [jnp.concatenate([one, two], axis=1) for one, two in zip(*halves)]
        key_others = [slice(2 * r * long_local, (2 * r + 1) * long_local) for r in range(tensor_axis - 1)]
        value_others = [slice((2 * r + 1) * long_local, (2 * r + 2) * long_local) for r in range(tensor_axis - 1)]

        def keyed(index, spots):
            short = slice(index * short_len, (index + 1) * short_len)
            rows = slice(index * long_local, (index + 1) * long_local)
            lefts = jnp.concatenate([normed_low, normed_others], axis=0)
            rights = jnp.concatenate([whole[1][rows], whole[3][short]] + [whole[2][spot] for spot in spots], axis=0)
            return mm(lefts, rights, TN)

        rel_grad = jnp.concatenate(rel_halves, axis=1)
        rel_row = jnp.pad(rel_grad.reshape(1, -1), ((0, 0), (0, width - rel_grad.size)))
        small = jnp.concatenate([rel_row, moe_gain_grad, router_grad], axis=0)
        query_grad, key_grad, value_grad, proj_grad, small = lax.psum(
            (
                mm(normed_low, whole[0], TN),
                keyed(0, key_others),
                keyed(1, value_others),
                mm(mixed, branch, TN),
                small,
            ),
            ("expert", "tensor"),
        )
        attn_gain_grad = jnp.sum(
            query_grad * w_query.astype(f32) + key_grad * w_key.astype(f32) + value_grad * w_value.astype(f32),
            axis=1,
        ) / attn_gain.astype(f32)
        rel_grad = small[0, : rel_grad.size].reshape(rel_grad.shape)
    if paired:
        weight_grads = weight_fill(facts, sent, weight_grads)

    outs_back = send_outs()
    slot_places = jnp.arange(local * block, dtype=jnp.int32)
    outputs = resid
    for k in range(top_count):
        chosen = mm((wide_slots[k][:, None] == slot_places).astype(bf16), outs_back)
        outputs = outputs + gates[k][:, None] * chosen
    return (
        outputs.astype(bf16),
        inputs_grad,
        attn_gain_grad,
        query_grad,
        key_grad,
        value_grad,
        proj_grad,
        rel_grad,
        small[1],
        jnp.transpose(small[2 : 2 + experts]),
        jnp.swapaxes(weight_grads[0], 1, 2),
        jnp.swapaxes(weight_grads[1], 1, 2),
        weight_grads[2],
    )


def solution(mesh):
    return jax.shard_map(
        per_device,
        mesh=mesh,
        in_specs=(
            P(("expert", "tensor"), None),
            P(),
            P(),
            P(),
            P(),
            P(),
            P(),
            P(),
            P(),
            P("expert", None, "tensor"),
            P("expert", None, "tensor"),
            P("expert", "tensor", None),
            P(("expert", "tensor"), None),
            P(),
            P(),
            P("expert"),
            P(("expert", "tensor")),
            P(("expert", "tensor"), None),
        ),
        out_specs=(
            P(("expert", "tensor"), None),
            P(("expert", "tensor"), None),
            P(),
            P(),
            P(),
            P(),
            P(),
            P(),
            P(),
            P(),
            P("expert", None, "tensor"),
            P("expert", None, "tensor"),
            P("expert", "tensor", None),
        ),
        check_vma=False,
    )
```

```python
from functools import partial
import math

import jax
import jax.numpy as jnp
from jax import lax
from jax.experimental import pallas as pl
from jax.experimental.pallas import tpu as pltpu
from jax.sharding import PartitionSpec as P

precise = lax.Precision.HIGHEST
bf16 = jnp.bfloat16
f32 = jnp.float32
NT = (((1,), (1,)), ((), ()))
NN = (((1,), (0,)), ((), ()))
TN = (((0,), (0,)), ((), ()))
VMEM_BYTES = 56 * 1024 * 1024


def mm(left, right, dims=NN):
    return lax.dot_general(left, right, dims, preferred_element_type=f32)


def params():
    return pltpu.CompilerParams(
        dimension_semantics=("arbitrary",), vmem_limit_bytes=VMEM_BYTES
    )


def cost(micros):
    return pl.CostEstimate(flops=int(micros * 1.15e9), bytes_accessed=0, transcendentals=0)


def table_hot(table, count):
    return (table[:, None] == jnp.arange(count, dtype=jnp.int32)[None, :]).astype(f32)


def swap(rows, axis, mask):
    count = lax.axis_size(axis)
    return lax.ppermute(rows, axis, [(i, i ^ mask) for i in range(count)])


def after(value, *others):
    return lax.optimization_barrier((value,) + tuple(jax.tree.leaves(others)))[0]


def after_all(values, *others):
    leaves = tuple(jax.tree.leaves(others))
    return list(lax.optimization_barrier(tuple(values) + leaves)[: len(values)])


def ring_gather(rows, move):
    half = rows.shape[0] // 2
    first, second = move(rows, 0), move(rows, 1)
    return [rows, first, second, move(first[:half], 1), move(second[half:], 0)]


def ring_sum_first(parts, move):
    half = parts[3].shape[0]
    left = move(parts[3], 0)
    right = move(parts[4], 1)
    to_second = jnp.concatenate([add_low(parts[2][:half], left), parts[2][half:]], axis=0)
    to_first = jnp.concatenate([parts[1][:half], add_low(parts[1][half:], right)], axis=0)
    return parts[0], to_first, to_second


def ring_sum_second(own, to_first, to_second, move):
    first = move(to_first, 0)
    second = move(to_second, 1)
    return own.astype(f32) + first.astype(f32) + second.astype(f32)


def ring_sum(parts, move):
    return ring_sum_second(*ring_sum_first(parts, move), move)


def in_plane(rows, way):
    return swap(rows, "tensor", 1 + way)


def gather_parts(rows):
    count = lax.axis_size("tensor")
    if count == 4:
        return ring_gather(rows, in_plane)
    return [rows] + [swap(rows, "tensor", r) for r in range(1, count)]


def sum_parts(parts):
    count = lax.axis_size("tensor")
    if count == 4:
        return ring_sum(parts, in_plane)
    arrived = [swap(parts[r], "tensor", r) for r in range(1, count)]
    return sum([part.astype(f32) for part in arrived], parts[0].astype(f32))


def over_experts(rows):
    experts_axis = lax.axis_size("expert")
    blocks = rows.reshape(experts_axis, rows.shape[0] // experts_axis, rows.shape[1])
    return lax.all_to_all(blocks, "expert", 0, 0, tiled=True).reshape(rows.shape)


def add_low(left, right):
    return (left.astype(f32) + right.astype(f32)).astype(bf16)


def sum_cores(near, far):
    return add_low(near, swap(far, "expert", 1))


def plane_parts(rest):
    return [rest[0:4], rest[4:8], rest[8:12], rest[12:14], rest[14:16]]


def sum_depth(rest):
    own = rest[0].astype(f32)
    for m in range(1, 4):
        own = own + swap(rest[m], "expert", 2 * m).astype(f32)
    return own.astype(bf16)


def spread_depth(own):
    return jnp.stack([own] + [swap(own, "expert", 2 * m) for m in range(1, 4)])


def spread_plane(rest):
    return jnp.concatenate(ring_gather(rest, in_plane), axis=0)


def project_kernel(long_local, inputs, gain, w_query, w_key, w_value, normed, query, pair, near, held):
    @pl.when(pl.program_id(0) == 0)
    def _():
        rows = inputs[...].astype(f32)
        scale = lax.rsqrt(jnp.mean(rows * rows, axis=-1, keepdims=True) + 1e-06)
        held[...] = (rows * scale * gain[...].astype(f32)).astype(bf16)
        normed[...] = held[...]

    rows = held[...]
    query[...] = mm(rows, w_query[...]).astype(bf16)
    keys = mm(rows, w_key[...]).astype(bf16)
    values = mm(rows, w_value[...]).astype(bf16)
    pair[:long_local] = keys[:long_local]
    pair[long_local:] = values[:long_local]
    short = keys.shape[0] - long_local
    near[:short] = keys[long_local:]
    near[short:] = values[long_local:]


def project(inputs, gain, w_query, w_key, w_value, long_local):
    rows, width = inputs.shape
    short = rows - long_local
    step = 256
    whole = lambda count: pl.BlockSpec((count, width), lambda i: (0, 0))
    cut = lambda count: pl.BlockSpec((count, step), lambda i: (0, i))
    return pl.pallas_call(
        partial(project_kernel, long_local),
        grid=(width // step,),
        in_specs=[whole(rows), whole(1), cut(width), cut(width), cut(width)],
        out_specs=[whole(rows), cut(rows), cut(2 * long_local), cut(2 * short)],
        out_shape=[
            jax.ShapeDtypeStruct((rows, width), bf16),
            jax.ShapeDtypeStruct((rows, width), bf16),
            jax.ShapeDtypeStruct((2 * long_local, width), bf16),
            jax.ShapeDtypeStruct((2 * short, width), bf16),
        ],
        scratch_shapes=[pltpu.VMEM((rows, width), bf16)],
        compiler_params=params(),
        cost_estimate=cost(6.9),
        name="project",
    )(inputs, gain.reshape(1, width), w_query, w_key, w_value)


def project_others_kernel(local, gain, w_key, w_value, *refs):
    sources, (normed, pairs, held) = refs[:-3], refs[-3:]

    @pl.when(pl.program_id(0) == 0)
    def _():
        rows = jnp.concatenate([source[...] for source in sources], axis=0).astype(f32)
        scale = lax.rsqrt(jnp.mean(rows * rows, axis=-1, keepdims=True) + 1e-06)
        held[...] = (rows * scale * gain[...].astype(f32)).astype(bf16)
        normed[...] = held[...]

    keys = mm(held[...], w_key[...]).astype(bf16)
    values = mm(held[...], w_value[...]).astype(bf16)
    for r in range(keys.shape[0] // local):
        pairs[2 * r * local : (2 * r + 1) * local] = keys[r * local : (r + 1) * local]
        pairs[(2 * r + 1) * local : (2 * r + 2) * local] = values[r * local : (r + 1) * local]


def project_others(sources, gain, w_key, w_value, local):
    rows = sum(source.shape[0] for source in sources)
    width = gain.shape[0]
    step = 256
    whole = lambda count: pl.BlockSpec((count, width), lambda i: (0, 0))
    cut = lambda count: pl.BlockSpec((count, step), lambda i: (0, i))
    return pl.pallas_call(
        partial(project_others_kernel, local),
        grid=(width // step,),
        in_specs=[whole(1), cut(width), cut(width)] + [whole(source.shape[0]) for source in sources],
        out_specs=[whole(rows), cut(2 * rows)],
        out_shape=[
            jax.ShapeDtypeStruct((rows, width), bf16),
            jax.ShapeDtypeStruct((2 * rows, width), bf16),
        ],
        scratch_shapes=[pltpu.VMEM((rows, width), bf16)],
        compiler_params=params(),
        cost_estimate=cost(7.7),
        name="project_others",
    )(gain.reshape(1, width), w_key, w_value, *sources)


def key_value_views(pair, others, count, rows):
    views = [(pair, slice(0, rows), pair, slice(rows, 2 * rows))]
    for r in range(count - 1):
        at = 2 * r * rows
        views.append((others, slice(at, at + rows), others, slice(at + rows, at + 2 * rows)))
    return views


def own_lanes(head, dim, shape, axis):
    place = lax.broadcasted_iota(jnp.int32, shape, axis)
    return (place >= head * dim) & (place < (head + 1) * dim)


def forward_kernel(
    count,
    rows,
    dim,
    facts,
    query,
    pair,
    others,
    near,
    far_bias,
    near_bias,
    mixed,
    far_attend,
    near_attend,
    window,
    scores,
):
    place, far_len, near_len = facts[0], facts[1], facts[2]
    scale = 1.0 / math.sqrt(dim)
    views = key_value_views(pair, others, count, rows)
    short = near.shape[0] // 2
    band, reach = window.shape[1:]
    low = (query[...].astype(f32) * scale).astype(bf16)
    starts = [(place ^ r) * rows for r in range(count)]
    spot = lax.broadcasted_iota(jnp.int32, (1, rows), 1)
    kept = [start + spot < far_len for start in starts]
    near_kept = lax.broadcasted_iota(jnp.int32, (1, short), 1) < near_len
    mine = [jnp.where(own_lanes(head, dim, low.shape, 1), low, jnp.zeros_like(low)) for head in range(2)]
    far_mine = jnp.concatenate([part[:rows] for part in mine], axis=0)
    near_parts = mm(jnp.concatenate([part[rows:] for part in mine], axis=0), near[:short], NT)
    near_parts = [near_parts[:short], near_parts[short:]]
    for r in range(count):
        part = mm(far_mine, views[r][0][views[r][1]], NT)
        for head in range(2):
            scores[head, :, r * rows : (r + 1) * rows] = part[head * rows : (head + 1) * rows]
    for head in range(2):
        table = jnp.broadcast_to(far_bias[0, head : head + 1, :], (band, reach))
        window[head] = pltpu.roll(table, reach - (band - 1), 1, stride=1, stride_axis=0)
    for head in range(2):
        table = jnp.broadcast_to(near_bias[0, head : head + 1, :], (short, 2 * short))
        bias = pltpu.roll(table, short + 1, 1, stride=1, stride_axis=0)[:, :short]
        part = jnp.where(near_kept, near_parts[head] + bias, -1e30)
        part = jnp.exp(part - jnp.max(part, axis=-1, keepdims=True))
        near_attend[head] = (part * (1.0 / jnp.sum(part, axis=-1, keepdims=True))).astype(bf16)
        for at in range(0, rows, 32):
            shift = band * (rows // band - 1 - at // band)
            lines = slice(at % band, at % band + 32)
            parts = []
            for r in range(count):
                begin = pl.multiple_of(starts[r] + shift, 128)
                part = scores[head, at : at + 32, r * rows : (r + 1) * rows]
                part = part + window[head, lines, pl.ds(begin, rows)]
                parts.append(jnp.where(kept[r], part, -1e30))
            highest = parts[0]
            for part in parts[1:]:
                highest = jnp.maximum(highest, part)
            highest = jnp.max(highest, axis=-1, keepdims=True)
            parts = [jnp.exp(part - highest) for part in parts]
            whole = parts[0]
            for part in parts[1:]:
                whole = whole + part
            inverse = 1.0 / jnp.sum(whole, axis=-1, keepdims=True)
            for r in range(count):
                far_attend[head, at : at + 32, r * rows : (r + 1) * rows] = (parts[r] * inverse).astype(bf16)
    out = jnp.zeros((2 * rows, 2 * dim), f32)
    for r in range(count):
        attend = far_attend[:, :, r * rows : (r + 1) * rows].reshape(2 * rows, rows)
        out = out + mm(attend, views[r][2][views[r][3]])
    near_out = mm(near_attend[...].reshape(2 * short, short), near[short:])
    second = own_lanes(1, dim, (rows, 2 * dim), 1)
    mixed[:rows] = jnp.where(second, out[rows:], out[:rows]).astype(bf16)
    second = own_lanes(1, dim, (short, 2 * dim), 1)
    mixed[rows:] = jnp.where(second, near_out[short:], near_out[:short]).astype(bf16)


def attention_specs(count, rows, short, reach, tokens):
    cut = lambda size: pl.BlockSpec((size, 128), lambda i, *_: (0, i))
    parts = [cut(2 * rows), cut(2 * (count - 1) * rows)]
    table = lambda size: pl.BlockSpec((1, 2, size), lambda i, *_: (i, 0, 0))
    weights = lambda size, span: pl.BlockSpec((2, size, span), lambda i, *_: (i, 0, 0))
    return (
        cut(tokens),
        parts,
        cut(2 * short),
        [table(reach), table(2 * short)],
        [weights(rows, count * rows), weights(short, short)],
    )


def attend_forward(facts, query, parts, near, far_bias, near_bias, count, rows, dim):
    tokens, width = query.shape
    heads = width // dim
    short = near.shape[0] // 2
    reach = far_bias.shape[-1]
    cut, part_specs, near_spec, tables, weights = attention_specs(count, rows, short, reach, tokens)
    return pl.pallas_call(
        partial(forward_kernel, count, rows, dim),
        grid_spec=pltpu.PrefetchScalarGridSpec(
            num_scalar_prefetch=1,
            grid=(heads // 2,),
            in_specs=[cut] + part_specs + [near_spec] + tables,
            out_specs=[cut] + weights,
            scratch_shapes=[pltpu.VMEM((2, 128, reach), f32), pltpu.VMEM((2, rows, count * rows), f32)],
        ),
        out_shape=[
            jax.ShapeDtypeStruct((tokens, width), bf16),
            jax.ShapeDtypeStruct((heads, rows, count * rows), bf16),
            jax.ShapeDtypeStruct((heads, short, short), bf16),
        ],
        compiler_params=params(),
        cost_estimate=cost(17),
        name="attend_forward",
    )(facts, query, *parts, near, far_bias, near_bias)


def backward_kernel(
    count,
    rows,
    dim,
    facts,
    query,
    grad,
    pair,
    others,
    near,
    far_attend,
    near_attend,
    far_hot,
    near_hot,
    grad_query,
    grad_pair,
    grad_others,
    grad_near,
    bias_grad,
    window,
    near_window,
    products,
    scores,
    near_scores,
):
    place = facts[0]
    scale = 1.0 / math.sqrt(dim)
    views = key_value_views(pair, others, count, rows)
    grad_views = key_value_views(grad_pair, grad_others, count, rows)
    short = near.shape[0] // 2
    band = window.shape[1]
    starts = [(place ^ r) * rows for r in range(count)]

    @pl.when(pl.program_id(0) == 0)
    def _():
        near_window[...] = jnp.zeros_like(near_window)

    def reversal(size):
        up = lax.broadcasted_iota(jnp.int32, (size, size), 0)
        across = lax.broadcasted_iota(jnp.int32, (size, size), 1)
        return (up + across == size - 1).astype(bf16)

    far_turn = reversal(band)
    near_turn = far_turn if short == band else reversal(short)
    low, grad_low = query[...], grad[...]
    turned = jnp.transpose(low.astype(f32) * scale, (1, 0)).astype(bf16)
    grad_turned = jnp.transpose(grad_low.astype(f32), (1, 0)).astype(bf16)
    mine, grad_mine, grad_heads = [], [], []
    for head in range(2):
        lines = own_lanes(head, dim, turned.shape, 0)
        mine.append(jnp.where(lines, turned, jnp.zeros_like(turned)))
        grad_mine.append(jnp.where(lines, grad_turned, jnp.zeros_like(turned)))
        lanes = own_lanes(head, dim, low.shape, 1)
        grad_heads.append(jnp.where(lanes, grad_low, jnp.zeros_like(grad_low)))
    far_grads = jnp.concatenate([part[:rows] for part in grad_heads], axis=0)
    near_parts = mm(jnp.concatenate([part[rows:] for part in grad_heads], axis=0), near[short:], NT)
    for r in range(count):
        part = mm(far_grads, views[r][2][views[r][3]], NT)
        for head in range(2):
            products[head, :, r * rows : (r + 1) * rows] = part[head * rows : (head + 1) * rows]
    window[...] = jnp.zeros_like(window)
    for head in range(2):
        wide = near_attend[head].astype(f32)
        part = near_parts[head * short : (head + 1) * short]
        part = wide * (part - jnp.sum(wide * part, axis=-1, keepdims=True))
        near_scores[head] = part.astype(bf16)
        for at in range(0, rows, 32):
            attend = far_attend[head, at : at + 32].astype(f32)
            part = products[head, at : at + 32]
            inner = jnp.sum(attend * part, axis=-1, keepdims=True)
            scores[head, at : at + 32] = (attend * (part - inner)).astype(bf16)
    out = jnp.zeros((2 * rows, 2 * dim), f32)
    for r in range(count):
        part = scores[:, :, r * rows : (r + 1) * rows].reshape(2 * rows, rows)
        out = out + mm(part, views[r][0][views[r][1]])
        for head in range(2):
            for h in range(rows // band):
                begin = pl.multiple_of(starts[r] + band * (rows // band - 1 - h), 128)
                lines = slice(head * rows + h * band, head * rows + (h + 1) * band)
                window[head, :, pl.ds(begin, rows)] += mm(far_turn, part[lines])
    near_out = mm(near_scores[...].reshape(2 * short, short), near[:short])
    second = own_lanes(1, dim, (rows, 2 * dim), 1)
    grad_query[:rows] = (jnp.where(second, out[rows:], out[:rows]) * scale).astype(bf16)
    second = own_lanes(1, dim, (short, 2 * dim), 1)
    grad_query[rows:] = (jnp.where(second, near_out[short:], near_out[:short]) * scale).astype(bf16)
    def by_bucket(lines, hot):
        row = lax.broadcasted_iota(jnp.int32, (16, lines.shape[1]), 0)
        high = lines.astype(bf16).astype(f32)
        rest = lines - high
        middle = rest.astype(bf16).astype(f32)
        stack = jnp.where(row == 0, high, jnp.where(row == 1, middle, jnp.where(row == 2, rest - middle, 0.0)))
        return jnp.sum(mm(stack.astype(bf16), hot[...]), axis=0, keepdims=True)

    for head in range(2):
        rolled = pltpu.roll(window[head], 0, 1, stride=1, stride_axis=0)
        sums = by_bucket(jnp.sum(rolled, axis=0, keepdims=True), far_hot)
        near_window[head, :, :short] = mm(near_turn, near_scores[head])
        rolled = pltpu.roll(near_window[head], 0, 1, stride=1, stride_axis=0)
        sums = sums + by_bucket(jnp.sum(rolled, axis=0, keepdims=True), near_hot)
        bias_grad[0, head : head + 1, :] = sums
    for r in range(count):
        lanes = slice(r * rows, (r + 1) * rows)
        keys = mm(mine[0][:, :rows], scores[0, :, lanes]) + mm(mine[1][:, :rows], scores[1, :, lanes])
        values = mm(grad_mine[0][:, :rows], far_attend[0, :, lanes]) + mm(
            grad_mine[1][:, :rows], far_attend[1, :, lanes]
        )
        view = grad_views[r]
        view[0][view[1]] = jnp.transpose(keys, (1, 0)).astype(bf16)
        view[2][view[3]] = jnp.transpose(values, (1, 0)).astype(bf16)
    keys = mm(mine[0][:, rows:], near_scores[0]) + mm(mine[1][:, rows:], near_scores[1])
    values = mm(grad_mine[0][:, rows:], near_attend[0]) + mm(grad_mine[1][:, rows:], near_attend[1])
    grad_near[:short] = jnp.transpose(keys, (1, 0)).astype(bf16)
    grad_near[short:] = jnp.transpose(values, (1, 0)).astype(bf16)


def attend_backward(facts, query, grad, parts, near, weights, hots, count, rows, dim):
    tokens, width = query.shape
    pairs = width // dim // 2
    short = near.shape[0] // 2
    reach, buckets = hots[0].shape
    cut, part_specs, near_spec, _, weight_specs = attention_specs(count, rows, short, reach, tokens)
    return pl.pallas_call(
        partial(backward_kernel, count, rows, dim),
        grid_spec=pltpu.PrefetchScalarGridSpec(
            num_scalar_prefetch=1,
            grid=(pairs,),
            in_specs=[cut, cut]
            + part_specs
            + [near_spec]
            + weight_specs
            + [pl.BlockSpec(hot.shape, lambda i, *_: (0, 0)) for hot in hots],
            out_specs=[cut]
            + part_specs
            + [near_spec, pl.BlockSpec((1, 2, buckets), lambda i, *_: (i, 0, 0))],
            scratch_shapes=[
                pltpu.VMEM((2, 128, reach), f32),
                pltpu.VMEM((2, short, 2 * short), f32),
                pltpu.VMEM((2, rows, count * rows), f32),
                pltpu.VMEM((2, rows, count * rows), bf16),
                pltpu.VMEM((2, short, short), bf16),
            ],
        ),
        out_shape=[
            jax.ShapeDtypeStruct((size, width), bf16)
            for size in (tokens, 2 * rows, 2 * (count - 1) * rows, 2 * short)
        ]
        + [jax.ShapeDtypeStruct((pairs, 2, buckets), f32)],
        compiler_params=params(),
        cost_estimate=cost(25),
        name="attend_backward",
    )(facts, query, grad, *parts, near, *weights, *hots)


def normed_grads_kernel(local, count, query, pair, others, near, w_query, w_key, w_value, *outs):
    own, own_short, away = outs
    short = near.shape[0] // 2

    @pl.when(pl.program_id(0) == 0)
    def _():
        for out in outs:
            out[...] = jnp.zeros_like(out)

    full = mm(query[...], w_query[...], NT)
    own[...] += full[:local] + mm(pair[:local], w_key[...], NT) + mm(pair[local:], w_value[...], NT)
    own_short[...] += full[local:] + mm(near[:short], w_key[...], NT) + mm(near[short:], w_value[...], NT)
    for r in range(count - 1):
        at = 2 * r * local
        away[r * local : (r + 1) * local] += mm(others[at : at + local], w_key[...], NT) + mm(
            others[at + local : at + 2 * local], w_value[...], NT
        )


def normed_grads(grads, w_query, w_key, w_value, local, count):
    width = w_query.shape[0]
    short = grads[3].shape[0] // 2
    cut = lambda size: pl.BlockSpec((size, width // 2), lambda i: (0, i))
    sizes = (local, short, (count - 1) * local)
    return pl.pallas_call(
        partial(normed_grads_kernel, local, count),
        grid=(2,),
        in_specs=[cut(array.shape[0]) for array in grads] + [cut(width)] * 3,
        out_specs=[pl.BlockSpec((size, width), lambda i: (0, 0)) for size in sizes],
        out_shape=[jax.ShapeDtypeStruct((size, width), f32) for size in sizes],
        compiler_params=params(),
        cost_estimate=cost(13),
        name="normed_grads",
    )(*grads, w_query, w_key, w_value)


def expert_kernel(chunks, capacity, padded, lanes_used, facts, rows_in, grads_in, *refs):
    sources, rest = refs[: 3 * chunks], refs[3 * chunks :]
    middles, (out_ref, grad_ref) = rest[: 3 * chunks], rest[3 * chunks : 3 * chunks + 2]
    held, sems = rest[3 * chunks + 2 : 6 * chunks + 2], rest[6 * chunks + 2]
    rows = rows_in.shape[0]
    groups = rows // padded
    first = pl.program_id(0) == 0

    def copy(i):
        index = facts[4] if i < 3 else i % 3
        return pltpu.make_async_copy(sources[i].at[index], held[i], sems.at[i])

    @pl.when(first)
    def _():
        for i in range(3 * chunks):
            copy(i).start()
        for i in range(3 * chunks):
            copy(i).wait()

    slots = rows_in[...]
    grads = grads_in[...]
    spare = 16 - (padded - capacity)
    lanes = lax.broadcasted_iota(jnp.int32, (padded, 128), 1)
    match = lax.broadcasted_iota(jnp.int32, (padded, 128), 0) == lanes
    columns = []
    for g in range(groups):
        tail = rows_in[pl.ds((g + 1) * padded - 16, 16), :128].astype(f32)
        line = tail[spare : spare + 1] + tail[spare + 1 : spare + 2]
        columns.append(jnp.sum(jnp.where(match, line, 0.0), axis=-1, keepdims=True))
    gate_column = jnp.concatenate(columns, axis=0)

    lows = []
    slope = math.sqrt(2.0 / math.pi)
    for c in range(chunks):
        gate_pre = mm(slots, held[3 * c][...], NT)
        up_pre = mm(slots, held[3 * c + 1][...], NT)
        grad_hidden = mm(grads, held[3 * c + 2][...], NT) * gate_column
        square = gate_pre * gate_pre
        curve = jnp.tanh(slope * gate_pre * (1.0 + 0.044715 * square))
        side = 0.5 * (1.0 + curve)
        bent = gate_pre * side
        hidden = bent * up_pre
        bent_slope = side + 0.5 * slope * gate_pre * (1.0 - curve * curve) * (
            1.0 + 3.0 * 0.044715 * square
        )
        gate_low = (grad_hidden * up_pre * bent_slope).astype(bf16)
        up_low = (grad_hidden * bent).astype(bf16)
        middles[3 * c][...] = (hidden * gate_column).astype(bf16)
        middles[3 * c + 1][...] = gate_low
        middles[3 * c + 2][...] = up_low
        lows.append((gate_low, up_low, hidden.astype(bf16)))
    left = [jnp.concatenate([low[k] for low in lows], axis=1) for k in range(3)]
    right = [
        jnp.concatenate([held[3 * c + k][...] for c in range(chunks)], axis=0) for k in range(3)
    ]
    out = mm(left[2], right[2])
    grad_out = mm(left[0], right[0]) + mm(left[1], right[1])
    out_ref[...] = out.astype(bf16)
    grad_ref[...] = grad_out.astype(bf16)

    grad_gate = jnp.sum(out * grads.astype(f32), axis=-1, keepdims=True)
    lanes = lax.broadcasted_iota(jnp.int32, (padded, lanes_used), 1)
    up = lax.broadcasted_iota(jnp.int32, (padded, lanes_used), 0)
    match = up + facts[5] * padded == lanes
    row = lax.broadcasted_iota(jnp.int32, (16, lanes_used), 0)
    for g in range(groups):
        values = jnp.where(match, grad_gate[g * padded : (g + 1) * padded], 0.0)
        line = jnp.sum(values, axis=0, keepdims=True)
        high = line.astype(bf16).astype(f32)
        tail = grad_out[(g + 1) * padded - 16 : (g + 1) * padded, :lanes_used]
        tail = jnp.where(row == spare, high, jnp.where(row == spare + 1, line - high, tail))
        grad_ref[pl.ds((g + 1) * padded - 16, 16), :lanes_used] = tail.astype(bf16)


def expert_pass(facts, slots, grads, own, other, capacity, padded, lanes_used):
    rows, width = slots.shape
    units = own[0].shape[1]
    chunks = 1 if other is None else 2
    sources = list(own) + ([] if other is None else [other] * 3)
    tile = rows
    cut = lambda size: pl.BlockSpec((tile, size), lambda i, f: (i, 0))
    outs = pl.pallas_call(
        partial(expert_kernel, chunks, capacity, padded, lanes_used),
        grid_spec=pltpu.PrefetchScalarGridSpec(
            num_scalar_prefetch=1,
            grid=(rows // tile,),
            in_specs=[cut(width)] * 2 + [pl.BlockSpec(memory_space=pl.ANY)] * (3 * chunks),
            out_specs=[cut(units)] * (3 * chunks) + [cut(width)] * 2,
            scratch_shapes=[pltpu.VMEM((units, width), bf16)] * (3 * chunks)
            + [pltpu.SemaphoreType.DMA((3 * chunks,))],
        ),
        out_shape=[jax.ShapeDtypeStruct((rows, units), bf16)] * (3 * chunks)
        + [jax.ShapeDtypeStruct((rows, width), bf16)] * 2,
        compiler_params=params(),
        cost_estimate=cost(18),
        name="expert_pass",
    )(facts, slots, grads, *sources)
    middles = [outs[3 * c : 3 * c + 3] for c in range(chunks)]
    return middles, outs[3 * chunks], outs[3 * chunks + 1]


def weight_body(count, packed, extra, facts, *refs):
    kinds = [refs[k * count : (k + 1) * count] for k in range(5)]
    outs = refs[5 * count + extra :]
    targets = outs[1:4] if packed else outs[:3]
    held, sems = refs[-6:-1], refs[-1]
    step = pl.program_id(0)
    slot = step % 2

    def fetch(index, side):
        for r in range(count):

            @pl.when(index == r)
            def _():
                for k in range(5):
                    pltpu.make_async_copy(kinds[k][r], held[k].at[side], sems.at[side, k]).start()

    @pl.when(step == 0)
    def _():
        fetch(step, slot)

    @pl.when(step + 1 < count)
    def _():
        fetch(step + 1, 1 - slot)

    for k in range(5):
        pltpu.make_async_copy(kinds[k][0], held[k].at[slot], sems.at[slot, k]).wait()

    @pl.when(step == 0)
    def _():
        for target in targets:
            target[...] = jnp.zeros_like(target)

    rows, grads = held[0][slot], held[1][slot]
    lefts = ((held[3], rows), (held[4], rows), (held[2], grads))
    for target, (left, right) in zip(targets, lefts):
        target[0] += mm(left[slot], right, TN)

    if packed:

        @pl.when(step == count - 1)
        def _():
            for i in range(3):
                outs[0][i] = targets[i][0].astype(bf16)


def weight_pass(facts, slots, grads, middles, before, local, packed):
    count = len(slots)
    rows, width = slots[0].shape
    units = middles[0][0].shape[1]
    anywhere = pl.BlockSpec(memory_space=pl.ANY)
    if packed:
        out_specs = [pl.BlockSpec((3, units, width), lambda i, f: (0, 0, 0))]
        out_shape = [jax.ShapeDtypeStruct((3, units, width), bf16)]
        totals = [pltpu.VMEM((1, units, width), f32)] * 3
    else:
        out_specs = [pl.BlockSpec((1, units, width), lambda i, f: (f[4], 0, 0))] * 3
        out_shape = [jax.ShapeDtypeStruct((local, units, width), f32)] * 3
        totals = []
    kinds = [list(slots), list(grads)] + [[middle[k] for middle in middles] for k in range(3)]
    body = partial(weight_body, count, packed, len(before))
    return pl.pallas_call(
        body,
        grid_spec=pltpu.PrefetchScalarGridSpec(
            num_scalar_prefetch=1,
            grid=(count,),
            in_specs=[anywhere] * (5 * count + len(before)),
            out_specs=out_specs,
            scratch_shapes=totals
            + [pltpu.VMEM((2, rows, width), bf16)] * 2
            + [pltpu.VMEM((2, rows, units), bf16)] * 3
            + [pltpu.SemaphoreType.DMA((2, 5))],
        ),
        out_shape=out_shape,
        input_output_aliases={1 + 5 * count + i: i for i in range(len(before))},
        compiler_params=params(),
        cost_estimate=cost(16),
        name="weight_pass",
    )(facts, *[array for kind in kinds for array in kind], *before)


def fill_kernel(facts, source, *refs):
    for i in range(3):
        refs[-3 + i][0] = source[i].astype(f32)


def weight_fill(facts, source, before):
    _, units, width = source.shape
    tile = units // 4
    anywhere = pl.BlockSpec(memory_space=pl.ANY)
    return pl.pallas_call(
        fill_kernel,
        grid_spec=pltpu.PrefetchScalarGridSpec(
            num_scalar_prefetch=1,
            grid=(4,),
            in_specs=[pl.BlockSpec((3, tile, width), lambda i, f: (0, i, 0))] + [anywhere] * 3,
            out_specs=[pl.BlockSpec((1, tile, width), lambda i, f: (f[6], i, 0))] * 3,
        ),
        out_shape=[jax.ShapeDtypeStruct(array.shape, f32) for array in before],
        input_output_aliases={2 + i: i for i in range(3)},
        compiler_params=params(),
        cost_estimate=cost(6.5),
        name="weight_fill",
    )(facts, source, *before)


def place_kernel(capacity, padded, block, local, turns, routes, rows, slots_out, wide_out, rows_out):
    experts_axis = block // padded
    tokens = rows.shape[0]
    experts = experts_axis * local
    number = lax.broadcasted_iota(jnp.int32, (experts, tokens), 0)
    picks = [number == routes[k : k + 1] for k in range(routes.shape[0])]
    named = picks[0]
    for pick in picks[1:]:
        named = named | pick
    earlier = lax.broadcasted_iota(jnp.int32, (tokens, tokens), 0) < lax.broadcasted_iota(
        jnp.int32, (tokens, tokens), 1
    )
    before = mm(named.astype(bf16), earlier.astype(bf16))
    places = []
    for k, pick in enumerate(picks):
        route = routes[k : k + 1]
        position = jnp.sum(jnp.where(pick, before, 0.0), axis=0, keepdims=True).astype(jnp.int32)
        owner = route // local
        turn = jnp.where(owner % 2 == 0, turns[:, 0:1], turns[:, 1:2])
        which = (route % local) ^ turn
        slot = which * block + owner * padded + position
        slots_out[k : k + 1] = jnp.where(position < capacity, slot, -1)
        slot = (owner * local + which) * padded + position
        places.append(jnp.where(position < capacity, slot, -1))
        wide_out[k : k + 1] = places[k]
    spots = lax.broadcasted_iota(jnp.int32, (local * block, tokens), 0)
    hot = spots == places[0]
    for slot in places[1:]:
        hot = hot | (spots == slot)
    rows_out[...] = mm(hot.astype(bf16), rows[...]).astype(bf16)


def place_rows(turns, routes, rows, capacity, padded, block, local):
    tops, tokens = routes.shape
    width = rows.shape[1]
    return pl.pallas_call(
        partial(place_kernel, capacity, padded, block, local),
        out_shape=[
            jax.ShapeDtypeStruct((tops, tokens), jnp.int32),
            jax.ShapeDtypeStruct((tops, tokens), jnp.int32),
            jax.ShapeDtypeStruct((local * block, width), bf16),
        ],
        compiler_params=pltpu.CompilerParams(vmem_limit_bytes=VMEM_BYTES),
        cost_estimate=cost(3.9),
        name="place_rows",
    )(turns, routes, rows)


def route_kernel(
    capacity, padded, mixed, w_proj, inputs, gain, router, routes, slots, resid, moe, probs, gates, *outs
):
    local, block = len(outs), outs[0].shape[0]
    tokens = inputs.shape[0]
    sums = inputs[...].astype(f32) + mm(mixed[...], w_proj[...])
    resid[...] = sums
    scale = lax.rsqrt(jnp.mean(sums * sums, axis=-1, keepdims=True) + 1e-06)
    low = (sums * scale * gain[...].astype(f32)).astype(bf16)
    moe[...] = low
    logits = mm(router[...], low, NT)
    grown = jnp.exp(logits - jnp.max(logits, axis=0, keepdims=True))
    share = grown / jnp.sum(grown, axis=0, keepdims=True)
    probs[...] = share
    number = lax.broadcasted_iota(jnp.int32, share.shape, 0)
    spots = lax.broadcasted_iota(jnp.int32, (local * block, tokens), 0)
    row = lax.broadcasted_iota(jnp.int32, (16, tokens), 0)
    hot = None
    lines = jnp.zeros((16, local * block), f32)
    for k in range(routes.shape[0]):
        gate = jnp.sum(jnp.where(number == routes[k : k + 1], share, 0.0), axis=0, keepdims=True)
        gates[k : k + 1] = gate
        high = gate.astype(bf16).astype(f32)
        both = jnp.where(row == 0, high, jnp.where(row == 1, gate - high, 0.0)).astype(bf16)
        mine = (spots == slots[k : k + 1]).astype(bf16)
        lines = lines + mm(both, mine, NT)
        hot = mine if hot is None else hot + mine
    filled = mm(hot, low).astype(bf16)
    spare = 16 - (padded - capacity)
    row = lax.broadcasted_iota(jnp.int32, (16, padded), 0)
    for j in range(local):
        outs[j][...] = filled[j * block : (j + 1) * block]
        for g in range(block // padded):
            at = j * block + g * padded
            tail = filled[at + padded - 16 : at + padded, :padded].astype(f32)
            line = lines[:, at : at + padded]
            tail = jnp.where(row == spare, line[0:1], jnp.where(row == spare + 1, line[1:2], tail))
            outs[j][pl.ds((g + 1) * padded - 16, 16), :padded] = tail.astype(bf16)


def route_rows(mixed, w_proj, inputs, gain, router, routes, slots, capacity, padded, block, local):
    tokens, width = inputs.shape
    tops = routes.shape[0]
    return pl.pallas_call(
        partial(route_kernel, capacity, padded),
        out_shape=[
            jax.ShapeDtypeStruct((tokens, width), f32),
            jax.ShapeDtypeStruct((tokens, width), bf16),
            jax.ShapeDtypeStruct((router.shape[0], tokens), f32),
            jax.ShapeDtypeStruct((tops, tokens), f32),
        ]
        + [jax.ShapeDtypeStruct((block, width), bf16)] * local,
        compiler_params=pltpu.CompilerParams(vmem_limit_bytes=VMEM_BYTES),
        cost_estimate=cost(6.4),
        name="route_rows",
    )(mixed, w_proj, inputs, gain.reshape(1, width), router, routes, slots)


def merge_kernel(
    capacity, padded, count, cotangent, resid, probs, moe, router, gain, w_proj, routes, slots, columns, *refs
):
    local = len(refs) - 5
    grads = refs[:local]
    grad_resid, grad_mixed, gain_grad, router_grad, branch_out = refs[local:]
    block = grads[0].shape[0]
    tokens = cotangent.shape[0]
    tops = routes.shape[0]
    spare = 16 - (padded - capacity)
    pieces = []
    for j in range(local):
        for g in range(block // padded):
            tail = grads[j][pl.ds((g + 1) * padded - 16, 16), : count * padded].astype(f32)
            line = tail[spare : spare + 1] + tail[spare + 1 : spare + 2]
            folded = line[:, :padded]
            for r in range(1, count):
                folded = folded + line[:, r * padded : (r + 1) * padded]
            pieces.append(folded)
    line = jnp.concatenate(pieces, axis=1)
    row = lax.broadcasted_iota(jnp.int32, (16, line.shape[1]), 0)
    high = line.astype(bf16).astype(f32)
    rest = line - high
    middle = rest.astype(bf16).astype(f32)
    stack = jnp.where(row == 0, high, jnp.where(row == 1, middle, jnp.where(row == 2, rest - middle, 0.0)))
    stack = stack.astype(bf16)
    share = probs[...]
    number = lax.broadcasted_iota(jnp.int32, share.shape, 0)
    spots = lax.broadcasted_iota(jnp.int32, (local * block, tokens), 0)
    grad_probs = jnp.zeros_like(share)
    for k in range(tops):
        picked = jnp.sum(mm(stack, (spots == slots[k : k + 1]).astype(bf16)), axis=0, keepdims=True)
        grad_probs = grad_probs + jnp.where(number == routes[k : k + 1], picked, 0.0)
    grad_logits = share * (grad_probs - jnp.sum(share * grad_probs, axis=0, keepdims=True))
    grad_logits = grad_logits.astype(bf16)
    router_grad[...] = mm(grad_logits, moe[...])
    grad_moe = mm(grad_logits, router[...], TN)
    spots = lax.broadcasted_iota(jnp.int32, (tokens, block), 1)
    for j in range(local):
        hot = None
        for k in range(tops):
            mine = spots + j * block == columns[:, k : k + 1]
            hot = mine if hot is None else hot | mine
        grad_moe = grad_moe + mm(hot.astype(bf16), grads[j][...])
    rows = resid[...]
    scale = lax.rsqrt(jnp.mean(rows * rows, axis=-1, keepdims=True) + 1e-06)
    normed = rows * scale
    gain_grad[...] = jnp.sum(grad_moe * normed, axis=0, keepdims=True)
    lifted = grad_moe * gain[...].astype(f32)
    spread = jnp.mean(lifted * normed, axis=-1, keepdims=True)
    back = cotangent[...].astype(f32) + scale * (lifted - normed * spread)
    grad_resid[...] = back
    branch = back.astype(bf16)
    grad_mixed[...] = mm(branch, w_proj[...], NT).astype(bf16)
    branch_out[...] = branch


def merge_rows(
    cotangent, resid, probs, moe, router, gain, w_proj, routes, slots, grads, capacity, padded, count
):
    tokens, width = cotangent.shape
    return pl.pallas_call(
        partial(merge_kernel, capacity, padded, count),
        out_shape=[
            jax.ShapeDtypeStruct((tokens, width), f32),
            jax.ShapeDtypeStruct((tokens, width), bf16),
            jax.ShapeDtypeStruct((1, width), f32),
            jax.ShapeDtypeStruct((router.shape[0], width), f32),
            jax.ShapeDtypeStruct((tokens, width), bf16),
        ],
        compiler_params=pltpu.CompilerParams(vmem_limit_bytes=VMEM_BYTES),
        cost_estimate=cost(7.4),
        name="merge_rows",
    )(
        cotangent, resid, probs, moe, router, gain.reshape(1, width), w_proj, routes, slots,
        jnp.transpose(slots), *grads,
    )


def blocks_kernel(
    local,
    facts,
    normed,
    normed_others,
    mixed,
    grad_query,
    grad_pair,
    grad_others,
    grad_near,
    branch,
    bias_grad,
    gain_grad,
    router_grad,
    near,
    far,
    near_right,
    far_right,
):
    step = pl.program_id(0)
    number = facts[3]
    group = step ^ (number // 8)
    share = (near.shape[1] - 8) // 4
    short = grad_near.shape[0] // 2
    own, own_short = normed[:local], normed[local:]

    def keyed(which):
        part = mm(own, grad_pair[which * local : (which + 1) * local], TN)
        part = part + mm(own_short, grad_near[which * short : (which + 1) * short], TN)
        for r in range(normed_others.shape[0] // local):
            at = (2 * r + which) * local
            part = part + mm(normed_others[r * local : (r + 1) * local], grad_others[at : at + local], TN)
        return part

    made = [mm(normed[...], grad_query[...], TN), keyed(0), keyed(1), mm(mixed[...], branch[...], TN)]
    made = [part.astype(bf16) for part in made]
    pairs, _, buckets = bias_grad.shape
    line = [bias_grad[p, h : h + 1, :] for p in range(pairs) for h in range(2)]
    line.append(jnp.zeros((1, 2 * near.shape[2] - 2 * pairs * buckets), f32))
    tail = jnp.zeros((24 - 2 - router_grad.shape[0], 2 * near.shape[2]), f32)
    small = jnp.concatenate(
        [jnp.concatenate(line, axis=1), gain_grad[...], router_grad[...], tail], axis=0
    )
    for s in range(8):
        spot = s ^ (number % 8)
        lines = [part[s * share : (s + 1) * share] for part in made]
        extra = jnp.zeros((8, 2 * near.shape[2]), f32)
        if s < 3:
            extra = jnp.where(group == 0, small[s * 8 : s * 8 + 8], extra)
        whole = jnp.concatenate(lines + [extra.astype(bf16)], axis=0)

        @pl.when(step < 2)
        def _():
            near[spot] = whole[:, : near.shape[2]]
            near_right[spot] = whole[:, near.shape[2] :]

        @pl.when(step >= 2)
        def _():
            far[spot] = whole[:, : near.shape[2]]
            far_right[spot] = whole[:, near.shape[2] :]


def weight_blocks(facts, lefts, rights, branch, bias_grad, gain_grad, router_grad, local):
    tokens, width = lefts[0].shape
    rows = 4 * width // 32 + 8
    cut = lambda count: pl.BlockSpec((count, width // 4), lambda i, f: (0, i ^ (f[3] // 8)))
    full = lambda count: pl.BlockSpec((count, width), lambda i, f: (0, 0))
    out = lambda which: pl.BlockSpec((8, rows, width // 2), which)
    return pl.pallas_call(
        partial(blocks_kernel, local),
        grid_spec=pltpu.PrefetchScalarGridSpec(
            num_scalar_prefetch=1,
            grid=(4,),
            in_specs=[cut(left.shape[0]) for left in lefts]
            + [full(right.shape[0]) for right in rights]
            + [
                full(tokens),
                pl.BlockSpec(bias_grad.shape, lambda i, f: (0, 0, 0)),
                full(1),
                full(router_grad.shape[0]),
            ],
            out_specs=[
                out(lambda i, f: (jnp.minimum(i, 1), 0, 0)),
                out(lambda i, f: (jnp.maximum(i - 2, 0), 0, 0)),
            ]
            * 2,
        ),
        out_shape=[jax.ShapeDtypeStruct((16, rows, width // 2), bf16)] * 4,
        compiler_params=params(),
        cost_estimate=cost(17),
        name="weight_blocks",
    )(facts, *lefts, *rights, branch, bias_grad, gain_grad, router_grad)


def unpack_kernel(facts, near, far, w_query, w_key, w_value, gain, *refs):
    query, key, value, proj, gain_grad, small = refs[-6:]
    step = pl.program_id(0)
    number = facts[3]
    group = step ^ (number // 8)
    share = (near.shape[1] - 8) // 4

    def spread(source):
        for s in range(8):
            block = source[s ^ (number % 8)].astype(f32)
            for which, out in enumerate((query, key, value, proj)):
                out[s * share : (s + 1) * share] = block[which * share : (which + 1) * share]
            if s < 3:

                @pl.when(group == 0)
                def _():
                    small[s * 8 : s * 8 + 8] = block[4 * share :]

    @pl.when(step < 2)
    def _():
        spread(near)

    @pl.when(step >= 2)
    def _():
        spread(far)

    sums = query[...] * w_query[...].astype(f32)
    sums = sums + key[...] * w_key[...].astype(f32)
    sums = sums + value[...] * w_value[...].astype(f32)
    column = jnp.sum(sums, axis=-1, keepdims=True)
    size = column.shape[0]
    match = lax.broadcasted_iota(jnp.int32, (size, size), 0) == lax.broadcasted_iota(
        jnp.int32, (size, size), 1
    )
    line = jnp.sum(jnp.where(match, column, 0.0), axis=0, keepdims=True)
    gain_grad[...] = line / gain[...].astype(f32)


def unpack_blocks(facts, near, far, w_query, w_key, w_value, gain, before, half):
    width = w_query.shape[0]
    wide = width // 2
    rows = near.shape[1]
    step = width // 4
    line = pl.BlockSpec((1, step), lambda i, f: (0, i ^ (f[3] // 8)))
    block = pl.BlockSpec((step, wide), lambda i, f: (i ^ (f[3] // 8), half))
    return pl.pallas_call(
        unpack_kernel,
        grid_spec=pltpu.PrefetchScalarGridSpec(
            num_scalar_prefetch=1,
            grid=(4,),
            in_specs=[
                pl.BlockSpec((8, rows, wide), lambda i, f: (jnp.minimum(i, 1), 0, 0)),
                pl.BlockSpec((8, rows, wide), lambda i, f: (jnp.maximum(i - 2, 0), 0, 0)),
                block,
                block,
                block,
                line,
            ]
            + [pl.BlockSpec(memory_space=pl.ANY)] * len(before),
            out_specs=[block, block, block, block, line, pl.BlockSpec((24, wide), lambda i, f: (0, 0))],
        ),
        out_shape=[jax.ShapeDtypeStruct((width, width), f32)] * 4
        + [jax.ShapeDtypeStruct((1, width), f32), jax.ShapeDtypeStruct((24, wide), f32)],
        input_output_aliases={7 + i: i for i in range(len(before))},
        compiler_params=params(),
        cost_estimate=cost(8),
        name="unpack_blocks",
    )(facts, near, far, w_query, w_key, w_value, gain.reshape(1, width), *before)


def per_device(
    inputs,
    attn_gain,
    w_query,
    w_key,
    w_value,
    w_proj,
    rel_bias,
    moe_gain,
    w_router,
    w_gate,
    w_up,
    w_down,
    routes,
    long_buckets,
    short_buckets,
    long_lens,
    short_lens,
    cotangent,
):
    experts_axis = lax.axis_size("expert")
    tensor_axis = lax.axis_size("tensor")
    place = lax.axis_index("tensor")
    tok_count, width = inputs.shape
    top_count = routes.shape[1]
    short_len = (short_buckets.shape[0] + 1) // 2
    long_span = (long_buckets.shape[0] + 1) // 2
    long_local = tok_count - short_len
    bucket_count, heads = rel_bias.shape
    head_dim = width // heads
    experts = w_router.shape[1]
    local = experts // experts_axis
    capacity = (5 * tok_count * top_count + 4 * experts - 1) // (4 * experts)
    padded = (capacity + 2 + 15) // 16 * 16
    block = experts_axis * padded
    rel_table = rel_bias.astype(f32)
    here = lax.axis_index("expert")
    number = (here % 2) * 16 + place * 4 + here // 2
    paired = tensor_axis == 4 and local == 2
    routes_rows = jnp.transpose(routes)
    router = jnp.transpose(w_router)
    gate_turned = jnp.swapaxes(w_gate, 1, 2)
    up_turned = jnp.swapaxes(w_up, 1, 2)
    if paired:
        turns = jnp.stack([place % 2, place // 2]).astype(jnp.int32)
        which = jnp.where(here % 2 == 0, turns[0], turns[1])
        part_of = jnp.where(here % 2 == 0, turns[1], turns[0])
        shares = 2
    else:
        turns = jnp.zeros((2,), jnp.int32)
        which, part_of, shares = jnp.int32(0), place, tensor_axis
    facts = [place, long_lens[0], short_lens[0], number, which, part_of, 1 - which]
    facts = jnp.stack([jnp.asarray(fact, jnp.int32) for fact in facts])

    def trade(rows, other):
        pairs = []
        for e in range(experts_axis):
            mask = (2 if e % 2 == 0 else 1) if other else (1 if e % 2 == 0 else 2)
            pairs += [(e * tensor_axis + t, e * tensor_axis + (t ^ mask)) for t in range(tensor_axis)]
        return lax.ppermute(rows, ("expert", "tensor"), pairs)

    long_rows = inputs[:long_local]
    sources = [swap(long_rows, "tensor", r) for r in range(1, tensor_axis)]
    normed_low, query, pair, near = project(inputs, attn_gain, w_query, w_key, w_value, long_local)
    slots, wide_slots, grad_slots_in = place_rows(
        turns.reshape(1, 2), after(routes_rows, normed_low), cotangent, capacity, padded, block, local
    )

    def by_expert(rows):
        split = rows.reshape(experts_axis, local, padded, width)
        return [split[:, j].reshape(block, width) for j in range(local)]

    def by_device(parts):
        split = [part.reshape(experts_axis, 1, padded, width) for part in parts]
        return jnp.concatenate(split, axis=1).reshape(local * block, width)

    grad_whole = over_experts(grad_slots_in)
    normed_others, others = project_others(sources, attn_gain, w_key, w_value, long_local)
    parts = (pair, others)
    if paired:
        other = jnp.stack(
            [
                lax.dynamic_index_in_dim(array, 1 - which, 0, keepdims=False)
                for array in (gate_turned, up_turned, w_down)
            ]
        )
        other = trade(after(other, sources), False)

    reach = long_span + long_local
    first = long_span - long_local - long_local * place
    long_table = jnp.pad(long_buckets, (0, 1), constant_values=-1)
    long_hot = table_hot(lax.dynamic_slice_in_dim(long_table, first, reach, 0), bucket_count)
    short_hot = table_hot(jnp.pad(short_buckets, (0, 1), constant_values=-1), bucket_count)
    spread = lambda hot: jnp.einsum(
        "cb,bh->hc", hot, rel_table, precision=precise, preferred_element_type=f32
    ).reshape(heads // 2, 2, hot.shape[0])
    mixed, far_attend, near_attend = attend_forward(
        facts, query, parts, near, spread(long_hot), spread(short_hot),
        tensor_axis, long_local, head_dim,
    )
    resid, moe_low, probs, gates, *slots_in = route_rows(
        mixed, w_proj, inputs, moe_gain, router, routes_rows, slots, capacity, padded, block, local
    )

    own = (gate_turned, up_turned, w_down)
    lanes_used = shares * padded
    if paired:

        run = lambda rows, grads: expert_pass(
            facts, rows, grads, own, other, capacity, padded, lanes_used
        )
        grad_arrived = by_expert(after(grad_whole, slots_in))
        grads_b = trade(grad_arrived[1], False)
        grads_d = trade(grads_b, True)
        rows_b = over_experts(slots_in[1])
        rows_a = over_experts(after(slots_in[0], rows_b))
        rows_b = trade(after(rows_b, grads_b), False)
        rows_d = trade(rows_b, True)
        grads_c = trade(after(grad_arrived[0], rows_d), True)
        pass_b = run(rows_b, grads_b)
        pass_d = run(after(rows_d, pass_b[1]), grads_d)
        rows_c = trade(after(rows_a, rows_d), True)
        pass_a = run(after(rows_a, pass_d[1], grads_c, rows_c), grad_arrived[0])
        traded = add_low(pass_b[2], after(trade(pass_d[2], True), pass_a[1]))
        traded = trade(traded, False)
        pass_c = run(after(rows_c, pass_a[1]), grads_c)
        traded = after(traded, pass_c[1])
        traded_back = over_experts(traded)
        kept = add_low(pass_a[2], trade(after(pass_c[2], traded), True))
        grad_slots = [over_experts(after(kept, traded_back)), traded_back]

        passes = [pass_a, pass_c, pass_b, pass_d]
        slot_blocks = [rows_a, rows_c, rows_b, rows_d]
        grad_blocks = [grad_arrived[0], grads_c, grads_b, grads_d]
        (sent,) = weight_pass(
            facts, slot_blocks, grad_blocks, [after_all(made[0][1], pass_c[1]) for made in passes], (), local, True
        )
        weight_grads = weight_pass(
            facts, slot_blocks, grad_blocks, [after_all(made[0][0], sent) for made in passes], (), local, False
        )
        outs_d = trade(after(pass_d[1], traded), True)
        outs_c = trade(after(pass_c[1], kept, outs_d), True)
        outs_traded = trade(add_low(pass_b[1], outs_d), False)
        outs_kept = add_low(pass_a[1], outs_c)
        grad_slots[0] = after(grad_slots[0], weight_grads, outs_c, outs_traded)
        held_back = outs_traded
        sent = trade(after(sent, outs_traded), False)
        outs_back = over_experts(after(by_device([outs_kept, outs_traded]), grad_slots[0]))
    else:
        grad_blocks = [gather_parts(rows) for rows in by_expert(grad_whole)]
        slot_blocks = [gather_parts(over_experts(slots_in[j])) for j in range(local)]
        weight_grads, passes = (), []
        for j in range(local):
            facts_j = facts.at[4].set(j)
            passes.append(
                [
                    expert_pass(facts_j, rows, grads, own, None, capacity, padded, lanes_used)
                    for rows, grads in zip(slot_blocks[j], grad_blocks[j])
                ]
            )
            weight_grads = weight_pass(
                facts_j, slot_blocks[j], grad_blocks[j], [made[0][0] for made in passes[j]], weight_grads, local, False
            )
        send_back = lambda which: [
            over_experts(sum_parts([made[which] for made in passes[j]]).astype(bf16)) for j in range(local)
        ]
        grad_slots = send_back(2)
        outs_back = by_device(send_back(1))
        held_back = sent = grad_slots[0]

    grad_resid, grad_mixed, moe_gain_grad, router_grad, branch = merge_rows(
        cotangent, resid, probs, moe_low, router, moe_gain, w_proj, routes_rows, slots, grad_slots,
        capacity, padded, shares,
    )
    grad_mixed = after(grad_mixed, held_back)
    quick = experts_axis == 8 and tensor_axis == 4
    hots = (long_hot.astype(bf16), short_hot.astype(bf16))
    *attn_grads, bias_grad = attend_backward(
        facts, query, grad_mixed, parts, near, (far_attend, near_attend), hots, tensor_axis, long_local, head_dim
    )
    if quick:
        bias_grad = after(bias_grad, sent, outs_back)
        made = weight_blocks(
            facts, (normed_low, normed_others, mixed), attn_grads, branch, bias_grad, moe_gain_grad, router_grad,
            long_local,
        )
        sums = [add_low(made[half], swap(made[half + 1], "expert", 1)) for half in (0, 2)]
        attn_grads = after_all(attn_grads, sums)
    own_grads, near_grads, away = normed_grads(attn_grads, w_query, w_key, w_value, long_local, tensor_axis)
    if quick:
        sums = [ring_sum(plane_parts(part), in_plane).astype(bf16) for part in sums]
        away = after(away, sums)
    pieces = [own_grads] + [
        away[r * long_local : (r + 1) * long_local].astype(bf16) for r in range(tensor_axis - 1)
    ]
    if tensor_axis == 4:
        pieces = pieces[:3] + [pieces[3][: long_local // 2], pieces[3][long_local // 2 :]]
    summed = sum_parts(pieces)
    if quick:
        sums = [spread_depth(sum_depth(part)) for part in sums]
        sums[1] = after(sums[1], summed)
        sent, outs_back, summed = after_all((sent, outs_back, summed), sums[0])
    if paired:
        weight_grads = weight_fill(facts, sent, weight_grads)
    slot_places = jnp.arange(local * block, dtype=jnp.int32)
    outputs = resid
    for k in range(top_count):
        chosen = mm((wide_slots[k][:, None] == slot_places).astype(bf16), outs_back)
        outputs = outputs + gates[k][:, None] * chosen
    outputs = outputs.astype(bf16)
    grad_normed = jnp.concatenate([summed, near_grads], axis=0)
    inputs_wide = inputs.astype(f32)
    scale = lax.rsqrt(jnp.mean(inputs_wide * inputs_wide, axis=-1, keepdims=True) + 1e-06)
    normed = inputs_wide * scale
    lifted = grad_normed * attn_gain.astype(f32)
    inputs_grad = grad_resid + scale * (
        lifted - normed * jnp.mean(lifted * normed, axis=-1, keepdims=True)
    )
    if quick:
        sums = [spread_plane(part) for part in sums]
        far = [swap(part, "expert", 1) for part in sums]
        sums[0] = after(sums[0], outputs, weight_grads, inputs_grad)
        unpack = partial(unpack_blocks, facts)
        weights = (w_query, w_key, w_value, attn_gain)
        first = unpack(sums[0], far[0], *weights, (), 0)
        second = unpack(sums[1], far[1], *weights, first[:4], 1)
        query_grad, key_grad, value_grad, proj_grad = second[:4]
        attn_gain_grad = (first[4] + second[4])[0]
        small = jnp.concatenate([first[5], second[5]], axis=1)
    else:
        key_others = [slice(2 * r * long_local, (2 * r + 1) * long_local) for r in range(tensor_axis - 1)]
        value_others = [slice((2 * r + 1) * long_local, (2 * r + 2) * long_local) for r in range(tensor_axis - 1)]

        def keyed(index, spots):
            short = slice(index * short_len, (index + 1) * short_len)
            rows = slice(index * long_local, (index + 1) * long_local)
            lefts = jnp.concatenate([normed_low, normed_others], axis=0)
            rights = jnp.concatenate(
                [attn_grads[1][rows], attn_grads[3][short]] + [attn_grads[2][spot] for spot in spots], axis=0
            )
            return mm(lefts, rights, TN)

        rel_row = jnp.pad(bias_grad.reshape(1, -1), ((0, 0), (0, width - bias_grad.size)))
        small = jnp.concatenate([rel_row, moe_gain_grad, router_grad], axis=0)
        query_grad, key_grad, value_grad, proj_grad, small = lax.psum(
            (
                mm(normed_low, attn_grads[0], TN),
                keyed(0, key_others),
                keyed(1, value_others),
                mm(mixed, branch, TN),
                small,
            ),
            ("expert", "tensor"),
        )
        attn_gain_grad = jnp.sum(
            query_grad * w_query.astype(f32) + key_grad * w_key.astype(f32) + value_grad * w_value.astype(f32),
            axis=1,
        ) / attn_gain.astype(f32)
    rel_grad = jnp.transpose(small[0, : heads * bucket_count].reshape(heads, bucket_count))
    return (
        outputs,
        inputs_grad,
        attn_gain_grad,
        query_grad,
        key_grad,
        value_grad,
        proj_grad,
        rel_grad,
        small[1],
        jnp.transpose(small[2 : 2 + experts]),
        jnp.swapaxes(weight_grads[0], 1, 2),
        jnp.swapaxes(weight_grads[1], 1, 2),
        weight_grads[2],
    )


def solution(mesh):
    return jax.shard_map(
        per_device,
        mesh=mesh,
        in_specs=(
            P(("expert", "tensor"), None),
            P(),
            P(),
            P(),
            P(),
            P(),
            P(),
            P(),
            P(),
            P("expert", None, "tensor"),
            P("expert", None, "tensor"),
            P("expert", "tensor", None),
            P(("expert", "tensor"), None),
            P(),
            P(),
            P("expert"),
            P(("expert", "tensor")),
            P(("expert", "tensor"), None),
        ),
        out_specs=(
            P(("expert", "tensor"), None),
            P(("expert", "tensor"), None),
            P(),
            P(),
            P(),
            P(),
            P(),
            P(),
            P(),
            P(),
            P("expert", None, "tensor"),
            P("expert", None, "tensor"),
            P("expert", "tensor", None),
        ),
        check_vma=False,
    )
```

```python
from functools import partial
import math

import jax
import jax.numpy as jnp
from jax import lax
from jax.experimental import pallas as pl
from jax.experimental.pallas import tpu as pltpu
from jax.sharding import PartitionSpec as P

precise = lax.Precision.HIGHEST
bf16 = jnp.bfloat16
f32 = jnp.float32
NT = (((1,), (1,)), ((), ()))
NN = (((1,), (0,)), ((), ()))
TN = (((0,), (0,)), ((), ()))
VMEM_BYTES = 56 * 1024 * 1024


def mm(left, right, dims=NN):
    return lax.dot_general(left, right, dims, preferred_element_type=f32)


def params():
    return pltpu.CompilerParams(
        dimension_semantics=("arbitrary",), vmem_limit_bytes=VMEM_BYTES
    )


def cost(micros):
    return pl.CostEstimate(flops=int(micros * 1.15e9), bytes_accessed=0, transcendentals=0)


def table_hot(table, count):
    return (table[:, None] == jnp.arange(count, dtype=jnp.int32)[None, :]).astype(f32)


def swap(rows, axis, mask):
    count = lax.axis_size(axis)
    return lax.ppermute(rows, axis, [(i, i ^ mask) for i in range(count)])


def after(value, *others):
    return lax.optimization_barrier((value,) + tuple(jax.tree.leaves(others)))[0]


def after_all(values, *others):
    leaves = tuple(jax.tree.leaves(others))
    return list(lax.optimization_barrier(tuple(values) + leaves)[: len(values)])


def ring_gather(rows, move):
    half = rows.shape[0] // 2
    first, second = move(rows, 0), move(rows, 1)
    return [rows, first, second, move(first[:half], 1), move(second[half:], 0)]


def ring_sum_first(parts, move):
    half = parts[3].shape[0]
    left = move(parts[3], 0)
    right = move(parts[4], 1)
    to_second = jnp.concatenate([add_low(parts[2][:half], left), parts[2][half:]], axis=0)
    to_first = jnp.concatenate([parts[1][:half], add_low(parts[1][half:], right)], axis=0)
    return parts[0], to_first, to_second


def ring_sum_second(own, to_first, to_second, move):
    first = move(to_first, 0)
    second = move(to_second, 1)
    return own.astype(f32) + first.astype(f32) + second.astype(f32)


def ring_sum(parts, move):
    return ring_sum_second(*ring_sum_first(parts, move), move)


def in_plane(rows, way):
    return swap(rows, "tensor", 1 + way)


def gather_parts(rows):
    count = lax.axis_size("tensor")
    if count == 4:
        return ring_gather(rows, in_plane)
    return [rows] + [swap(rows, "tensor", r) for r in range(1, count)]


def sum_parts(parts):
    count = lax.axis_size("tensor")
    if count == 4:
        return ring_sum(parts, in_plane)
    arrived = [swap(parts[r], "tensor", r) for r in range(1, count)]
    return sum([part.astype(f32) for part in arrived], parts[0].astype(f32))


def over_experts(rows):
    experts_axis = lax.axis_size("expert")
    blocks = rows.reshape(experts_axis, rows.shape[0] // experts_axis, rows.shape[1])
    return lax.all_to_all(blocks, "expert", 0, 0, tiled=True).reshape(rows.shape)


def add_low(left, right):
    return (left.astype(f32) + right.astype(f32)).astype(bf16)


def sum_cores(near, far):
    return add_low(near, swap(far, "expert", 1))


def plane_parts(rest):
    return [rest[0:4], rest[4:8], rest[8:12], rest[12:14], rest[14:16]]


def sum_depth(rest):
    arrived = swap(rest[1::2], "expert", 2)
    own, opposite = add_low(rest[0], arrived[0]), add_low(rest[2], arrived[1])
    return add_low(own, swap(opposite, "expert", 4))


def spread_depth(own):
    opposite = swap(own, "expert", 4)
    arrived = swap(jnp.stack([own, opposite]), "expert", 2)
    return jnp.stack([own, arrived[0], opposite, arrived[1]])


def spread_plane(rest):
    return jnp.concatenate(ring_gather(rest, in_plane), axis=0)


def project_kernel(long_local, inputs, gain, w_query, w_key, w_value, normed, query, pair, near, held):
    @pl.when(pl.program_id(0) == 0)
    def _():
        rows = inputs[...].astype(f32)
        scale = lax.rsqrt(jnp.mean(rows * rows, axis=-1, keepdims=True) + 1e-06)
        held[...] = (rows * scale * gain[...].astype(f32)).astype(bf16)
        normed[...] = held[...]

    rows = held[...]
    query[...] = mm(rows, w_query[...]).astype(bf16)
    keys = mm(rows, w_key[...]).astype(bf16)
    values = mm(rows, w_value[...]).astype(bf16)
    pair[:long_local] = keys[:long_local]
    pair[long_local:] = values[:long_local]
    short = keys.shape[0] - long_local
    near[:short] = keys[long_local:]
    near[short:] = values[long_local:]


def project(inputs, gain, w_query, w_key, w_value, long_local):
    rows, width = inputs.shape
    short = rows - long_local
    step = 256
    whole = lambda count: pl.BlockSpec((count, width), lambda i: (0, 0))
    cut = lambda count: pl.BlockSpec((count, step), lambda i: (0, i))
    return pl.pallas_call(
        partial(project_kernel, long_local),
        grid=(width // step,),
        in_specs=[whole(rows), whole(1), cut(width), cut(width), cut(width)],
        out_specs=[whole(rows), cut(rows), cut(2 * long_local), cut(2 * short)],
        out_shape=[
            jax.ShapeDtypeStruct((rows, width), bf16),
            jax.ShapeDtypeStruct((rows, width), bf16),
            jax.ShapeDtypeStruct((2 * long_local, width), bf16),
            jax.ShapeDtypeStruct((2 * short, width), bf16),
        ],
        scratch_shapes=[pltpu.VMEM((rows, width), bf16)],
        compiler_params=params(),
        cost_estimate=cost(6.9),
        name="project",
    )(inputs, gain.reshape(1, width), w_query, w_key, w_value)


def project_others_kernel(local, gain, w_key, w_value, *refs):
    sources, (normed, pairs, held) = refs[:-3], refs[-3:]

    @pl.when(pl.program_id(0) == 0)
    def _():
        rows = jnp.concatenate([source[...] for source in sources], axis=0).astype(f32)
        scale = lax.rsqrt(jnp.mean(rows * rows, axis=-1, keepdims=True) + 1e-06)
        held[...] = (rows * scale * gain[...].astype(f32)).astype(bf16)
        normed[...] = held[...]

    keys = mm(held[...], w_key[...]).astype(bf16)
    values = mm(held[...], w_value[...]).astype(bf16)
    for r in range(keys.shape[0] // local):
        pairs[2 * r * local : (2 * r + 1) * local] = keys[r * local : (r + 1) * local]
        pairs[(2 * r + 1) * local : (2 * r + 2) * local] = values[r * local : (r + 1) * local]


def project_others(sources, gain, w_key, w_value, local):
    rows = sum(source.shape[0] for source in sources)
    width = gain.shape[0]
    step = 256
    whole = lambda count: pl.BlockSpec((count, width), lambda i: (0, 0))
    cut = lambda count: pl.BlockSpec((count, step), lambda i: (0, i))
    return pl.pallas_call(
        partial(project_others_kernel, local),
        grid=(width // step,),
        in_specs=[whole(1), cut(width), cut(width)] + [whole(source.shape[0]) for source in sources],
        out_specs=[whole(rows), cut(2 * rows)],
        out_shape=[
            jax.ShapeDtypeStruct((rows, width), bf16),
            jax.ShapeDtypeStruct((2 * rows, width), bf16),
        ],
        scratch_shapes=[pltpu.VMEM((rows, width), bf16)],
        compiler_params=params(),
        cost_estimate=cost(7.7),
        name="project_others",
    )(gain.reshape(1, width), w_key, w_value, *sources)


def key_value_views(pair, others, count, rows):
    views = [(pair, slice(0, rows), pair, slice(rows, 2 * rows))]
    for r in range(count - 1):
        at = 2 * r * rows
        views.append((others, slice(at, at + rows), others, slice(at + rows, at + 2 * rows)))
    return views


def own_lanes(head, dim, shape, axis):
    place = lax.broadcasted_iota(jnp.int32, shape, axis)
    return (place >= head * dim) & (place < (head + 1) * dim)


def forward_kernel(
    count,
    rows,
    dim,
    facts,
    query,
    pair,
    others,
    near,
    far_bias,
    near_bias,
    mixed,
    far_attend,
    near_attend,
    window,
    scores,
):
    place, far_len, near_len = facts[0], facts[1], facts[2]
    scale = 1.0 / math.sqrt(dim)
    views = key_value_views(pair, others, count, rows)
    short = near.shape[0] // 2
    band, reach = window.shape[1:]
    low = (query[...].astype(f32) * scale).astype(bf16)
    starts = [(place ^ r) * rows for r in range(count)]
    spot = lax.broadcasted_iota(jnp.int32, (1, rows), 1)
    kept = [start + spot < far_len for start in starts]
    near_kept = lax.broadcasted_iota(jnp.int32, (1, short), 1) < near_len
    line = 2 * (pl.program_id(0) % 4)
    mine = [jnp.where(own_lanes(head, dim, low.shape, 1), low, jnp.zeros_like(low)) for head in range(2)]
    far_mine = jnp.concatenate([part[:rows] for part in mine], axis=0)
    near_parts = mm(jnp.concatenate([part[rows:] for part in mine], axis=0), near[:short], NT)
    near_parts = [near_parts[:short], near_parts[short:]]
    for r in range(count):
        part = mm(far_mine, views[r][0][views[r][1]], NT)
        for head in range(2):
            scores[head, :, r * rows : (r + 1) * rows] = part[head * rows : (head + 1) * rows]
    for head in range(2):
        table = jnp.broadcast_to(far_bias[pl.ds(line + head, 1)], (band, reach))
        window[head] = pltpu.roll(table, reach - (band - 1), 1, stride=1, stride_axis=0)
    for head in range(2):
        table = jnp.broadcast_to(near_bias[pl.ds(line + head, 1)], (short, 2 * short))
        bias = pltpu.roll(table, short + 1, 1, stride=1, stride_axis=0)[:, :short]
        part = jnp.where(near_kept, near_parts[head] + bias, -1e30)
        part = jnp.exp(part - jnp.max(part, axis=-1, keepdims=True))
        near_attend[head] = (part * (1.0 / jnp.sum(part, axis=-1, keepdims=True))).astype(bf16)
        for at in range(0, rows, 32):
            shift = band * (rows // band - 1 - at // band)
            lines = slice(at % band, at % band + 32)
            parts = []
            for r in range(count):
                begin = pl.multiple_of(starts[r] + shift, 128)
                part = scores[head, at : at + 32, r * rows : (r + 1) * rows]
                part = part + window[head, lines, pl.ds(begin, rows)]
                parts.append(jnp.where(kept[r], part, -1e30))
            highest = parts[0]
            for part in parts[1:]:
                highest = jnp.maximum(highest, part)
            highest = jnp.max(highest, axis=-1, keepdims=True)
            parts = [jnp.exp(part - highest) for part in parts]
            whole = parts[0]
            for part in parts[1:]:
                whole = whole + part
            inverse = 1.0 / jnp.sum(whole, axis=-1, keepdims=True)
            for r in range(count):
                far_attend[head, at : at + 32, r * rows : (r + 1) * rows] = (parts[r] * inverse).astype(bf16)
    out = jnp.zeros((2 * rows, 2 * dim), f32)
    for r in range(count):
        attend = far_attend[:, :, r * rows : (r + 1) * rows].reshape(2 * rows, rows)
        out = out + mm(attend, views[r][2][views[r][3]])
    near_out = mm(near_attend[...].reshape(2 * short, short), near[short:])
    second = own_lanes(1, dim, (rows, 2 * dim), 1)
    mixed[:rows] = jnp.where(second, out[rows:], out[:rows]).astype(bf16)
    second = own_lanes(1, dim, (short, 2 * dim), 1)
    mixed[rows:] = jnp.where(second, near_out[short:], near_out[:short]).astype(bf16)


def attention_specs(count, rows, short, reach, tokens):
    cut = lambda size: pl.BlockSpec((size, 128), lambda i, *_: (0, i))
    parts = [cut(2 * rows), cut(2 * (count - 1) * rows)]
    table = lambda size: pl.BlockSpec((8, size), lambda i, *_: (i // 4, 0))
    weights = lambda size, span: pl.BlockSpec((2, size, span), lambda i, *_: (i, 0, 0))
    return (
        cut(tokens),
        parts,
        cut(2 * short),
        [table(reach), table(2 * short)],
        [weights(rows, count * rows), weights(short, short)],
    )


def attend_forward(facts, query, parts, near, far_bias, near_bias, count, rows, dim):
    tokens, width = query.shape
    heads = width // dim
    short = near.shape[0] // 2
    reach = far_bias.shape[-1]
    cut, part_specs, near_spec, tables, weights = attention_specs(count, rows, short, reach, tokens)
    return pl.pallas_call(
        partial(forward_kernel, count, rows, dim),
        grid_spec=pltpu.PrefetchScalarGridSpec(
            num_scalar_prefetch=1,
            grid=(heads // 2,),
            in_specs=[cut] + part_specs + [near_spec] + tables,
            out_specs=[cut] + weights,
            scratch_shapes=[pltpu.VMEM((2, 128, reach), f32), pltpu.VMEM((2, rows, count * rows), f32)],
        ),
        out_shape=[
            jax.ShapeDtypeStruct((tokens, width), bf16),
            jax.ShapeDtypeStruct((heads, rows, count * rows), bf16),
            jax.ShapeDtypeStruct((heads, short, short), bf16),
        ],
        compiler_params=params(),
        cost_estimate=cost(17),
        name="attend_forward",
    )(facts, query, *parts, near, far_bias, near_bias)


def backward_kernel(
    count,
    rows,
    dim,
    facts,
    query,
    grad,
    pair,
    others,
    near,
    far_attend,
    near_attend,
    far_hot,
    near_hot,
    grad_query,
    grad_pair,
    grad_others,
    grad_near,
    bias_grad,
    window,
    near_window,
    products,
    scores,
    near_scores,
):
    place = facts[0]
    scale = 1.0 / math.sqrt(dim)
    views = key_value_views(pair, others, count, rows)
    grad_views = key_value_views(grad_pair, grad_others, count, rows)
    short = near.shape[0] // 2
    band = window.shape[1]
    starts = [(place ^ r) * rows for r in range(count)]

    @pl.when(pl.program_id(0) == 0)
    def _():
        near_window[...] = jnp.zeros_like(near_window)

    def reversal(size):
        up = lax.broadcasted_iota(jnp.int32, (size, size), 0)
        across = lax.broadcasted_iota(jnp.int32, (size, size), 1)
        return (up + across == size - 1).astype(bf16)

    far_turn = reversal(band)
    near_turn = far_turn if short == band else reversal(short)
    low, grad_low = query[...], grad[...]
    turned = jnp.transpose(low.astype(f32) * scale, (1, 0)).astype(bf16)
    grad_turned = jnp.transpose(grad_low.astype(f32), (1, 0)).astype(bf16)
    mine, grad_mine, grad_heads = [], [], []
    for head in range(2):
        lines = own_lanes(head, dim, turned.shape, 0)
        mine.append(jnp.where(lines, turned, jnp.zeros_like(turned)))
        grad_mine.append(jnp.where(lines, grad_turned, jnp.zeros_like(turned)))
        lanes = own_lanes(head, dim, low.shape, 1)
        grad_heads.append(jnp.where(lanes, grad_low, jnp.zeros_like(grad_low)))
    far_grads = jnp.concatenate([part[:rows] for part in grad_heads], axis=0)
    near_parts = mm(jnp.concatenate([part[rows:] for part in grad_heads], axis=0), near[short:], NT)
    for r in range(count):
        part = mm(far_grads, views[r][2][views[r][3]], NT)
        for head in range(2):
            products[head, :, r * rows : (r + 1) * rows] = part[head * rows : (head + 1) * rows]
    window[...] = jnp.zeros_like(window)
    for head in range(2):
        wide = near_attend[head].astype(f32)
        part = near_parts[head * short : (head + 1) * short]
        part = wide * (part - jnp.sum(wide * part, axis=-1, keepdims=True))
        near_scores[head] = part.astype(bf16)
        for at in range(0, rows, 32):
            attend = far_attend[head, at : at + 32].astype(f32)
            part = products[head, at : at + 32]
            inner = jnp.sum(attend * part, axis=-1, keepdims=True)
            scores[head, at : at + 32] = (attend * (part - inner)).astype(bf16)
    out = jnp.zeros((2 * rows, 2 * dim), f32)
    for r in range(count):
        part = scores[:, :, r * rows : (r + 1) * rows].reshape(2 * rows, rows)
        out = out + mm(part, views[r][0][views[r][1]])
        for head in range(2):
            for h in range(rows // band):
                begin = pl.multiple_of(starts[r] + band * (rows // band - 1 - h), 128)
                lines = slice(head * rows + h * band, head * rows + (h + 1) * band)
                window[head, :, pl.ds(begin, rows)] += mm(far_turn, part[lines])
    near_out = mm(near_scores[...].reshape(2 * short, short), near[:short])
    second = own_lanes(1, dim, (rows, 2 * dim), 1)
    grad_query[:rows] = (jnp.where(second, out[rows:], out[:rows]) * scale).astype(bf16)
    second = own_lanes(1, dim, (short, 2 * dim), 1)
    grad_query[rows:] = (jnp.where(second, near_out[short:], near_out[:short]) * scale).astype(bf16)
    def by_bucket(lines, hot):
        row = lax.broadcasted_iota(jnp.int32, (16, lines.shape[1]), 0)
        high = lines.astype(bf16).astype(f32)
        rest = lines - high
        middle = rest.astype(bf16).astype(f32)
        stack = jnp.where(row == 0, high, jnp.where(row == 1, middle, jnp.where(row == 2, rest - middle, 0.0)))
        return jnp.sum(mm(stack.astype(bf16), hot[...]), axis=0, keepdims=True)

    for head in range(2):
        rolled = pltpu.roll(window[head], 0, 1, stride=1, stride_axis=0)
        sums = by_bucket(jnp.sum(rolled, axis=0, keepdims=True), far_hot)
        near_window[head, :, :short] = mm(near_turn, near_scores[head])
        rolled = pltpu.roll(near_window[head], 0, 1, stride=1, stride_axis=0)
        sums = sums + by_bucket(jnp.sum(rolled, axis=0, keepdims=True), near_hot)
        bias_grad[0, head : head + 1, :] = sums
    for r in range(count):
        lanes = slice(r * rows, (r + 1) * rows)
        keys = mm(mine[0][:, :rows], scores[0, :, lanes]) + mm(mine[1][:, :rows], scores[1, :, lanes])
        values = mm(grad_mine[0][:, :rows], far_attend[0, :, lanes]) + mm(
            grad_mine[1][:, :rows], far_attend[1, :, lanes]
        )
        view = grad_views[r]
        view[0][view[1]] = jnp.transpose(keys, (1, 0)).astype(bf16)
        view[2][view[3]] = jnp.transpose(values, (1, 0)).astype(bf16)
    keys = mm(mine[0][:, rows:], near_scores[0]) + mm(mine[1][:, rows:], near_scores[1])
    values = mm(grad_mine[0][:, rows:], near_attend[0]) + mm(grad_mine[1][:, rows:], near_attend[1])
    grad_near[:short] = jnp.transpose(keys, (1, 0)).astype(bf16)
    grad_near[short:] = jnp.transpose(values, (1, 0)).astype(bf16)


def attend_backward(facts, query, grad, parts, near, weights, hots, count, rows, dim):
    tokens, width = query.shape
    pairs = width // dim // 2
    short = near.shape[0] // 2
    reach, buckets = hots[0].shape
    cut, part_specs, near_spec, _, weight_specs = attention_specs(count, rows, short, reach, tokens)
    return pl.pallas_call(
        partial(backward_kernel, count, rows, dim),
        grid_spec=pltpu.PrefetchScalarGridSpec(
            num_scalar_prefetch=1,
            grid=(pairs,),
            in_specs=[cut, cut]
            + part_specs
            + [near_spec]
            + weight_specs
            + [pl.BlockSpec(hot.shape, lambda i, *_: (0, 0)) for hot in hots],
            out_specs=[cut]
            + part_specs
            + [near_spec, pl.BlockSpec((1, 2, buckets), lambda i, *_: (i, 0, 0))],
            scratch_shapes=[
                pltpu.VMEM((2, 128, reach), f32),
                pltpu.VMEM((2, short, 2 * short), f32),
                pltpu.VMEM((2, rows, count * rows), f32),
                pltpu.VMEM((2, rows, count * rows), bf16),
                pltpu.VMEM((2, short, short), bf16),
            ],
        ),
        out_shape=[
            jax.ShapeDtypeStruct((size, width), bf16)
            for size in (tokens, 2 * rows, 2 * (count - 1) * rows, 2 * short)
        ]
        + [jax.ShapeDtypeStruct((pairs, 2, buckets), f32)],
        compiler_params=params(),
        cost_estimate=cost(25),
        name="attend_backward",
    )(facts, query, grad, *parts, near, *weights, *hots)


def normed_grads_kernel(local, count, query, pair, others, near, w_query, w_key, w_value, *outs):
    own, own_short, away = outs
    short = near.shape[0] // 2

    @pl.when(pl.program_id(0) == 0)
    def _():
        for out in outs:
            out[...] = jnp.zeros_like(out)

    full = mm(query[...], w_query[...], NT)
    own[...] += full[:local] + mm(pair[:local], w_key[...], NT) + mm(pair[local:], w_value[...], NT)
    own_short[...] += full[local:] + mm(near[:short], w_key[...], NT) + mm(near[short:], w_value[...], NT)
    for r in range(count - 1):
        at = 2 * r * local
        away[r * local : (r + 1) * local] += mm(others[at : at + local], w_key[...], NT) + mm(
            others[at + local : at + 2 * local], w_value[...], NT
        )


def normed_grads(grads, w_query, w_key, w_value, local, count):
    width = w_query.shape[0]
    short = grads[3].shape[0] // 2
    cut = lambda size: pl.BlockSpec((size, width // 2), lambda i: (0, i))
    sizes = (local, short, (count - 1) * local)
    return pl.pallas_call(
        partial(normed_grads_kernel, local, count),
        grid=(2,),
        in_specs=[cut(array.shape[0]) for array in grads] + [cut(width)] * 3,
        out_specs=[pl.BlockSpec((size, width), lambda i: (0, 0)) for size in sizes],
        out_shape=[jax.ShapeDtypeStruct((size, width), f32) for size in sizes],
        compiler_params=params(),
        cost_estimate=cost(13),
        name="normed_grads",
    )(*grads, w_query, w_key, w_value)


def expert_kernel(chunks, capacity, padded, lanes_used, facts, rows_in, grads_in, *refs):
    sources, rest = refs[: 3 * chunks], refs[3 * chunks :]
    middles, (out_ref, grad_ref) = rest[: 3 * chunks], rest[3 * chunks : 3 * chunks + 2]
    held, sems = rest[3 * chunks + 2 : 6 * chunks + 2], rest[6 * chunks + 2]
    rows = rows_in.shape[0]
    groups = rows // padded
    first = pl.program_id(0) == 0

    def copy(i):
        index = facts[4] if i < 3 else i % 3
        return pltpu.make_async_copy(sources[i].at[index], held[i], sems.at[i])

    @pl.when(first)
    def _():
        for i in range(3 * chunks):
            copy(i).start()
        for i in range(3 * chunks):
            copy(i).wait()

    slots = rows_in[...]
    grads = grads_in[...]
    spare = 16 - (padded - capacity)
    lanes = lax.broadcasted_iota(jnp.int32, (padded, 128), 1)
    match = lax.broadcasted_iota(jnp.int32, (padded, 128), 0) == lanes
    columns = []
    for g in range(groups):
        tail = rows_in[pl.ds((g + 1) * padded - 16, 16), :128].astype(f32)
        line = tail[spare : spare + 1] + tail[spare + 1 : spare + 2]
        columns.append(jnp.sum(jnp.where(match, line, 0.0), axis=-1, keepdims=True))
    gate_column = jnp.concatenate(columns, axis=0)

    lows = []
    slope = math.sqrt(2.0 / math.pi)
    for c in range(chunks):
        gate_pre = mm(slots, held[3 * c][...], NT)
        up_pre = mm(slots, held[3 * c + 1][...], NT)
        grad_hidden = mm(grads, held[3 * c + 2][...], NT) * gate_column
        square = gate_pre * gate_pre
        curve = jnp.tanh(slope * gate_pre * (1.0 + 0.044715 * square))
        side = 0.5 * (1.0 + curve)
        bent = gate_pre * side
        hidden = bent * up_pre
        bent_slope = side + 0.5 * slope * gate_pre * (1.0 - curve * curve) * (
            1.0 + 3.0 * 0.044715 * square
        )
        gate_low = (grad_hidden * up_pre * bent_slope).astype(bf16)
        up_low = (grad_hidden * bent).astype(bf16)
        middles[3 * c][...] = (hidden * gate_column).astype(bf16)
        middles[3 * c + 1][...] = gate_low
        middles[3 * c + 2][...] = up_low
        lows.append((gate_low, up_low, hidden.astype(bf16)))
    left = [jnp.concatenate([low[k] for low in lows], axis=1) for k in range(3)]
    right = [
        jnp.concatenate([held[3 * c + k][...] for c in range(chunks)], axis=0) for k in range(3)
    ]
    out = mm(left[2], right[2])
    grad_out = mm(left[0], right[0]) + mm(left[1], right[1])
    out_ref[...] = out.astype(bf16)
    grad_ref[...] = grad_out.astype(bf16)

    grad_gate = jnp.sum(out * grads.astype(f32), axis=-1, keepdims=True)
    lanes = lax.broadcasted_iota(jnp.int32, (padded, lanes_used), 1)
    up = lax.broadcasted_iota(jnp.int32, (padded, lanes_used), 0)
    match = up + facts[5] * padded == lanes
    row = lax.broadcasted_iota(jnp.int32, (16, lanes_used), 0)
    for g in range(groups):
        values = jnp.where(match, grad_gate[g * padded : (g + 1) * padded], 0.0)
        line = jnp.sum(values, axis=0, keepdims=True)
        high = line.astype(bf16).astype(f32)
        tail = grad_out[(g + 1) * padded - 16 : (g + 1) * padded, :lanes_used]
        tail = jnp.where(row == spare, high, jnp.where(row == spare + 1, line - high, tail))
        grad_ref[pl.ds((g + 1) * padded - 16, 16), :lanes_used] = tail.astype(bf16)


def expert_pass(facts, slots, grads, own, other, capacity, padded, lanes_used):
    rows, width = slots.shape
    units = own[0].shape[1]
    chunks = 1 if other is None else 2
    sources = list(own) + ([] if other is None else [other] * 3)
    tile = rows
    cut = lambda size: pl.BlockSpec((tile, size), lambda i, f: (i, 0))
    outs = pl.pallas_call(
        partial(expert_kernel, chunks, capacity, padded, lanes_used),
        grid_spec=pltpu.PrefetchScalarGridSpec(
            num_scalar_prefetch=1,
            grid=(rows // tile,),
            in_specs=[cut(width)] * 2 + [pl.BlockSpec(memory_space=pl.ANY)] * (3 * chunks),
            out_specs=[cut(units)] * (3 * chunks) + [cut(width)] * 2,
            scratch_shapes=[pltpu.VMEM((units, width), bf16)] * (3 * chunks)
            + [pltpu.SemaphoreType.DMA((3 * chunks,))],
        ),
        out_shape=[jax.ShapeDtypeStruct((rows, units), bf16)] * (3 * chunks)
        + [jax.ShapeDtypeStruct((rows, width), bf16)] * 2,
        compiler_params=params(),
        cost_estimate=cost(18),
        name="expert_pass",
    )(facts, slots, grads, *sources)
    middles = [outs[3 * c : 3 * c + 3] for c in range(chunks)]
    return middles, outs[3 * chunks], outs[3 * chunks + 1]


def weight_body(count, packed, extra, facts, *refs):
    kinds = [refs[k * count : (k + 1) * count] for k in range(5)]
    outs = refs[5 * count + extra :]
    targets = outs[1:4] if packed else outs[:3]
    held, sems = refs[-6:-1], refs[-1]
    step = pl.program_id(0)
    slot = step % 2

    def fetch(index, side):
        for r in range(count):

            @pl.when(index == r)
            def _():
                for k in range(5):
                    pltpu.make_async_copy(kinds[k][r], held[k].at[side], sems.at[side, k]).start()

    @pl.when(step == 0)
    def _():
        fetch(step, slot)

    @pl.when(step + 1 < count)
    def _():
        fetch(step + 1, 1 - slot)

    for k in range(5):
        pltpu.make_async_copy(kinds[k][0], held[k].at[slot], sems.at[slot, k]).wait()

    @pl.when(step == 0)
    def _():
        for target in targets:
            target[...] = jnp.zeros_like(target)

    rows, grads = held[0][slot], held[1][slot]
    lefts = ((held[3], rows), (held[4], rows), (held[2], grads))
    for target, (left, right) in zip(targets, lefts):
        target[0] += mm(left[slot], right, TN)

    if packed:

        @pl.when(step == count - 1)
        def _():
            for i in range(3):
                outs[0][i] = targets[i][0].astype(bf16)


def weight_pass(facts, slots, grads, middles, before, local, packed):
    count = len(slots)
    rows, width = slots[0].shape
    units = middles[0][0].shape[1]
    anywhere = pl.BlockSpec(memory_space=pl.ANY)
    if packed:
        out_specs = [pl.BlockSpec((3, units, width), lambda i, f: (0, 0, 0))]
        out_shape = [jax.ShapeDtypeStruct((3, units, width), bf16)]
        totals = [pltpu.VMEM((1, units, width), f32)] * 3
    else:
        out_specs = [pl.BlockSpec((1, units, width), lambda i, f: (f[4], 0, 0))] * 3
        out_shape = [jax.ShapeDtypeStruct((local, units, width), f32)] * 3
        totals = []
    kinds = [list(slots), list(grads)] + [[middle[k] for middle in middles] for k in range(3)]
    body = partial(weight_body, count, packed, len(before))
    return pl.pallas_call(
        body,
        grid_spec=pltpu.PrefetchScalarGridSpec(
            num_scalar_prefetch=1,
            grid=(count,),
            in_specs=[anywhere] * (5 * count + len(before)),
            out_specs=out_specs,
            scratch_shapes=totals
            + [pltpu.VMEM((2, rows, width), bf16)] * 2
            + [pltpu.VMEM((2, rows, units), bf16)] * 3
            + [pltpu.SemaphoreType.DMA((2, 5))],
        ),
        out_shape=out_shape,
        input_output_aliases={1 + 5 * count + i: i for i in range(len(before))},
        compiler_params=params(),
        cost_estimate=cost(16),
        name="weight_pass",
    )(facts, *[array for kind in kinds for array in kind], *before)


def fill_kernel(facts, source, *refs):
    for i in range(3):
        refs[-3 + i][0] = source[i].astype(f32)


def weight_fill(facts, source, before):
    _, units, width = source.shape
    tile = units // 4
    anywhere = pl.BlockSpec(memory_space=pl.ANY)
    return pl.pallas_call(
        fill_kernel,
        grid_spec=pltpu.PrefetchScalarGridSpec(
            num_scalar_prefetch=1,
            grid=(4,),
            in_specs=[pl.BlockSpec((3, tile, width), lambda i, f: (0, i, 0))] + [anywhere] * 3,
            out_specs=[pl.BlockSpec((1, tile, width), lambda i, f: (f[6], i, 0))] * 3,
        ),
        out_shape=[jax.ShapeDtypeStruct(array.shape, f32) for array in before],
        input_output_aliases={2 + i: i for i in range(3)},
        compiler_params=params(),
        cost_estimate=cost(6.5),
        name="weight_fill",
    )(facts, source, *before)


def place_kernel(capacity, padded, block, local, turns, routes, rows, slots_out, wide_out, rows_out):
    experts_axis = block // padded
    tokens = rows.shape[0]
    experts = experts_axis * local
    number = lax.broadcasted_iota(jnp.int32, (experts, tokens), 0)
    picks = [number == routes[k : k + 1] for k in range(routes.shape[0])]
    named = picks[0]
    for pick in picks[1:]:
        named = named | pick
    earlier = lax.broadcasted_iota(jnp.int32, (tokens, tokens), 0) < lax.broadcasted_iota(
        jnp.int32, (tokens, tokens), 1
    )
    before = mm(named.astype(bf16), earlier.astype(bf16))
    places = []
    for k, pick in enumerate(picks):
        route = routes[k : k + 1]
        position = jnp.sum(jnp.where(pick, before, 0.0), axis=0, keepdims=True).astype(jnp.int32)
        owner = route // local
        turn = jnp.where(owner % 2 == 0, turns[:, 0:1], turns[:, 1:2])
        which = (route % local) ^ turn
        slot = which * block + owner * padded + position
        slots_out[k : k + 1] = jnp.where(position < capacity, slot, -1)
        slot = (owner * local + which) * padded + position
        places.append(jnp.where(position < capacity, slot, -1))
        wide_out[k : k + 1] = places[k]
    spots = lax.broadcasted_iota(jnp.int32, (local * block, tokens), 0)
    hot = spots == places[0]
    for slot in places[1:]:
        hot = hot | (spots == slot)
    rows_out[...] = mm(hot.astype(bf16), rows[...]).astype(bf16)


def place_rows(turns, routes, rows, capacity, padded, block, local):
    tops, tokens = routes.shape
    width = rows.shape[1]
    return pl.pallas_call(
        partial(place_kernel, capacity, padded, block, local),
        out_shape=[
            jax.ShapeDtypeStruct((tops, tokens), jnp.int32),
            jax.ShapeDtypeStruct((tops, tokens), jnp.int32),
            jax.ShapeDtypeStruct((local * block, width), bf16),
        ],
        compiler_params=pltpu.CompilerParams(vmem_limit_bytes=VMEM_BYTES),
        cost_estimate=cost(3.9),
        name="place_rows",
    )(turns, routes, rows)


def route_kernel(
    capacity, padded, mixed, w_proj, inputs, gain, router, routes, slots, resid, moe, probs, gates, *outs
):
    local, block = len(outs), outs[0].shape[0]
    tokens = inputs.shape[0]
    sums = inputs[...].astype(f32) + mm(mixed[...], w_proj[...])
    resid[...] = sums
    scale = lax.rsqrt(jnp.mean(sums * sums, axis=-1, keepdims=True) + 1e-06)
    low = (sums * scale * gain[...].astype(f32)).astype(bf16)
    moe[...] = low
    logits = mm(router[...], low, NT)
    grown = jnp.exp(logits - jnp.max(logits, axis=0, keepdims=True))
    share = grown / jnp.sum(grown, axis=0, keepdims=True)
    probs[...] = share
    number = lax.broadcasted_iota(jnp.int32, share.shape, 0)
    spots = lax.broadcasted_iota(jnp.int32, (local * block, tokens), 0)
    row = lax.broadcasted_iota(jnp.int32, (16, tokens), 0)
    hot = None
    lines = jnp.zeros((16, local * block), f32)
    for k in range(routes.shape[0]):
        gate = jnp.sum(jnp.where(number == routes[k : k + 1], share, 0.0), axis=0, keepdims=True)
        gates[k : k + 1] = gate
        high = gate.astype(bf16).astype(f32)
        both = jnp.where(row == 0, high, jnp.where(row == 1, gate - high, 0.0)).astype(bf16)
        mine = (spots == slots[k : k + 1]).astype(bf16)
        lines = lines + mm(both, mine, NT)
        hot = mine if hot is None else hot + mine
    filled = mm(hot, low).astype(bf16)
    spare = 16 - (padded - capacity)
    row = lax.broadcasted_iota(jnp.int32, (16, padded), 0)
    for j in range(local):
        outs[j][...] = filled[j * block : (j + 1) * block]
        for g in range(block // padded):
            at = j * block + g * padded
            tail = filled[at + padded - 16 : at + padded, :padded].astype(f32)
            line = lines[:, at : at + padded]
            tail = jnp.where(row == spare, line[0:1], jnp.where(row == spare + 1, line[1:2], tail))
            outs[j][pl.ds((g + 1) * padded - 16, 16), :padded] = tail.astype(bf16)


def route_rows(mixed, w_proj, inputs, gain, router, routes, slots, capacity, padded, block, local):
    tokens, width = inputs.shape
    tops = routes.shape[0]
    return pl.pallas_call(
        partial(route_kernel, capacity, padded),
        out_shape=[
            jax.ShapeDtypeStruct((tokens, width), f32),
            jax.ShapeDtypeStruct((tokens, width), bf16),
            jax.ShapeDtypeStruct((router.shape[0], tokens), f32),
            jax.ShapeDtypeStruct((tops, tokens), f32),
        ]
        + [jax.ShapeDtypeStruct((block, width), bf16)] * local,
        compiler_params=pltpu.CompilerParams(vmem_limit_bytes=VMEM_BYTES),
        cost_estimate=cost(6.4),
        name="route_rows",
    )(mixed, w_proj, inputs, gain.reshape(1, width), router, routes, slots)


def merge_kernel(
    capacity, padded, count, cotangent, resid, probs, moe, router, gain, w_proj, routes, slots, columns, *refs
):
    local = len(refs) - 5
    grads = refs[:local]
    grad_resid, grad_mixed, gain_grad, router_grad, branch_out = refs[local:]
    block = grads[0].shape[0]
    tokens = cotangent.shape[0]
    tops = routes.shape[0]
    spare = 16 - (padded - capacity)
    pieces = []
    for j in range(local):
        for g in range(block // padded):
            tail = grads[j][pl.ds((g + 1) * padded - 16, 16), : count * padded].astype(f32)
            line = tail[spare : spare + 1] + tail[spare + 1 : spare + 2]
            folded = line[:, :padded]
            for r in range(1, count):
                folded = folded + line[:, r * padded : (r + 1) * padded]
            pieces.append(folded)
    line = jnp.concatenate(pieces, axis=1)
    row = lax.broadcasted_iota(jnp.int32, (16, line.shape[1]), 0)
    high = line.astype(bf16).astype(f32)
    rest = line - high
    middle = rest.astype(bf16).astype(f32)
    stack = jnp.where(row == 0, high, jnp.where(row == 1, middle, jnp.where(row == 2, rest - middle, 0.0)))
    stack = stack.astype(bf16)
    share = probs[...]
    number = lax.broadcasted_iota(jnp.int32, share.shape, 0)
    spots = lax.broadcasted_iota(jnp.int32, (local * block, tokens), 0)
    grad_probs = jnp.zeros_like(share)
    for k in range(tops):
        picked = jnp.sum(mm(stack, (spots == slots[k : k + 1]).astype(bf16)), axis=0, keepdims=True)
        grad_probs = grad_probs + jnp.where(number == routes[k : k + 1], picked, 0.0)
    grad_logits = share * (grad_probs - jnp.sum(share * grad_probs, axis=0, keepdims=True))
    grad_logits = grad_logits.astype(bf16)
    router_grad[...] = mm(grad_logits, moe[...])
    grad_moe = mm(grad_logits, router[...], TN)
    spots = lax.broadcasted_iota(jnp.int32, (tokens, block), 1)
    for j in range(local):
        hot = None
        for k in range(tops):
            mine = spots + j * block == columns[:, k : k + 1]
            hot = mine if hot is None else hot | mine
        grad_moe = grad_moe + mm(hot.astype(bf16), grads[j][...])
    rows = resid[...]
    scale = lax.rsqrt(jnp.mean(rows * rows, axis=-1, keepdims=True) + 1e-06)
    normed = rows * scale
    gain_grad[...] = jnp.sum(grad_moe * normed, axis=0, keepdims=True)
    lifted = grad_moe * gain[...].astype(f32)
    spread = jnp.mean(lifted * normed, axis=-1, keepdims=True)
    back = cotangent[...].astype(f32) + scale * (lifted - normed * spread)
    grad_resid[...] = back
    branch = back.astype(bf16)
    grad_mixed[...] = mm(branch, w_proj[...], NT).astype(bf16)
    branch_out[...] = branch


def merge_rows(
    cotangent, resid, probs, moe, router, gain, w_proj, routes, slots, grads, capacity, padded, count
):
    tokens, width = cotangent.shape
    return pl.pallas_call(
        partial(merge_kernel, capacity, padded, count),
        out_shape=[
            jax.ShapeDtypeStruct((tokens, width), f32),
            jax.ShapeDtypeStruct((tokens, width), bf16),
            jax.ShapeDtypeStruct((1, width), f32),
            jax.ShapeDtypeStruct((router.shape[0], width), f32),
            jax.ShapeDtypeStruct((tokens, width), bf16),
        ],
        compiler_params=pltpu.CompilerParams(vmem_limit_bytes=VMEM_BYTES),
        cost_estimate=cost(7.4),
        name="merge_rows",
    )(
        cotangent, resid, probs, moe, router, gain.reshape(1, width), w_proj, routes, slots,
        jnp.transpose(slots), *grads,
    )


def blocks_kernel(
    local,
    facts,
    normed,
    normed_others,
    mixed,
    grad_query,
    grad_pair,
    grad_others,
    grad_near,
    branch,
    bias_grad,
    gain_grad,
    router_grad,
    near,
    far,
    near_right,
    far_right,
):
    step = pl.program_id(0)
    number = facts[3]
    group = step ^ (number // 8)
    share = (near.shape[1] - 8) // 4
    short = grad_near.shape[0] // 2
    own, own_short = normed[:local], normed[local:]

    def keyed(which):
        part = mm(own, grad_pair[which * local : (which + 1) * local], TN)
        part = part + mm(own_short, grad_near[which * short : (which + 1) * short], TN)
        for r in range(normed_others.shape[0] // local):
            at = (2 * r + which) * local
            part = part + mm(normed_others[r * local : (r + 1) * local], grad_others[at : at + local], TN)
        return part

    made = [mm(normed[...], grad_query[...], TN), keyed(0), keyed(1), mm(mixed[...], branch[...], TN)]
    made = [part.astype(bf16) for part in made]
    pairs, _, buckets = bias_grad.shape
    line = [bias_grad[p, h : h + 1, :] for p in range(pairs) for h in range(2)]
    line.append(jnp.zeros((1, 2 * near.shape[2] - 2 * pairs * buckets), f32))
    tail = jnp.zeros((24 - 2 - router_grad.shape[0], 2 * near.shape[2]), f32)
    small = jnp.concatenate(
        [jnp.concatenate(line, axis=1), gain_grad[...], router_grad[...], tail], axis=0
    )
    for s in range(8):
        spot = s ^ (number % 8)
        lines = [part[s * share : (s + 1) * share] for part in made]
        extra = jnp.zeros((8, 2 * near.shape[2]), f32)
        if s < 3:
            extra = jnp.where(group == 0, small[s * 8 : s * 8 + 8], extra)
        whole = jnp.concatenate(lines + [extra.astype(bf16)], axis=0)

        @pl.when(step < 2)
        def _():
            near[spot] = whole[:, : near.shape[2]]
            near_right[spot] = whole[:, near.shape[2] :]

        @pl.when(step >= 2)
        def _():
            far[spot] = whole[:, : near.shape[2]]
            far_right[spot] = whole[:, near.shape[2] :]


def weight_blocks(facts, lefts, rights, branch, bias_grad, gain_grad, router_grad, local):
    tokens, width = lefts[0].shape
    rows = 4 * width // 32 + 8
    cut = lambda count: pl.BlockSpec((count, width // 4), lambda i, f: (0, i ^ (f[3] // 8)))
    full = lambda count: pl.BlockSpec((count, width), lambda i, f: (0, 0))
    out = lambda which: pl.BlockSpec((8, rows, width // 2), which)
    return pl.pallas_call(
        partial(blocks_kernel, local),
        grid_spec=pltpu.PrefetchScalarGridSpec(
            num_scalar_prefetch=1,
            grid=(4,),
            in_specs=[cut(left.shape[0]) for left in lefts]
            + [full(right.shape[0]) for right in rights]
            + [
                full(tokens),
                pl.BlockSpec(bias_grad.shape, lambda i, f: (0, 0, 0)),
                full(1),
                full(router_grad.shape[0]),
            ],
            out_specs=[
                out(lambda i, f: (jnp.minimum(i, 1), 0, 0)),
                out(lambda i, f: (jnp.maximum(i - 2, 0), 0, 0)),
            ]
            * 2,
        ),
        out_shape=[jax.ShapeDtypeStruct((16, rows, width // 2), bf16)] * 4,
        compiler_params=params(),
        cost_estimate=cost(17),
        name="weight_blocks",
    )(facts, *lefts, *rights, branch, bias_grad, gain_grad, router_grad)


def unpack_kernel(facts, near, far, w_query, w_key, w_value, gain, *refs):
    query, key, value, proj, gain_grad, small = refs[-6:]
    step = pl.program_id(0)
    number = facts[3]
    group = step ^ (number // 8)
    share = (near.shape[1] - 8) // 4

    def spread(source):
        for s in range(8):
            block = source[s ^ (number % 8)].astype(f32)
            for which, out in enumerate((query, key, value, proj)):
                out[s * share : (s + 1) * share] = block[which * share : (which + 1) * share]
            if s < 3:

                @pl.when(group == 0)
                def _():
                    small[s * 8 : s * 8 + 8] = block[4 * share :]

    @pl.when(step < 2)
    def _():
        spread(near)

    @pl.when(step >= 2)
    def _():
        spread(far)

    sums = query[...] * w_query[...].astype(f32)
    sums = sums + key[...] * w_key[...].astype(f32)
    sums = sums + value[...] * w_value[...].astype(f32)
    column = jnp.sum(sums, axis=-1, keepdims=True)
    size = column.shape[0]
    match = lax.broadcasted_iota(jnp.int32, (size, size), 0) == lax.broadcasted_iota(
        jnp.int32, (size, size), 1
    )
    line = jnp.sum(jnp.where(match, column, 0.0), axis=0, keepdims=True)
    gain_grad[...] = line / gain[...].astype(f32)


def unpack_blocks(facts, near, far, w_query, w_key, w_value, gain, before, half):
    width = w_query.shape[0]
    wide = width // 2
    rows = near.shape[1]
    step = width // 4
    line = pl.BlockSpec((1, step), lambda i, f: (0, i ^ (f[3] // 8)))
    block = pl.BlockSpec((step, wide), lambda i, f: (i ^ (f[3] // 8), half))
    return pl.pallas_call(
        unpack_kernel,
        grid_spec=pltpu.PrefetchScalarGridSpec(
            num_scalar_prefetch=1,
            grid=(4,),
            in_specs=[
                pl.BlockSpec((8, rows, wide), lambda i, f: (jnp.minimum(i, 1), 0, 0)),
                pl.BlockSpec((8, rows, wide), lambda i, f: (jnp.maximum(i - 2, 0), 0, 0)),
                block,
                block,
                block,
                line,
            ]
            + [pl.BlockSpec(memory_space=pl.ANY)] * len(before),
            out_specs=[block, block, block, block, line, pl.BlockSpec((24, wide), lambda i, f: (0, 0))],
        ),
        out_shape=[jax.ShapeDtypeStruct((width, width), f32)] * 4
        + [jax.ShapeDtypeStruct((1, width), f32), jax.ShapeDtypeStruct((24, wide), f32)],
        input_output_aliases={7 + i: i for i in range(len(before))},
        compiler_params=params(),
        cost_estimate=cost(8),
        name="unpack_blocks",
    )(facts, near, far, w_query, w_key, w_value, gain.reshape(1, width), *before)


def per_device(
    inputs,
    attn_gain,
    w_query,
    w_key,
    w_value,
    w_proj,
    rel_bias,
    moe_gain,
    w_router,
    w_gate,
    w_up,
    w_down,
    routes,
    long_buckets,
    short_buckets,
    long_lens,
    short_lens,
    cotangent,
):
    experts_axis = lax.axis_size("expert")
    tensor_axis = lax.axis_size("tensor")
    place = lax.axis_index("tensor")
    tok_count, width = inputs.shape
    top_count = routes.shape[1]
    short_len = (short_buckets.shape[0] + 1) // 2
    long_span = (long_buckets.shape[0] + 1) // 2
    long_local = tok_count - short_len
    bucket_count, heads = rel_bias.shape
    head_dim = width // heads
    experts = w_router.shape[1]
    local = experts // experts_axis
    capacity = (5 * tok_count * top_count + 4 * experts - 1) // (4 * experts)
    padded = (capacity + 2 + 15) // 16 * 16
    block = experts_axis * padded
    rel_table = rel_bias.astype(f32)
    here = lax.axis_index("expert")
    number = (here % 2) * 16 + place * 4 + here // 2
    paired = tensor_axis == 4 and local == 2
    routes_rows = jnp.transpose(routes)
    router = jnp.transpose(w_router)
    gate_turned = jnp.swapaxes(w_gate, 1, 2)
    up_turned = jnp.swapaxes(w_up, 1, 2)
    if paired:
        turns = jnp.stack([place % 2, place // 2]).astype(jnp.int32)
        which = jnp.where(here % 2 == 0, turns[0], turns[1])
        part_of = jnp.where(here % 2 == 0, turns[1], turns[0])
        shares = 2
    else:
        turns = jnp.zeros((2,), jnp.int32)
        which, part_of, shares = jnp.int32(0), place, tensor_axis
    facts = [place, long_lens[0], short_lens[0], number, which, part_of, 1 - which]
    facts = jnp.stack([jnp.asarray(fact, jnp.int32) for fact in facts])

    def trade(rows, other):
        pairs = []
        for e in range(experts_axis):
            mask = (2 if e % 2 == 0 else 1) if other else (1 if e % 2 == 0 else 2)
            pairs += [(e * tensor_axis + t, e * tensor_axis + (t ^ mask)) for t in range(tensor_axis)]
        return lax.ppermute(rows, ("expert", "tensor"), pairs)

    long_rows = inputs[:long_local]
    sources = [swap(long_rows, "tensor", r) for r in range(1, tensor_axis)]
    slots, wide_slots, grad_slots_in = place_rows(
        turns.reshape(1, 2), routes_rows, cotangent, capacity, padded, block, local
    )
    normed_low, query, pair, near = project(
        after(inputs, sources), attn_gain, w_query, w_key, w_value, long_local
    )

    def by_expert(rows):
        split = rows.reshape(experts_axis, local, padded, width)
        return [split[:, j].reshape(block, width) for j in range(local)]

    def by_device(parts):
        split = [part.reshape(experts_axis, 1, padded, width) for part in parts]
        return jnp.concatenate(split, axis=1).reshape(local * block, width)

    grad_whole = over_experts(grad_slots_in)
    normed_others, others = project_others(sources, attn_gain, w_key, w_value, long_local)
    parts = (pair, others)
    if paired:
        other = jnp.stack(
            [
                lax.dynamic_index_in_dim(array, 1 - which, 0, keepdims=False)
                for array in (gate_turned, up_turned, w_down)
            ]
        )
        other = trade(after(other, sources), False)

    reach = long_span + long_local
    first = long_span - long_local - long_local * place
    long_table = jnp.pad(long_buckets, (0, 1), constant_values=-1)
    long_hot = table_hot(lax.dynamic_slice_in_dim(long_table, first, reach, 0), bucket_count)
    short_hot = table_hot(jnp.pad(short_buckets, (0, 1), constant_values=-1), bucket_count)
    spread = lambda hot: jnp.einsum(
        "cb,bh->hc", hot, rel_table, precision=precise, preferred_element_type=f32
    )
    mixed, far_attend, near_attend = attend_forward(
        facts, query, parts, near, spread(long_hot), spread(short_hot),
        tensor_axis, long_local, head_dim,
    )
    resid, moe_low, probs, gates, *slots_in = route_rows(
        mixed, w_proj, inputs, moe_gain, router, routes_rows, slots, capacity, padded, block, local
    )

    own = (gate_turned, up_turned, w_down)
    lanes_used = shares * padded
    if paired:

        run = lambda rows, grads: expert_pass(
            facts, rows, grads, own, other, capacity, padded, lanes_used
        )
        grad_arrived = by_expert(after(grad_whole, slots_in))
        grads_b = trade(grad_arrived[1], False)
        grads_d = trade(grads_b, True)
        rows_b = over_experts(slots_in[1])
        rows_a = over_experts(after(slots_in[0], rows_b))
        rows_b = trade(after(rows_b, grads_b), False)
        rows_d = trade(rows_b, True)
        grads_c = trade(after(grad_arrived[0], rows_d), True)
        pass_b = run(rows_b, grads_b)
        pass_d = run(after(rows_d, pass_b[1]), grads_d)
        rows_c = trade(after(rows_a, rows_d), True)
        pass_a = run(after(rows_a, pass_d[1], rows_c), grad_arrived[0])
        traded = add_low(pass_b[2], after(trade(pass_d[2], True), pass_a[1]))
        traded = trade(traded, False)
        pass_c = run(after(rows_c, pass_a[1]), grads_c)
        traded = after(traded, pass_c[1])
        traded_back = over_experts(traded)
        kept = add_low(pass_a[2], trade(after(pass_c[2], traded), True))
        grad_slots = [over_experts(after(kept, traded_back)), traded_back]

        passes = [pass_a, pass_c, pass_b, pass_d]
        slot_blocks = [rows_a, rows_c, rows_b, rows_d]
        grad_blocks = [grad_arrived[0], grads_c, grads_b, grads_d]
        (sent,) = weight_pass(
            facts, slot_blocks, grad_blocks, [after_all(made[0][1], pass_c[1]) for made in passes], (), local, True
        )
        weight_grads = weight_pass(
            facts, slot_blocks, grad_blocks, [after_all(made[0][0], sent) for made in passes], (), local, False
        )
        outs_d = trade(after(pass_d[1], traded), True)
        outs_c = trade(after(pass_c[1], kept, outs_d), True)
        outs_traded = trade(add_low(pass_b[1], outs_d), False)
        outs_kept = add_low(pass_a[1], outs_c)
        grad_slots[0] = after(grad_slots[0], weight_grads, outs_c, outs_traded)
        held_back = outs_traded
        sent = trade(after(sent, outs_traded), False)
        outs_back = over_experts(after(by_device([outs_kept, outs_traded]), grad_slots[0]))
    else:
        grad_blocks = [gather_parts(rows) for rows in by_expert(grad_whole)]
        slot_blocks = [gather_parts(over_experts(slots_in[j])) for j in range(local)]
        weight_grads, passes = (), []
        for j in range(local):
            facts_j = facts.at[4].set(j)
            passes.append(
                [
                    expert_pass(facts_j, rows, grads, own, None, capacity, padded, lanes_used)
                    for rows, grads in zip(slot_blocks[j], grad_blocks[j])
                ]
            )
            weight_grads = weight_pass(
                facts_j, slot_blocks[j], grad_blocks[j], [made[0][0] for made in passes[j]], weight_grads, local, False
            )
        send_back = lambda which: [
            over_experts(sum_parts([made[which] for made in passes[j]]).astype(bf16)) for j in range(local)
        ]
        grad_slots = send_back(2)
        outs_back = by_device(send_back(1))
        held_back = sent = grad_slots[0]

    grad_resid, grad_mixed, moe_gain_grad, router_grad, branch = merge_rows(
        cotangent, resid, probs, moe_low, router, moe_gain, w_proj, routes_rows, slots, grad_slots,
        capacity, padded, shares,
    )
    grad_mixed = after(grad_mixed, held_back)
    quick = experts_axis == 8 and tensor_axis == 4
    hots = (long_hot.astype(bf16), short_hot.astype(bf16))
    *attn_grads, bias_grad = attend_backward(
        facts, query, grad_mixed, parts, near, (far_attend, near_attend), hots, tensor_axis, long_local, head_dim
    )
    if quick:
        bias_grad = after(bias_grad, sent)
        made = weight_blocks(
            facts, (normed_low, normed_others, mixed), attn_grads, branch, bias_grad, moe_gain_grad, router_grad,
            long_local,
        )
        sums = [add_low(made[half], swap(made[half + 1], "expert", 1)) for half in (0, 2)]
        attn_grads = after_all(attn_grads, sums, outs_back)
    own_grads, near_grads, away = normed_grads(attn_grads, w_query, w_key, w_value, long_local, tensor_axis)
    if quick:
        sums = [ring_sum(plane_parts(part), in_plane).astype(bf16) for part in sums]
        away = after(away, sums)
    pieces = [own_grads] + [
        away[r * long_local : (r + 1) * long_local].astype(bf16) for r in range(tensor_axis - 1)
    ]
    if tensor_axis == 4:
        pieces = pieces[:3] + [pieces[3][: long_local // 2], pieces[3][long_local // 2 :]]
    summed = sum_parts(pieces)
    if quick:
        owns = [sum_depth(part) for part in sums]
        sums = [spread_depth(own) for own in owns]
        sent, outs_back, summed = after_all((sent, outs_back, summed), sums[0], owns[1])
        sums[1] = after(sums[1], summed)
    if paired:
        weight_grads = weight_fill(facts, sent, weight_grads)
    slot_places = jnp.arange(local * block, dtype=jnp.int32)
    outputs = resid
    for k in range(top_count):
        chosen = mm((wide_slots[k][:, None] == slot_places).astype(bf16), outs_back)
        outputs = outputs + gates[k][:, None] * chosen
    outputs = outputs.astype(bf16)
    grad_normed = jnp.concatenate([summed, near_grads], axis=0)
    inputs_wide = inputs.astype(f32)
    scale = lax.rsqrt(jnp.mean(inputs_wide * inputs_wide, axis=-1, keepdims=True) + 1e-06)
    normed = inputs_wide * scale
    lifted = grad_normed * attn_gain.astype(f32)
    inputs_grad = grad_resid + scale * (
        lifted - normed * jnp.mean(lifted * normed, axis=-1, keepdims=True)
    )
    if quick:
        unpack = partial(unpack_blocks, facts)
        weights = (w_query, w_key, w_value, attn_gain)
        one, two = sums
        by_x, by_y = in_plane(one, 0), in_plane(one, 1)
        half_x, half_y = after_all((by_x[:2], by_y[2:]), outputs, weight_grads, two)
        one = jnp.concatenate([one, by_x, by_y, in_plane(half_x, 1), in_plane(half_y, 0)], axis=0)
        first = unpack(one, swap(one, "expert", 1), *weights, (), 0)
        by_x, by_y = in_plane(two, 0), in_plane(two, 1)
        rest = after_all((in_plane(by_x[:2], 1), in_plane(by_y[2:], 0)), first[5], inputs_grad)
        two = jnp.concatenate([two, by_x, by_y] + rest, axis=0)
        second = unpack(two, swap(two, "expert", 1), *weights, first[:4], 1)
        query_grad, key_grad, value_grad, proj_grad = second[:4]
        attn_gain_grad = (first[4] + second[4])[0]
        small = jnp.concatenate([first[5], second[5]], axis=1)
    else:
        key_others = [slice(2 * r * long_local, (2 * r + 1) * long_local) for r in range(tensor_axis - 1)]
        value_others = [slice((2 * r + 1) * long_local, (2 * r + 2) * long_local) for r in range(tensor_axis - 1)]

        def keyed(index, spots):
            short = slice(index * short_len, (index + 1) * short_len)
            rows = slice(index * long_local, (index + 1) * long_local)
            lefts = jnp.concatenate([normed_low, normed_others], axis=0)
            rights = jnp.concatenate(
                [attn_grads[1][rows], attn_grads[3][short]] + [attn_grads[2][spot] for spot in spots], axis=0
            )
            return mm(lefts, rights, TN)

        rel_row = jnp.pad(bias_grad.reshape(1, -1), ((0, 0), (0, width - bias_grad.size)))
        small = jnp.concatenate([rel_row, moe_gain_grad, router_grad], axis=0)
        query_grad, key_grad, value_grad, proj_grad, small = lax.psum(
            (
                mm(normed_low, attn_grads[0], TN),
                keyed(0, key_others),
                keyed(1, value_others),
                mm(mixed, branch, TN),
                small,
            ),
            ("expert", "tensor"),
        )
        attn_gain_grad = jnp.sum(
            query_grad * w_query.astype(f32) + key_grad * w_key.astype(f32) + value_grad * w_value.astype(f32),
            axis=1,
        ) / attn_gain.astype(f32)
    rel_grad = jnp.transpose(small[0, : heads * bucket_count].reshape(heads, bucket_count))
    return (
        outputs,
        inputs_grad,
        attn_gain_grad,
        query_grad,
        key_grad,
        value_grad,
        proj_grad,
        rel_grad,
        small[1],
        jnp.transpose(small[2 : 2 + experts]),
        jnp.swapaxes(weight_grads[0], 1, 2),
        jnp.swapaxes(weight_grads[1], 1, 2),
        weight_grads[2],
    )


def solution(mesh):
    return jax.shard_map(
        per_device,
        mesh=mesh,
        in_specs=(
            P(("expert", "tensor"), None),
            P(),
            P(),
            P(),
            P(),
            P(),
            P(),
            P(),
            P(),
            P("expert", None, "tensor"),
            P("expert", None, "tensor"),
            P("expert", "tensor", None),
            P(("expert", "tensor"), None),
            P(),
            P(),
            P("expert"),
            P(("expert", "tensor")),
            P(("expert", "tensor"), None),
        ),
        out_specs=(
            P(("expert", "tensor"), None),
            P(("expert", "tensor"), None),
            P(),
            P(),
            P(),
            P(),
            P(),
            P(),
            P(),
            P(),
            P("expert", None, "tensor"),
            P("expert", None, "tensor"),
            P("expert", "tensor", None),
        ),
        check_vma=False,
    )
```

```python
from functools import partial
import math

import jax
import jax.numpy as jnp
from jax import lax
from jax.experimental import pallas as pl
from jax.experimental.pallas import tpu as pltpu
from jax.sharding import PartitionSpec as P

precise = lax.Precision.HIGHEST
bf16 = jnp.bfloat16
f32 = jnp.float32
NT = (((1,), (1,)), ((), ()))
NN = (((1,), (0,)), ((), ()))
TN = (((0,), (0,)), ((), ()))
VMEM_BYTES = 56 * 1024 * 1024


def mm(left, right, dims=NN):
    return lax.dot_general(left, right, dims, preferred_element_type=f32)


def params():
    return pltpu.CompilerParams(
        dimension_semantics=("arbitrary",), vmem_limit_bytes=VMEM_BYTES
    )


def cost(micros):
    return pl.CostEstimate(flops=int(micros * 1.15e9), bytes_accessed=0, transcendentals=0)


def table_hot(table, count):
    return (table[:, None] == jnp.arange(count, dtype=jnp.int32)[None, :]).astype(f32)


def swap(rows, axis, mask):
    count = lax.axis_size(axis)
    return lax.ppermute(rows, axis, [(i, i ^ mask) for i in range(count)])


def after(value, *others):
    return lax.optimization_barrier((value,) + tuple(jax.tree.leaves(others)))[0]


def after_all(values, *others):
    leaves = tuple(jax.tree.leaves(others))
    return list(lax.optimization_barrier(tuple(values) + leaves)[: len(values)])


def ring_gather(rows, move):
    half = rows.shape[0] // 2
    first, second = move(rows, 0), move(rows, 1)
    return [rows, first, second, move(first[:half], 1), move(second[half:], 0)]


def ring_sum_first(parts, move):
    half = parts[3].shape[0]
    left = move(parts[3], 0)
    right = move(parts[4], 1)
    to_second = jnp.concatenate([add_low(parts[2][:half], left), parts[2][half:]], axis=0)
    to_first = jnp.concatenate([parts[1][:half], add_low(parts[1][half:], right)], axis=0)
    return parts[0], to_first, to_second


def ring_sum_second(own, to_first, to_second, move):
    first = move(to_first, 0)
    second = move(to_second, 1)
    return own.astype(f32) + first.astype(f32) + second.astype(f32)


def ring_sum(parts, move):
    return ring_sum_second(*ring_sum_first(parts, move), move)


def in_plane(rows, way):
    return swap(rows, "tensor", 1 + way)


def gather_parts(rows):
    count = lax.axis_size("tensor")
    if count == 4:
        return ring_gather(rows, in_plane)
    return [rows] + [swap(rows, "tensor", r) for r in range(1, count)]


def sum_parts(parts):
    count = lax.axis_size("tensor")
    if count == 4:
        return ring_sum(parts, in_plane)
    arrived = [swap(parts[r], "tensor", r) for r in range(1, count)]
    return sum([part.astype(f32) for part in arrived], parts[0].astype(f32))


def over_experts(rows):
    experts_axis = lax.axis_size("expert")
    blocks = rows.reshape(experts_axis, rows.shape[0] // experts_axis, rows.shape[1])
    return lax.all_to_all(blocks, "expert", 0, 0, tiled=True).reshape(rows.shape)


def add_low(left, right):
    return (left.astype(f32) + right.astype(f32)).astype(bf16)


def sum_cores(near, far):
    return add_low(near, swap(far, "expert", 1))


def plane_parts(rest):
    return [rest[0:4], rest[4:8], rest[8:12], rest[12:14], rest[14:16]]


def sum_depth(rest):
    arrived = swap(rest[1::2], "expert", 2)
    own, opposite = add_low(rest[0], arrived[0]), add_low(rest[2], arrived[1])
    return add_low(own, swap(opposite, "expert", 4))


def spread_depth(own):
    opposite = swap(own, "expert", 4)
    arrived = swap(jnp.stack([own, opposite]), "expert", 2)
    return jnp.stack([own, arrived[0], opposite, arrived[1]])


def spread_plane(rest):
    return jnp.concatenate(ring_gather(rest, in_plane), axis=0)


def project_kernel(
    local, gain, w_query, w_key, w_value, inputs, *refs
):
    sources, (normed, normed_others, query, pair, others, near, held) = refs[:-7], refs[-7:]
    tokens = inputs.shape[0]

    @pl.when(pl.program_id(0) == 0)
    def _():
        rows = jnp.concatenate([inputs[...]] + [source[...] for source in sources], axis=0).astype(f32)
        scale = lax.rsqrt(jnp.mean(rows * rows, axis=-1, keepdims=True) + 1e-06)
        held[...] = (rows * scale * gain[...].astype(f32)).astype(bf16)
        normed[...] = held[:tokens]
        normed_others[...] = held[tokens:]

    query[...] = mm(held[:tokens], w_query[...]).astype(bf16)
    keys = mm(held[...], w_key[...]).astype(bf16)
    values = mm(held[...], w_value[...]).astype(bf16)
    pair[:local] = keys[:local]
    pair[local:] = values[:local]
    short = tokens - local
    near[:short] = keys[local:tokens]
    near[short:] = values[local:tokens]
    for r in range((held.shape[0] - tokens) // local):
        low = tokens + r * local
        others[2 * r * local : (2 * r + 1) * local] = keys[low : low + local]
        others[(2 * r + 1) * local : (2 * r + 2) * local] = values[low : low + local]


def project(inputs, sources, gain, w_query, w_key, w_value, local):
    tokens, width = inputs.shape
    away = sum(source.shape[0] for source in sources)
    short = tokens - local
    step = 256
    whole = lambda count: pl.BlockSpec((count, width), lambda i: (0, 0))
    cut = lambda count: pl.BlockSpec((count, step), lambda i: (0, i))
    return pl.pallas_call(
        partial(project_kernel, local),
        grid=(width // step,),
        in_specs=[whole(1), cut(width), cut(width), cut(width), whole(tokens)]
        + [whole(source.shape[0]) for source in sources],
        out_specs=[whole(tokens), whole(away), cut(tokens), cut(2 * local), cut(2 * away), cut(2 * short)],
        out_shape=[
            jax.ShapeDtypeStruct((size, width), bf16)
            for size in (tokens, away, tokens, 2 * local, 2 * away, 2 * short)
        ],
        scratch_shapes=[pltpu.VMEM((tokens + away, width), bf16)],
        compiler_params=params(),
        cost_estimate=cost(12),
        name="project",
    )(gain.reshape(1, width), w_query, w_key, w_value, inputs, *sources)


def key_value_views(pair, others, count, rows):
    views = [(pair, slice(0, rows), pair, slice(rows, 2 * rows))]
    for r in range(count - 1):
        at = 2 * r * rows
        views.append((others, slice(at, at + rows), others, slice(at + rows, at + 2 * rows)))
    return views


def own_lanes(head, dim, shape, axis):
    place = lax.broadcasted_iota(jnp.int32, shape, axis)
    return (place >= head * dim) & (place < (head + 1) * dim)


def forward_kernel(
    count,
    rows,
    dim,
    facts,
    query,
    pair,
    others,
    near,
    far_bias,
    near_bias,
    mixed,
    far_attend,
    near_attend,
    window,
    scores,
):
    place, far_len, near_len = facts[0], facts[1], facts[2]
    scale = 1.0 / math.sqrt(dim)
    views = key_value_views(pair, others, count, rows)
    short = near.shape[0] // 2
    band, reach = window.shape[1:]
    low = (query[...].astype(f32) * scale).astype(bf16)
    starts = [(place ^ r) * rows for r in range(count)]
    spot = lax.broadcasted_iota(jnp.int32, (1, rows), 1)
    kept = [start + spot < far_len for start in starts]
    near_kept = lax.broadcasted_iota(jnp.int32, (1, short), 1) < near_len
    line = 2 * (pl.program_id(0) % 4)
    mine = [jnp.where(own_lanes(head, dim, low.shape, 1), low, jnp.zeros_like(low)) for head in range(2)]
    far_mine = jnp.concatenate([part[:rows] for part in mine], axis=0)
    near_parts = mm(jnp.concatenate([part[rows:] for part in mine], axis=0), near[:short], NT)
    near_parts = [near_parts[:short], near_parts[short:]]
    for r in range(count):
        part = mm(far_mine, views[r][0][views[r][1]], NT)
        for head in range(2):
            scores[head, :, r * rows : (r + 1) * rows] = part[head * rows : (head + 1) * rows]
    for head in range(2):
        table = jnp.broadcast_to(far_bias[pl.ds(line + head, 1)], (band, reach))
        window[head] = pltpu.roll(table, reach - (band - 1), 1, stride=1, stride_axis=0)
    for head in range(2):
        table = jnp.broadcast_to(near_bias[pl.ds(line + head, 1)], (short, 2 * short))
        bias = pltpu.roll(table, short + 1, 1, stride=1, stride_axis=0)[:, :short]
        part = jnp.where(near_kept, near_parts[head] + bias, -1e30)
        part = jnp.exp(part - jnp.max(part, axis=-1, keepdims=True))
        near_attend[head] = (part * (1.0 / jnp.sum(part, axis=-1, keepdims=True))).astype(bf16)
        for at in range(0, rows, 32):
            shift = band * (rows // band - 1 - at // band)
            lines = slice(at % band, at % band + 32)
            parts = []
            for r in range(count):
                begin = pl.multiple_of(starts[r] + shift, 128)
                part = scores[head, at : at + 32, r * rows : (r + 1) * rows]
                part = part + window[head, lines, pl.ds(begin, rows)]
                parts.append(jnp.where(kept[r], part, -1e30))
            highest = parts[0]
            for part in parts[1:]:
                highest = jnp.maximum(highest, part)
            highest = jnp.max(highest, axis=-1, keepdims=True)
            parts = [jnp.exp(part - highest) for part in parts]
            whole = parts[0]
            for part in parts[1:]:
                whole = whole + part
            inverse = 1.0 / jnp.sum(whole, axis=-1, keepdims=True)
            for r in range(count):
                far_attend[head, at : at + 32, r * rows : (r + 1) * rows] = (parts[r] * inverse).astype(bf16)
    out = jnp.zeros((2 * rows, 2 * dim), f32)
    for r in range(count):
        attend = far_attend[:, :, r * rows : (r + 1) * rows].reshape(2 * rows, rows)
        out = out + mm(attend, views[r][2][views[r][3]])
    near_out = mm(near_attend[...].reshape(2 * short, short), near[short:])
    second = own_lanes(1, dim, (rows, 2 * dim), 1)
    mixed[:rows] = jnp.where(second, out[rows:], out[:rows]).astype(bf16)
    second = own_lanes(1, dim, (short, 2 * dim), 1)
    mixed[rows:] = jnp.where(second, near_out[short:], near_out[:short]).astype(bf16)


def attention_specs(count, rows, short, reach, tokens):
    cut = lambda size: pl.BlockSpec((size, 128), lambda i, *_: (0, i))
    parts = [cut(2 * rows), cut(2 * (count - 1) * rows)]
    table = lambda size: pl.BlockSpec((8, size), lambda i, *_: (i // 4, 0))
    weights = lambda size, span: pl.BlockSpec((2, size, span), lambda i, *_: (i, 0, 0))
    return (
        cut(tokens),
        parts,
        cut(2 * short),
        [table(reach), table(2 * short)],
        [weights(rows, count * rows), weights(short, short)],
    )


def attend_forward(facts, query, parts, near, far_bias, near_bias, count, rows, dim):
    tokens, width = query.shape
    heads = width // dim
    short = near.shape[0] // 2
    reach = far_bias.shape[-1]
    cut, part_specs, near_spec, tables, weights = attention_specs(count, rows, short, reach, tokens)
    return pl.pallas_call(
        partial(forward_kernel, count, rows, dim),
        grid_spec=pltpu.PrefetchScalarGridSpec(
            num_scalar_prefetch=1,
            grid=(heads // 2,),
            in_specs=[cut] + part_specs + [near_spec] + tables,
            out_specs=[cut] + weights,
            scratch_shapes=[pltpu.VMEM((2, 128, reach), f32), pltpu.VMEM((2, rows, count * rows), f32)],
        ),
        out_shape=[
            jax.ShapeDtypeStruct((tokens, width), bf16),
            jax.ShapeDtypeStruct((heads, rows, count * rows), bf16),
            jax.ShapeDtypeStruct((heads, short, short), bf16),
        ],
        compiler_params=params(),
        cost_estimate=cost(17),
        name="attend_forward",
    )(facts, query, *parts, near, far_bias, near_bias)


def backward_kernel(
    count,
    rows,
    dim,
    facts,
    query,
    grad,
    pair,
    others,
    near,
    far_attend,
    near_attend,
    far_hot,
    near_hot,
    grad_query,
    grad_pair,
    grad_others,
    grad_near,
    bias_grad,
    window,
    near_window,
    products,
    scores,
    near_scores,
):
    place = facts[0]
    scale = 1.0 / math.sqrt(dim)
    views = key_value_views(pair, others, count, rows)
    grad_views = key_value_views(grad_pair, grad_others, count, rows)
    short = near.shape[0] // 2
    band = window.shape[1]
    starts = [(place ^ r) * rows for r in range(count)]

    @pl.when(pl.program_id(0) == 0)
    def _():
        near_window[...] = jnp.zeros_like(near_window)

    def reversal(size):
        up = lax.broadcasted_iota(jnp.int32, (size, size), 0)
        across = lax.broadcasted_iota(jnp.int32, (size, size), 1)
        return (up + across == size - 1).astype(bf16)

    far_turn = reversal(band)
    near_turn = far_turn if short == band else reversal(short)
    low, grad_low = query[...], grad[...]
    turned = jnp.transpose(low.astype(f32) * scale, (1, 0)).astype(bf16)
    grad_turned = jnp.transpose(grad_low.astype(f32), (1, 0)).astype(bf16)
    mine, grad_mine, grad_heads = [], [], []
    for head in range(2):
        lines = own_lanes(head, dim, turned.shape, 0)
        mine.append(jnp.where(lines, turned, jnp.zeros_like(turned)))
        grad_mine.append(jnp.where(lines, grad_turned, jnp.zeros_like(turned)))
        lanes = own_lanes(head, dim, low.shape, 1)
        grad_heads.append(jnp.where(lanes, grad_low, jnp.zeros_like(grad_low)))
    far_grads = jnp.concatenate([part[:rows] for part in grad_heads], axis=0)
    near_parts = mm(jnp.concatenate([part[rows:] for part in grad_heads], axis=0), near[short:], NT)
    for r in range(count):
        part = mm(far_grads, views[r][2][views[r][3]], NT)
        for head in range(2):
            products[head, :, r * rows : (r + 1) * rows] = part[head * rows : (head + 1) * rows]
    window[...] = jnp.zeros_like(window)
    for head in range(2):
        wide = near_attend[head].astype(f32)
        part = near_parts[head * short : (head + 1) * short]
        part = wide * (part - jnp.sum(wide * part, axis=-1, keepdims=True))
        near_scores[head] = part.astype(bf16)
        for at in range(0, rows, 32):
            attend = far_attend[head, at : at + 32].astype(f32)
            part = products[head, at : at + 32]
            inner = jnp.sum(attend * part, axis=-1, keepdims=True)
            scores[head, at : at + 32] = (attend * (part - inner)).astype(bf16)
    out = jnp.zeros((2 * rows, 2 * dim), f32)
    for r in range(count):
        part = scores[:, :, r * rows : (r + 1) * rows].reshape(2 * rows, rows)
        out = out + mm(part, views[r][0][views[r][1]])
        for head in range(2):
            for h in range(rows // band):
                begin = pl.multiple_of(starts[r] + band * (rows // band - 1 - h), 128)
                lines = slice(head * rows + h * band, head * rows + (h + 1) * band)
                window[head, :, pl.ds(begin, rows)] += mm(far_turn, part[lines])
    near_out = mm(near_scores[...].reshape(2 * short, short), near[:short])
    second = own_lanes(1, dim, (rows, 2 * dim), 1)
    grad_query[:rows] = (jnp.where(second, out[rows:], out[:rows]) * scale).astype(bf16)
    second = own_lanes(1, dim, (short, 2 * dim), 1)
    grad_query[rows:] = (jnp.where(second, near_out[short:], near_out[:short]) * scale).astype(bf16)
    def by_bucket(lines, hot):
        row = lax.broadcasted_iota(jnp.int32, (16, lines.shape[1]), 0)
        high = lines.astype(bf16).astype(f32)
        rest = lines - high
        middle = rest.astype(bf16).astype(f32)
        stack = jnp.where(row == 0, high, jnp.where(row == 1, middle, jnp.where(row == 2, rest - middle, 0.0)))
        return jnp.sum(mm(stack.astype(bf16), hot[...]), axis=0, keepdims=True)

    for head in range(2):
        rolled = pltpu.roll(window[head], 0, 1, stride=1, stride_axis=0)
        sums = by_bucket(jnp.sum(rolled, axis=0, keepdims=True), far_hot)
        near_window[head, :, :short] = mm(near_turn, near_scores[head])
        rolled = pltpu.roll(near_window[head], 0, 1, stride=1, stride_axis=0)
        sums = sums + by_bucket(jnp.sum(rolled, axis=0, keepdims=True), near_hot)
        bias_grad[0, head : head + 1, :] = sums
    for r in range(count):
        lanes = slice(r * rows, (r + 1) * rows)
        keys = mm(mine[0][:, :rows], scores[0, :, lanes]) + mm(mine[1][:, :rows], scores[1, :, lanes])
        values = mm(grad_mine[0][:, :rows], far_attend[0, :, lanes]) + mm(
            grad_mine[1][:, :rows], far_attend[1, :, lanes]
        )
        view = grad_views[r]
        view[0][view[1]] = jnp.transpose(keys, (1, 0)).astype(bf16)
        view[2][view[3]] = jnp.transpose(values, (1, 0)).astype(bf16)
    keys = mm(mine[0][:, rows:], near_scores[0]) + mm(mine[1][:, rows:], near_scores[1])
    values = mm(grad_mine[0][:, rows:], near_attend[0]) + mm(grad_mine[1][:, rows:], near_attend[1])
    grad_near[:short] = jnp.transpose(keys, (1, 0)).astype(bf16)
    grad_near[short:] = jnp.transpose(values, (1, 0)).astype(bf16)


def attend_backward(facts, query, grad, parts, near, weights, hots, count, rows, dim):
    tokens, width = query.shape
    pairs = width // dim // 2
    short = near.shape[0] // 2
    reach, buckets = hots[0].shape
    cut, part_specs, near_spec, _, weight_specs = attention_specs(count, rows, short, reach, tokens)
    return pl.pallas_call(
        partial(backward_kernel, count, rows, dim),
        grid_spec=pltpu.PrefetchScalarGridSpec(
            num_scalar_prefetch=1,
            grid=(pairs,),
            in_specs=[cut, cut]
            + part_specs
            + [near_spec]
            + weight_specs
            + [pl.BlockSpec(hot.shape, lambda i, *_: (0, 0)) for hot in hots],
            out_specs=[cut]
            + part_specs
            + [near_spec, pl.BlockSpec((1, 2, buckets), lambda i, *_: (i, 0, 0))],
            scratch_shapes=[
                pltpu.VMEM((2, 128, reach), f32),
                pltpu.VMEM((2, short, 2 * short), f32),
                pltpu.VMEM((2, rows, count * rows), f32),
                pltpu.VMEM((2, rows, count * rows), bf16),
                pltpu.VMEM((2, short, short), bf16),
            ],
        ),
        out_shape=[
            jax.ShapeDtypeStruct((size, width), bf16)
            for size in (tokens, 2 * rows, 2 * (count - 1) * rows, 2 * short)
        ]
        + [jax.ShapeDtypeStruct((pairs, 2, buckets), f32)],
        compiler_params=params(),
        cost_estimate=cost(25),
        name="attend_backward",
    )(facts, query, grad, *parts, near, *weights, *hots)


def normed_grads_kernel(local, count, query, pair, others, near, w_query, w_key, w_value, *outs):
    own, own_short, away = outs
    short = near.shape[0] // 2

    @pl.when(pl.program_id(0) == 0)
    def _():
        for out in outs:
            out[...] = jnp.zeros_like(out)

    full = mm(query[...], w_query[...], NT)
    own[...] += full[:local] + mm(pair[:local], w_key[...], NT) + mm(pair[local:], w_value[...], NT)
    own_short[...] += full[local:] + mm(near[:short], w_key[...], NT) + mm(near[short:], w_value[...], NT)
    for r in range(count - 1):
        at = 2 * r * local
        away[r * local : (r + 1) * local] += mm(others[at : at + local], w_key[...], NT) + mm(
            others[at + local : at + 2 * local], w_value[...], NT
        )


def normed_grads(grads, w_query, w_key, w_value, local, count):
    width = w_query.shape[0]
    short = grads[3].shape[0] // 2
    cut = lambda size: pl.BlockSpec((size, width // 2), lambda i: (0, i))
    sizes = (local, short, (count - 1) * local)
    return pl.pallas_call(
        partial(normed_grads_kernel, local, count),
        grid=(2,),
        in_specs=[cut(array.shape[0]) for array in grads] + [cut(width)] * 3,
        out_specs=[pl.BlockSpec((size, width), lambda i: (0, 0)) for size in sizes],
        out_shape=[jax.ShapeDtypeStruct((size, width), f32) for size in sizes],
        compiler_params=params(),
        cost_estimate=cost(13),
        name="normed_grads",
    )(*grads, w_query, w_key, w_value)


def pick_kernel(facts, *refs):
    for i in range(3):
        refs[3][i] = refs[i][0]


def pick_weights(facts, *weights):
    _, units, width = weights[0].shape
    tile = units // 4
    return pl.pallas_call(
        pick_kernel,
        grid_spec=pltpu.PrefetchScalarGridSpec(
            num_scalar_prefetch=1,
            grid=(4,),
            in_specs=[pl.BlockSpec((1, tile, width), lambda i, f: (f[6], i, 0))] * 3,
            out_specs=pl.BlockSpec((3, tile, width), lambda i, f: (0, i, 0)),
        ),
        out_shape=jax.ShapeDtypeStruct((3, units, width), bf16),
        compiler_params=params(),
        cost_estimate=cost(5),
        name="pick_weights",
    )(facts, *weights)


def expert_kernel(chunks, capacity, padded, lanes_used, facts, slots_in, grads_in, *refs):
    sources, rest = refs[: 3 * chunks], refs[3 * chunks :]
    outs, rest = rest[: 3 * chunks + 2], rest[3 * chunks + 2 :]
    rows_buffer, grads_buffer, held, middles, out_buffer, grad_buffer, in_sems, out_sems = rest
    rows = rows_buffer.shape[0]
    units = sources[0].shape[1]
    wide = held.shape[1] // chunks
    groups = rows // padded
    spare = 16 - (padded - capacity)

    arrivals = [
        pltpu.make_async_copy(slots_in, rows_buffer, in_sems.at[0]),
        pltpu.make_async_copy(grads_in, grads_buffer, in_sems.at[1]),
    ]
    weights = []
    for k in range(3):
        for c in range(chunks):
            i = 3 * c + k
            index = facts[4] if c == 0 else k
            place = held.at[k, pl.ds(c * wide, units)]
            weights.append(pltpu.make_async_copy(sources[i].at[index], place, in_sems.at[2 + i]))
    arrivals[0].start()
    for copy in weights[: 2 * chunks]:
        copy.start()
    arrivals[1].start()
    for copy in weights[2 * chunks :]:
        copy.start()
    if wide > units:
        for k in range(3):
            for c in range(chunks):
                held[k, c * wide + units : (c + 1) * wide] = jnp.zeros((wide - units, held.shape[2]), bf16)

    arrivals[0].wait()
    lanes = lax.broadcasted_iota(jnp.int32, (padded, 128), 1)
    match = lax.broadcasted_iota(jnp.int32, (padded, 128), 0) == lanes
    columns = []
    for g in range(groups):
        tail = rows_buffer[pl.ds((g + 1) * padded - 16, 16), :128].astype(f32)
        line = tail[spare : spare + 1] + tail[spare + 1 : spare + 2]
        columns.append(jnp.sum(jnp.where(match, line, 0.0), axis=-1, keepdims=True))
    gate_column = jnp.concatenate(columns, axis=0)

    slots = rows_buffer[...]
    for copy in weights[:chunks]:
        copy.wait()
    gate_pre = mm(slots, held[0], NT)
    for copy in weights[chunks : 2 * chunks]:
        copy.wait()
    up_pre = mm(slots, held[1], NT)
    arrivals[1].wait()
    for copy in weights[2 * chunks :]:
        copy.wait()
    grads = grads_buffer[...]
    grad_hidden = mm(grads, held[2], NT) * gate_column
    slope = math.sqrt(2.0 / math.pi)
    square = gate_pre * gate_pre
    curve = jnp.tanh(slope * gate_pre * (1.0 + 0.044715 * square))
    side = 0.5 * (1.0 + curve)
    bent = gate_pre * side
    hidden = bent * up_pre
    bent_slope = side + 0.5 * slope * gate_pre * (1.0 - curve * curve) * (
        1.0 + 3.0 * 0.044715 * square
    )
    gate_low = (grad_hidden * up_pre * bent_slope).astype(bf16)
    up_low = (grad_hidden * bent).astype(bf16)
    departures = []

    def depart(buffer, target):
        copy = pltpu.make_async_copy(buffer, target, out_sems.at[len(departures)])
        copy.start()
        departures.append(copy)

    for k, value in enumerate(((hidden * gate_column).astype(bf16), gate_low, up_low)):
        for c in range(chunks):
            middles[3 * c + k] = value[:, c * wide : c * wide + units]
            depart(middles.at[3 * c + k], outs[3 * c + k])
    out = mm(hidden.astype(bf16), held[2])
    out_buffer[...] = out.astype(bf16)
    depart(out_buffer, outs[3 * chunks])
    grad_out = mm(gate_low, held[0]) + mm(up_low, held[1])
    grad_buffer[...] = grad_out.astype(bf16)

    grad_gate = jnp.sum(out * grads.astype(f32), axis=-1, keepdims=True)
    lanes = lax.broadcasted_iota(jnp.int32, (padded, lanes_used), 1)
    up = lax.broadcasted_iota(jnp.int32, (padded, lanes_used), 0)
    match = up + facts[5] * padded == lanes
    row = lax.broadcasted_iota(jnp.int32, (16, lanes_used), 0)
    for g in range(groups):
        values = jnp.where(match, grad_gate[g * padded : (g + 1) * padded], 0.0)
        line = jnp.sum(values, axis=0, keepdims=True)
        high = line.astype(bf16).astype(f32)
        tail = grad_out[(g + 1) * padded - 16 : (g + 1) * padded, :lanes_used]
        tail = jnp.where(row == spare, high, jnp.where(row == spare + 1, line - high, tail))
        grad_buffer[pl.ds((g + 1) * padded - 16, 16), :lanes_used] = tail.astype(bf16)
    depart(grad_buffer, outs[3 * chunks + 1])
    for copy in departures:
        copy.wait()


def expert_pass(facts, slots, grads, own, other, capacity, padded, lanes_used):
    rows, width = slots.shape
    units = own[0].shape[1]
    wide = (units + 127) // 128 * 128
    chunks = 1 if other is None else 2
    sources = list(own) + ([] if other is None else [other] * 3)
    anywhere = pl.BlockSpec(memory_space=pl.ANY)
    outs = pl.pallas_call(
        partial(expert_kernel, chunks, capacity, padded, lanes_used),
        grid_spec=pltpu.PrefetchScalarGridSpec(
            num_scalar_prefetch=1,
            grid=(1,),
            in_specs=[anywhere] * (2 + 3 * chunks),
            out_specs=[anywhere] * (3 * chunks + 2),
            scratch_shapes=[pltpu.VMEM((rows, width), bf16)] * 2
            + [pltpu.VMEM((3, chunks * wide, width), bf16), pltpu.VMEM((3 * chunks, rows, units), bf16)]
            + [pltpu.VMEM((rows, width), bf16)] * 2
            + [pltpu.SemaphoreType.DMA((2 + 3 * chunks,)), pltpu.SemaphoreType.DMA((3 * chunks + 2,))],
        ),
        out_shape=[jax.ShapeDtypeStruct((rows, units), bf16)] * (3 * chunks)
        + [jax.ShapeDtypeStruct((rows, width), bf16)] * 2,
        compiler_params=params(),
        cost_estimate=cost(15),
        name="expert_pass",
    )(facts, slots, grads, *sources)
    middles = [outs[3 * c : 3 * c + 3] for c in range(chunks)]
    return middles, outs[3 * chunks], outs[3 * chunks + 1]


def weight_body(count, packed, extra, facts, *refs):
    kinds = [refs[k * count : (k + 1) * count] for k in range(5)]
    outs = refs[5 * count + extra :]
    targets = outs[1:4] if packed else outs[:3]
    held, sems = refs[-6:-1], refs[-1]
    step = pl.program_id(0)
    slot = step % 2

    def fetch(index, side):
        for r in range(count):

            @pl.when(index == r)
            def _():
                for k in range(5):
                    pltpu.make_async_copy(kinds[k][r], held[k].at[side], sems.at[side, k]).start()

    @pl.when(step == 0)
    def _():
        fetch(step, slot)

    @pl.when(step + 1 < count)
    def _():
        fetch(step + 1, 1 - slot)

    for k in range(5):
        pltpu.make_async_copy(kinds[k][0], held[k].at[slot], sems.at[slot, k]).wait()

    @pl.when(step == 0)
    def _():
        for target in targets:
            target[...] = jnp.zeros_like(target)

    rows, grads = held[0][slot], held[1][slot]
    lefts = ((held[3], rows), (held[4], rows), (held[2], grads))
    for target, (left, right) in zip(targets, lefts):
        target[0] += mm(left[slot], right, TN)

    if packed:

        @pl.when(step == count - 1)
        def _():
            for i in range(3):
                outs[0][i] = targets[i][0].astype(bf16)


def weight_pass(facts, slots, grads, middles, before, local, packed):
    count = len(slots)
    rows, width = slots[0].shape
    units = middles[0][0].shape[1]
    anywhere = pl.BlockSpec(memory_space=pl.ANY)
    if packed:
        out_specs = [pl.BlockSpec((3, units, width), lambda i, f: (0, 0, 0))]
        out_shape = [jax.ShapeDtypeStruct((3, units, width), bf16)]
        totals = [pltpu.VMEM((1, units, width), f32)] * 3
    else:
        out_specs = [pl.BlockSpec((1, units, width), lambda i, f: (f[4], 0, 0))] * 3
        out_shape = [jax.ShapeDtypeStruct((local, units, width), f32)] * 3
        totals = []
    kinds = [list(slots), list(grads)] + [[middle[k] for middle in middles] for k in range(3)]
    body = partial(weight_body, count, packed, len(before))
    return pl.pallas_call(
        body,
        grid_spec=pltpu.PrefetchScalarGridSpec(
            num_scalar_prefetch=1,
            grid=(count,),
            in_specs=[anywhere] * (5 * count + len(before)),
            out_specs=out_specs,
            scratch_shapes=totals
            + [pltpu.VMEM((2, rows, width), bf16)] * 2
            + [pltpu.VMEM((2, rows, units), bf16)] * 3
            + [pltpu.SemaphoreType.DMA((2, 5))],
        ),
        out_shape=out_shape,
        input_output_aliases={1 + 5 * count + i: i for i in range(len(before))},
        compiler_params=params(),
        cost_estimate=cost(16),
        name="weight_pass",
    )(facts, *[array for kind in kinds for array in kind], *before)


def fill_kernel(facts, source, *refs):
    for i in range(3):
        refs[-3 + i][0] = source[i].astype(f32)


def weight_fill(facts, source, before):
    _, units, width = source.shape
    tile = units // 4
    anywhere = pl.BlockSpec(memory_space=pl.ANY)
    return pl.pallas_call(
        fill_kernel,
        grid_spec=pltpu.PrefetchScalarGridSpec(
            num_scalar_prefetch=1,
            grid=(4,),
            in_specs=[pl.BlockSpec((3, tile, width), lambda i, f: (0, i, 0))] + [anywhere] * 3,
            out_specs=[pl.BlockSpec((1, tile, width), lambda i, f: (f[6], i, 0))] * 3,
        ),
        out_shape=[jax.ShapeDtypeStruct(array.shape, f32) for array in before],
        input_output_aliases={2 + i: i for i in range(3)},
        compiler_params=params(),
        cost_estimate=cost(6.5),
        name="weight_fill",
    )(facts, source, *before)


def place_kernel(capacity, padded, block, local, turns, routes, rows, slots_out, wide_out, rows_out):
    experts_axis = block // padded
    tokens = rows.shape[0]
    experts = experts_axis * local
    number = lax.broadcasted_iota(jnp.int32, (experts, tokens), 0)
    picks = [number == routes[k : k + 1] for k in range(routes.shape[0])]
    named = picks[0]
    for pick in picks[1:]:
        named = named | pick
    earlier = lax.broadcasted_iota(jnp.int32, (tokens, tokens), 0) < lax.broadcasted_iota(
        jnp.int32, (tokens, tokens), 1
    )
    before = mm(named.astype(bf16), earlier.astype(bf16))
    places = []
    for k, pick in enumerate(picks):
        route = routes[k : k + 1]
        position = jnp.sum(jnp.where(pick, before, 0.0), axis=0, keepdims=True).astype(jnp.int32)
        owner = route // local
        turn = jnp.where(owner % 2 == 0, turns[:, 0:1], turns[:, 1:2])
        which = (route % local) ^ turn
        slot = which * block + owner * padded + position
        slots_out[k : k + 1] = jnp.where(position < capacity, slot, -1)
        slot = (owner * local + which) * padded + position
        places.append(jnp.where(position < capacity, slot, -1))
        wide_out[k : k + 1] = places[k]
    spots = lax.broadcasted_iota(jnp.int32, (local * block, tokens), 0)
    hot = spots == places[0]
    for slot in places[1:]:
        hot = hot | (spots == slot)
    rows_out[...] = mm(hot.astype(bf16), rows[...]).astype(bf16)


def place_rows(turns, routes, rows, capacity, padded, block, local):
    tops, tokens = routes.shape
    width = rows.shape[1]
    return pl.pallas_call(
        partial(place_kernel, capacity, padded, block, local),
        out_shape=[
            jax.ShapeDtypeStruct((tops, tokens), jnp.int32),
            jax.ShapeDtypeStruct((tops, tokens), jnp.int32),
            jax.ShapeDtypeStruct((local * block, width), bf16),
        ],
        compiler_params=pltpu.CompilerParams(vmem_limit_bytes=VMEM_BYTES),
        cost_estimate=cost(3.9),
        name="place_rows",
    )(turns, routes, rows)


def route_kernel(
    capacity, padded, mixed, w_proj, inputs, gain, router, routes, slots, resid, moe, probs, gates, *outs
):
    local, block = len(outs), outs[0].shape[0]
    tokens = inputs.shape[0]
    sums = inputs[...].astype(f32) + mm(mixed[...], w_proj[...])
    resid[...] = sums
    scale = lax.rsqrt(jnp.mean(sums * sums, axis=-1, keepdims=True) + 1e-06)
    low = (sums * scale * gain[...].astype(f32)).astype(bf16)
    moe[...] = low
    logits = mm(router[...], low, NT)
    grown = jnp.exp(logits - jnp.max(logits, axis=0, keepdims=True))
    share = grown / jnp.sum(grown, axis=0, keepdims=True)
    probs[...] = share
    number = lax.broadcasted_iota(jnp.int32, share.shape, 0)
    spots = lax.broadcasted_iota(jnp.int32, (local * block, tokens), 0)
    row = lax.broadcasted_iota(jnp.int32, (16, tokens), 0)
    hot = None
    lines = jnp.zeros((16, local * block), f32)
    for k in range(routes.shape[0]):
        gate = jnp.sum(jnp.where(number == routes[k : k + 1], share, 0.0), axis=0, keepdims=True)
        gates[k : k + 1] = gate
        high = gate.astype(bf16).astype(f32)
        both = jnp.where(row == 0, high, jnp.where(row == 1, gate - high, 0.0)).astype(bf16)
        mine = (spots == slots[k : k + 1]).astype(bf16)
        lines = lines + mm(both, mine, NT)
        hot = mine if hot is None else hot + mine
    filled = mm(hot, low).astype(bf16)
    spare = 16 - (padded - capacity)
    row = lax.broadcasted_iota(jnp.int32, (16, padded), 0)
    for j in range(local):
        outs[j][...] = filled[j * block : (j + 1) * block]
        for g in range(block // padded):
            at = j * block + g * padded
            tail = filled[at + padded - 16 : at + padded, :padded].astype(f32)
            line = lines[:, at : at + padded]
            tail = jnp.where(row == spare, line[0:1], jnp.where(row == spare + 1, line[1:2], tail))
            outs[j][pl.ds((g + 1) * padded - 16, 16), :padded] = tail.astype(bf16)


def route_rows(mixed, w_proj, inputs, gain, router, routes, slots, capacity, padded, block, local):
    tokens, width = inputs.shape
    tops = routes.shape[0]
    return pl.pallas_call(
        partial(route_kernel, capacity, padded),
        out_shape=[
            jax.ShapeDtypeStruct((tokens, width), f32),
            jax.ShapeDtypeStruct((tokens, width), bf16),
            jax.ShapeDtypeStruct((router.shape[0], tokens), f32),
            jax.ShapeDtypeStruct((tops, tokens), f32),
        ]
        + [jax.ShapeDtypeStruct((block, width), bf16)] * local,
        compiler_params=pltpu.CompilerParams(vmem_limit_bytes=VMEM_BYTES),
        cost_estimate=cost(6.4),
        name="route_rows",
    )(mixed, w_proj, inputs, gain.reshape(1, width), router, routes, slots)


def merge_kernel(
    capacity, padded, count, cotangent, resid, probs, moe, router, gain, w_proj, routes, slots, columns, *refs
):
    local = len(refs) - 5
    grads = refs[:local]
    grad_resid, grad_mixed, gain_grad, router_grad, branch_out = refs[local:]
    block = grads[0].shape[0]
    tokens = cotangent.shape[0]
    tops = routes.shape[0]
    spare = 16 - (padded - capacity)
    pieces = []
    for j in range(local):
        for g in range(block // padded):
            tail = grads[j][pl.ds((g + 1) * padded - 16, 16), : count * padded].astype(f32)
            line = tail[spare : spare + 1] + tail[spare + 1 : spare + 2]
            folded = line[:, :padded]
            for r in range(1, count):
                folded = folded + line[:, r * padded : (r + 1) * padded]
            pieces.append(folded)
    line = jnp.concatenate(pieces, axis=1)
    row = lax.broadcasted_iota(jnp.int32, (16, line.shape[1]), 0)
    high = line.astype(bf16).astype(f32)
    rest = line - high
    middle = rest.astype(bf16).astype(f32)
    stack = jnp.where(row == 0, high, jnp.where(row == 1, middle, jnp.where(row == 2, rest - middle, 0.0)))
    stack = stack.astype(bf16)
    share = probs[...]
    number = lax.broadcasted_iota(jnp.int32, share.shape, 0)
    spots = lax.broadcasted_iota(jnp.int32, (local * block, tokens), 0)
    grad_probs = jnp.zeros_like(share)
    for k in range(tops):
        picked = jnp.sum(mm(stack, (spots == slots[k : k + 1]).astype(bf16)), axis=0, keepdims=True)
        grad_probs = grad_probs + jnp.where(number == routes[k : k + 1], picked, 0.0)
    grad_logits = share * (grad_probs - jnp.sum(share * grad_probs, axis=0, keepdims=True))
    grad_logits = grad_logits.astype(bf16)
    router_grad[...] = mm(grad_logits, moe[...])
    grad_moe = mm(grad_logits, router[...], TN)
    spots = lax.broadcasted_iota(jnp.int32, (tokens, block), 1)
    for j in range(local):
        hot = None
        for k in range(tops):
            mine = spots + j * block == columns[:, k : k + 1]
            hot = mine if hot is None else hot | mine
        grad_moe = grad_moe + mm(hot.astype(bf16), grads[j][...])
    rows = resid[...]
    scale = lax.rsqrt(jnp.mean(rows * rows, axis=-1, keepdims=True) + 1e-06)
    normed = rows * scale
    gain_grad[...] = jnp.sum(grad_moe * normed, axis=0, keepdims=True)
    lifted = grad_moe * gain[...].astype(f32)
    spread = jnp.mean(lifted * normed, axis=-1, keepdims=True)
    back = cotangent[...].astype(f32) + scale * (lifted - normed * spread)
    grad_resid[...] = back
    branch = back.astype(bf16)
    grad_mixed[...] = mm(branch, w_proj[...], NT).astype(bf16)
    branch_out[...] = branch


def merge_rows(
    cotangent, resid, probs, moe, router, gain, w_proj, routes, slots, grads, capacity, padded, count
):
    tokens, width = cotangent.shape
    return pl.pallas_call(
        partial(merge_kernel, capacity, padded, count),
        out_shape=[
            jax.ShapeDtypeStruct((tokens, width), f32),
            jax.ShapeDtypeStruct((tokens, width), bf16),
            jax.ShapeDtypeStruct((1, width), f32),
            jax.ShapeDtypeStruct((router.shape[0], width), f32),
            jax.ShapeDtypeStruct((tokens, width), bf16),
        ],
        compiler_params=pltpu.CompilerParams(vmem_limit_bytes=VMEM_BYTES),
        cost_estimate=cost(7.4),
        name="merge_rows",
    )(
        cotangent, resid, probs, moe, router, gain.reshape(1, width), w_proj, routes, slots,
        jnp.transpose(slots), *grads,
    )


def blocks_kernel(
    local,
    facts,
    normed,
    normed_others,
    mixed,
    grad_query,
    grad_pair,
    grad_others,
    grad_near,
    branch,
    bias_grad,
    gain_grad,
    router_grad,
    near,
    far,
    near_right,
    far_right,
):
    step = pl.program_id(0)
    number = facts[3]
    group = step ^ (number // 8)
    share = (near.shape[1] - 8) // 4
    short = grad_near.shape[0] // 2
    own, own_short = normed[:local], normed[local:]

    def keyed(which):
        part = mm(own, grad_pair[which * local : (which + 1) * local], TN)
        part = part + mm(own_short, grad_near[which * short : (which + 1) * short], TN)
        for r in range(normed_others.shape[0] // local):
            at = (2 * r + which) * local
            part = part + mm(normed_others[r * local : (r + 1) * local], grad_others[at : at + local], TN)
        return part

    made = [mm(normed[...], grad_query[...], TN), keyed(0), keyed(1), mm(mixed[...], branch[...], TN)]
    made = [part.astype(bf16) for part in made]
    pairs, _, buckets = bias_grad.shape
    line = [bias_grad[p, h : h + 1, :] for p in range(pairs) for h in range(2)]
    line.append(jnp.zeros((1, 2 * near.shape[2] - 2 * pairs * buckets), f32))
    tail = jnp.zeros((24 - 2 - router_grad.shape[0], 2 * near.shape[2]), f32)
    small = jnp.concatenate(
        [jnp.concatenate(line, axis=1), gain_grad[...], router_grad[...], tail], axis=0
    )
    for s in range(8):
        spot = s ^ (number % 8)
        lines = [part[s * share : (s + 1) * share] for part in made]
        extra = jnp.zeros((8, 2 * near.shape[2]), f32)
        if s < 3:
            extra = jnp.where(group == 0, small[s * 8 : s * 8 + 8], extra)
        whole = jnp.concatenate(lines + [extra.astype(bf16)], axis=0)

        @pl.when(step < 2)
        def _():
            near[spot] = whole[:, : near.shape[2]]
            near_right[spot] = whole[:, near.shape[2] :]

        @pl.when(step >= 2)
        def _():
            far[spot] = whole[:, : near.shape[2]]
            far_right[spot] = whole[:, near.shape[2] :]


def weight_blocks(facts, lefts, rights, branch, bias_grad, gain_grad, router_grad, local):
    tokens, width = lefts[0].shape
    rows = 4 * width // 32 + 8
    cut = lambda count: pl.BlockSpec((count, width // 4), lambda i, f: (0, i ^ (f[3] // 8)))
    full = lambda count: pl.BlockSpec((count, width), lambda i, f: (0, 0))
    out = lambda which: pl.BlockSpec((8, rows, width // 2), which)
    return pl.pallas_call(
        partial(blocks_kernel, local),
        grid_spec=pltpu.PrefetchScalarGridSpec(
            num_scalar_prefetch=1,
            grid=(4,),
            in_specs=[cut(left.shape[0]) for left in lefts]
            + [full(right.shape[0]) for right in rights]
            + [
                full(tokens),
                pl.BlockSpec(bias_grad.shape, lambda i, f: (0, 0, 0)),
                full(1),
                full(router_grad.shape[0]),
            ],
            out_specs=[
                out(lambda i, f: (jnp.minimum(i, 1), 0, 0)),
                out(lambda i, f: (jnp.maximum(i - 2, 0), 0, 0)),
            ]
            * 2,
        ),
        out_shape=[jax.ShapeDtypeStruct((16, rows, width // 2), bf16)] * 4,
        compiler_params=params(),
        cost_estimate=cost(17),
        name="weight_blocks",
    )(facts, *lefts, *rights, branch, bias_grad, gain_grad, router_grad)


def unpack_kernel(facts, near, far, w_query, w_key, w_value, gain, gain_before, *refs):
    query, key, value, proj, small, gain_grad = refs[-6:]
    step = pl.program_id(0)
    number = facts[3]
    group = step ^ (number // 8)
    share = (near.shape[1] - 8) // 4

    def spread(source):
        for s in range(8):
            block = source[s ^ (number % 8)].astype(f32)
            for which, out in enumerate((query, key, value, proj)):
                out[s * share : (s + 1) * share] = block[which * share : (which + 1) * share]
            if s < 3:

                @pl.when(group == 0)
                def _():
                    small[s * 8 : s * 8 + 8] = block[4 * share :]

    @pl.when(step < 2)
    def _():
        spread(near)

    @pl.when(step >= 2)
    def _():
        spread(far)

    sums = query[...] * w_query[...].astype(f32)
    sums = sums + key[...] * w_key[...].astype(f32)
    sums = sums + value[...] * w_value[...].astype(f32)
    column = jnp.sum(sums, axis=-1, keepdims=True)
    size = column.shape[0]
    match = lax.broadcasted_iota(jnp.int32, (size, size), 0) == lax.broadcasted_iota(
        jnp.int32, (size, size), 1
    )
    line = jnp.sum(jnp.where(match, column, 0.0), axis=0, keepdims=True)
    gain_grad[...] = gain_before[...] + line / gain[...].astype(f32)


def unpack_blocks(facts, near, far, w_query, w_key, w_value, gain, gain_before, before, half):
    width = w_query.shape[0]
    wide = width // 2
    rows = near.shape[1]
    step = width // 4
    line = pl.BlockSpec((1, step), lambda i, f: (0, i ^ (f[3] // 8)))
    block = pl.BlockSpec((step, wide), lambda i, f: (i ^ (f[3] // 8), half))
    return pl.pallas_call(
        unpack_kernel,
        grid_spec=pltpu.PrefetchScalarGridSpec(
            num_scalar_prefetch=1,
            grid=(4,),
            in_specs=[
                pl.BlockSpec((8, rows, wide), lambda i, f: (jnp.minimum(i, 1), 0, 0)),
                pl.BlockSpec((8, rows, wide), lambda i, f: (jnp.maximum(i - 2, 0), 0, 0)),
                block,
                block,
                block,
                line,
                line,
            ]
            + [pl.BlockSpec(memory_space=pl.ANY)] * len(before),
            out_specs=[block, block, block, block, pl.BlockSpec((24, wide), lambda i, f: (0, half)), line],
        ),
        out_shape=[jax.ShapeDtypeStruct((width, width), f32)] * 4
        + [jax.ShapeDtypeStruct((24, width), f32), jax.ShapeDtypeStruct((1, width), f32)],
        input_output_aliases={8 + i: i for i in range(len(before))},
        compiler_params=params(),
        cost_estimate=cost(8),
        name="unpack_blocks",
    )(facts, near, far, w_query, w_key, w_value, gain.reshape(1, width), gain_before, *before)


def per_device(
    inputs,
    attn_gain,
    w_query,
    w_key,
    w_value,
    w_proj,
    rel_bias,
    moe_gain,
    w_router,
    w_gate,
    w_up,
    w_down,
    routes,
    long_buckets,
    short_buckets,
    long_lens,
    short_lens,
    cotangent,
):
    experts_axis = lax.axis_size("expert")
    tensor_axis = lax.axis_size("tensor")
    place = lax.axis_index("tensor")
    tok_count, width = inputs.shape
    top_count = routes.shape[1]
    short_len = (short_buckets.shape[0] + 1) // 2
    long_span = (long_buckets.shape[0] + 1) // 2
    long_local = tok_count - short_len
    bucket_count, heads = rel_bias.shape
    head_dim = width // heads
    experts = w_router.shape[1]
    local = experts // experts_axis
    capacity = (5 * tok_count * top_count + 4 * experts - 1) // (4 * experts)
    padded = (capacity + 2 + 15) // 16 * 16
    block = experts_axis * padded
    rel_table = rel_bias.astype(f32)
    here = lax.axis_index("expert")
    number = (here % 2) * 16 + place * 4 + here // 2
    paired = tensor_axis == 4 and local == 2
    routes_rows = jnp.transpose(routes)
    router = jnp.transpose(w_router)
    gate_turned = jnp.swapaxes(w_gate, 1, 2)
    up_turned = jnp.swapaxes(w_up, 1, 2)
    if paired:
        turns = jnp.stack([place % 2, place // 2]).astype(jnp.int32)
        which = jnp.where(here % 2 == 0, turns[0], turns[1])
        part_of = jnp.where(here % 2 == 0, turns[1], turns[0])
        shares = 2
    else:
        turns = jnp.zeros((2,), jnp.int32)
        which, part_of, shares = jnp.int32(0), place, tensor_axis
    facts = [place, long_lens[0], short_lens[0], number, which, part_of, 1 - which]
    facts = jnp.stack([jnp.asarray(fact, jnp.int32) for fact in facts])

    def trade(rows, other):
        pairs = []
        for e in range(experts_axis):
            mask = (2 if e % 2 == 0 else 1) if other else (1 if e % 2 == 0 else 2)
            pairs += [(e * tensor_axis + t, e * tensor_axis + (t ^ mask)) for t in range(tensor_axis)]
        return lax.ppermute(rows, ("expert", "tensor"), pairs)

    long_rows = inputs[:long_local]
    sources = [swap(long_rows, "tensor", r) for r in range(1, tensor_axis)]
    slots, wide_slots, grad_slots_in = place_rows(
        turns.reshape(1, 2), routes_rows, cotangent, capacity, padded, block, local
    )
    normed_low, normed_others, query, pair, others, near = project(
        inputs, sources, attn_gain, w_query, w_key, w_value, long_local
    )

    def by_expert(rows):
        split = rows.reshape(experts_axis, local, padded, width)
        return [split[:, j].reshape(block, width) for j in range(local)]

    def by_device(parts):
        split = [part.reshape(experts_axis, 1, padded, width) for part in parts]
        return jnp.concatenate(split, axis=1).reshape(local * block, width)

    grad_whole = over_experts(grad_slots_in)
    parts = (pair, others)
    if paired:
        other = pick_weights(facts, gate_turned, up_turned, w_down)
        other = trade(after(other, sources), False)

    reach = long_span + long_local
    first = long_span - long_local - long_local * place
    long_table = jnp.pad(long_buckets, (0, 1), constant_values=-1)
    long_hot = table_hot(lax.dynamic_slice_in_dim(long_table, first, reach, 0), bucket_count)
    short_hot = table_hot(jnp.pad(short_buckets, (0, 1), constant_values=-1), bucket_count)
    spread = lambda hot: jnp.einsum(
        "cb,bh->hc", hot, rel_table, precision=precise, preferred_element_type=f32
    )
    mixed, far_attend, near_attend = attend_forward(
        facts, query, parts, near, spread(long_hot), spread(short_hot),
        tensor_axis, long_local, head_dim,
    )
    resid, moe_low, probs, gates, *slots_in = route_rows(
        mixed, w_proj, inputs, moe_gain, router, routes_rows, slots, capacity, padded, block, local
    )

    own = (gate_turned, up_turned, w_down)
    lanes_used = shares * padded
    if paired:

        run = lambda rows, grads: expert_pass(
            facts, rows, grads, own, other, capacity, padded, lanes_used
        )
        grad_arrived = by_expert(after(grad_whole, slots_in))
        grads_b = trade(grad_arrived[1], False)
        grads_d = trade(grads_b, True)
        rows_b = over_experts(slots_in[1])
        rows_a = over_experts(after(slots_in[0], rows_b))
        rows_b = trade(after(rows_b, grads_b, grads_d), False)
        rows_d = trade(rows_b, True)
        grads_c = trade(after(grad_arrived[0], rows_d), True)
        pass_b = run(rows_b, grads_b)
        pass_d = run(after(rows_d, pass_b[1]), grads_d)
        rows_c = trade(after(rows_a, rows_d), True)
        pass_a = run(after(rows_a, pass_d[1], rows_c), grad_arrived[0])
        traded = add_low(pass_b[2], after(trade(pass_d[2], True), pass_a[1]))
        traded = trade(traded, False)
        pass_c = run(after(rows_c, pass_a[1]), grads_c)
        traded = after(traded, pass_c[1])
        traded_back = over_experts(traded)
        kept = add_low(pass_a[2], trade(after(pass_c[2], traded), True))
        grad_slots = [over_experts(after(kept, traded_back)), traded_back]

        passes = [pass_a, pass_c, pass_b, pass_d]
        slot_blocks = [rows_a, rows_c, rows_b, rows_d]
        grad_blocks = [grad_arrived[0], grads_c, grads_b, grads_d]
        (sent,) = weight_pass(
            facts, slot_blocks, grad_blocks, [after_all(made[0][1], pass_c[1]) for made in passes], (), local, True
        )
        weight_grads = weight_pass(
            facts, slot_blocks, grad_blocks, [after_all(made[0][0], sent) for made in passes], (), local, False
        )
        outs_d = trade(after(pass_d[1], traded), True)
        outs_c = trade(after(pass_c[1], kept, outs_d), True)
        outs_traded = trade(add_low(pass_b[1], outs_d), False)
        outs_kept = add_low(pass_a[1], outs_c)
        grad_slots[0] = after(grad_slots[0], weight_grads, outs_c, outs_traded)
        held_back = outs_traded
        sent = trade(after(sent, outs_traded), False)
        outs_back = over_experts(after(by_device([outs_kept, outs_traded]), grad_slots[0]))
    else:
        grad_blocks = [gather_parts(rows) for rows in by_expert(grad_whole)]
        slot_blocks = [gather_parts(over_experts(slots_in[j])) for j in range(local)]
        weight_grads, passes = (), []
        for j in range(local):
            facts_j = facts.at[4].set(j)
            passes.append(
                [
                    expert_pass(facts_j, rows, grads, own, None, capacity, padded, lanes_used)
                    for rows, grads in zip(slot_blocks[j], grad_blocks[j])
                ]
            )
            weight_grads = weight_pass(
                facts_j, slot_blocks[j], grad_blocks[j], [made[0][0] for made in passes[j]], weight_grads, local, False
            )
        send_back = lambda which: [
            over_experts(sum_parts([made[which] for made in passes[j]]).astype(bf16)) for j in range(local)
        ]
        grad_slots = send_back(2)
        outs_back = by_device(send_back(1))
        held_back = sent = grad_slots[0]

    grad_resid, grad_mixed, moe_gain_grad, router_grad, branch = merge_rows(
        cotangent, resid, probs, moe_low, router, moe_gain, w_proj, routes_rows, slots, grad_slots,
        capacity, padded, shares,
    )
    grad_mixed = after(grad_mixed, held_back)
    quick = experts_axis == 8 and tensor_axis == 4
    hots = (long_hot.astype(bf16), short_hot.astype(bf16))
    *attn_grads, bias_grad = attend_backward(
        facts, query, grad_mixed, parts, near, (far_attend, near_attend), hots, tensor_axis, long_local, head_dim
    )
    if quick:
        bias_grad = after(bias_grad, sent)
        made = weight_blocks(
            facts, (normed_low, normed_others, mixed), attn_grads, branch, bias_grad, moe_gain_grad, router_grad,
            long_local,
        )
        sums = [add_low(made[half], swap(made[half + 1], "expert", 1)) for half in (0, 2)]
        attn_grads = after_all(attn_grads, sums, outs_back)
    own_grads, near_grads, away = normed_grads(attn_grads, w_query, w_key, w_value, long_local, tensor_axis)
    if quick:
        sums = [ring_sum(plane_parts(part), in_plane).astype(bf16) for part in sums]
        away = after(away, sums)
    pieces = [own_grads] + [
        away[r * long_local : (r + 1) * long_local].astype(bf16) for r in range(tensor_axis - 1)
    ]
    if tensor_axis == 4:
        pieces = pieces[:3] + [pieces[3][: long_local // 2], pieces[3][long_local // 2 :]]
    summed = sum_parts(pieces)
    if quick:
        owns = [sum_depth(part) for part in sums]
        sums = [spread_depth(own) for own in owns]
        sent, outs_back, summed = after_all((sent, outs_back, summed), sums[0], owns[1])
        sums[1] = after(sums[1], summed)
    if paired:
        weight_grads = weight_fill(facts, sent, weight_grads)
    slot_places = jnp.arange(local * block, dtype=jnp.int32)
    outputs = resid
    for k in range(top_count):
        chosen = mm((wide_slots[k][:, None] == slot_places).astype(bf16), outs_back)
        outputs = outputs + gates[k][:, None] * chosen
    outputs = outputs.astype(bf16)
    grad_normed = jnp.concatenate([summed, near_grads], axis=0)
    inputs_wide = inputs.astype(f32)
    scale = lax.rsqrt(jnp.mean(inputs_wide * inputs_wide, axis=-1, keepdims=True) + 1e-06)
    normed = inputs_wide * scale
    lifted = grad_normed * attn_gain.astype(f32)
    inputs_grad = grad_resid + scale * (
        lifted - normed * jnp.mean(lifted * normed, axis=-1, keepdims=True)
    )
    if quick:
        unpack = partial(unpack_blocks, facts)
        weights = (w_query, w_key, w_value, attn_gain)
        one, two = sums
        by_x, by_y = in_plane(one, 0), in_plane(one, 1)
        half_x, half_y = after_all((by_x[:2], by_y[2:]), outputs, weight_grads, two)
        one = jnp.concatenate([one, by_x, by_y, in_plane(half_x, 1), in_plane(half_y, 0)], axis=0)
        first = unpack(one, swap(one, "expert", 1), *weights, jnp.zeros((1, width), f32), (), 0)
        by_x, by_y = in_plane(two, 0), in_plane(two, 1)
        rest = after_all((in_plane(by_x[:2], 1), in_plane(by_y[2:], 0)), first[5], inputs_grad)
        two = jnp.concatenate([two, by_x, by_y] + rest, axis=0)
        second = unpack(two, swap(two, "expert", 1), *weights, first[5], first[:5], 1)
        query_grad, key_grad, value_grad, proj_grad = second[:4]
        attn_gain_grad = second[5][0]
        small = second[4]
    else:
        key_others = [slice(2 * r * long_local, (2 * r + 1) * long_local) for r in range(tensor_axis - 1)]
        value_others = [slice((2 * r + 1) * long_local, (2 * r + 2) * long_local) for r in range(tensor_axis - 1)]

        def keyed(index, spots):
            short = slice(index * short_len, (index + 1) * short_len)
            rows = slice(index * long_local, (index + 1) * long_local)
            lefts = jnp.concatenate([normed_low, normed_others], axis=0)
            rights = jnp.concatenate(
                [attn_grads[1][rows], attn_grads[3][short]] + [attn_grads[2][spot] for spot in spots], axis=0
            )
            return mm(lefts, rights, TN)

        rel_row = jnp.pad(bias_grad.reshape(1, -1), ((0, 0), (0, width - bias_grad.size)))
        small = jnp.concatenate([rel_row, moe_gain_grad, router_grad], axis=0)
        query_grad, key_grad, value_grad, proj_grad, small = lax.psum(
            (
                mm(normed_low, attn_grads[0], TN),
                keyed(0, key_others),
                keyed(1, value_others),
                mm(mixed, branch, TN),
                small,
            ),
            ("expert", "tensor"),
        )
        attn_gain_grad = jnp.sum(
            query_grad * w_query.astype(f32) + key_grad * w_key.astype(f32) + value_grad * w_value.astype(f32),
            axis=1,
        ) / attn_gain.astype(f32)
    rel_grad = jnp.transpose(small[0, : heads * bucket_count].reshape(heads, bucket_count))
    return (
        outputs,
        inputs_grad,
        attn_gain_grad,
        query_grad,
        key_grad,
        value_grad,
        proj_grad,
        rel_grad,
        small[1],
        jnp.transpose(small[2 : 2 + experts]),
        jnp.swapaxes(weight_grads[0], 1, 2),
        jnp.swapaxes(weight_grads[1], 1, 2),
        weight_grads[2],
    )


def solution(mesh):
    return jax.shard_map(
        per_device,
        mesh=mesh,
        in_specs=(
            P(("expert", "tensor"), None),
            P(),
            P(),
            P(),
            P(),
            P(),
            P(),
            P(),
            P(),
            P("expert", None, "tensor"),
            P("expert", None, "tensor"),
            P("expert", "tensor", None),
            P(("expert", "tensor"), None),
            P(),
            P(),
            P("expert"),
            P(("expert", "tensor")),
            P(("expert", "tensor"), None),
        ),
        out_specs=(
            P(("expert", "tensor"), None),
            P(("expert", "tensor"), None),
            P(),
            P(),
            P(),
            P(),
            P(),
            P(),
            P(),
            P(),
            P("expert", None, "tensor"),
            P("expert", None, "tensor"),
            P("expert", "tensor", None),
        ),
        check_vma=False,
    )
```

```python
from functools import partial
import math

import jax
import jax.numpy as jnp
from jax import lax
from jax.experimental import pallas as pl
from jax.experimental.pallas import tpu as pltpu
from jax.sharding import PartitionSpec as P

precise = lax.Precision.HIGHEST
bf16 = jnp.bfloat16
f32 = jnp.float32
NT = (((1,), (1,)), ((), ()))
NN = (((1,), (0,)), ((), ()))
TN = (((0,), (0,)), ((), ()))
VMEM_BYTES = 56 * 1024 * 1024


def mm(left, right, dims=NN):
    return lax.dot_general(left, right, dims, preferred_element_type=f32)


def params():
    return pltpu.CompilerParams(
        dimension_semantics=("arbitrary",), vmem_limit_bytes=VMEM_BYTES
    )


def cost(micros):
    return pl.CostEstimate(flops=int(micros * 1.15e9), bytes_accessed=0, transcendentals=0)


def table_hot(table, count):
    return (table[:, None] == jnp.arange(count, dtype=jnp.int32)[None, :]).astype(f32)


def swap(rows, axis, mask):
    count = lax.axis_size(axis)
    return lax.ppermute(rows, axis, [(i, i ^ mask) for i in range(count)])


def after(value, *others):
    return lax.optimization_barrier((value,) + tuple(jax.tree.leaves(others)))[0]


def after_all(values, *others):
    leaves = tuple(jax.tree.leaves(others))
    return list(lax.optimization_barrier(tuple(values) + leaves)[: len(values)])


def ring_gather(rows, move):
    half = rows.shape[0] // 2
    first, second = move(rows, 0), move(rows, 1)
    return [rows, first, second, move(first[:half], 1), move(second[half:], 0)]


def ring_sum_first(parts, move):
    half = parts[3].shape[0]
    left = move(parts[3], 0)
    right = move(parts[4], 1)
    to_second = jnp.concatenate([add_low(parts[2][:half], left), parts[2][half:]], axis=0)
    to_first = jnp.concatenate([parts[1][:half], add_low(parts[1][half:], right)], axis=0)
    return parts[0], to_first, to_second


def ring_sum_second(own, to_first, to_second, move):
    first = move(to_first, 0)
    second = move(to_second, 1)
    return own.astype(f32) + first.astype(f32) + second.astype(f32)


def ring_sum(parts, move):
    return ring_sum_second(*ring_sum_first(parts, move), move)


def in_plane(rows, way):
    return swap(rows, "tensor", 1 + way)


def gather_parts(rows):
    count = lax.axis_size("tensor")
    if count == 4:
        return ring_gather(rows, in_plane)
    return [rows] + [swap(rows, "tensor", r) for r in range(1, count)]


def sum_parts(parts):
    count = lax.axis_size("tensor")
    if count == 4:
        return ring_sum(parts, in_plane)
    arrived = [swap(parts[r], "tensor", r) for r in range(1, count)]
    return sum([part.astype(f32) for part in arrived], parts[0].astype(f32))


def over_experts(rows):
    experts_axis = lax.axis_size("expert")
    blocks = rows.reshape(experts_axis, rows.shape[0] // experts_axis, rows.shape[1])
    return lax.all_to_all(blocks, "expert", 0, 0, tiled=True).reshape(rows.shape)


def add_low(left, right):
    return (left.astype(f32) + right.astype(f32)).astype(bf16)


def sum_cores(near, far):
    return add_low(near, swap(far, "expert", 1))


def plane_parts(rest):
    return [rest[0:4], rest[4:8], rest[8:12], rest[12:14], rest[14:16]]


def sum_depth(rest):
    arrived = swap(rest[1::2], "expert", 2)
    own, opposite = add_low(rest[0], arrived[0]), add_low(rest[2], arrived[1])
    return add_low(own, swap(opposite, "expert", 4))


def spread_depth(own):
    opposite = swap(own, "expert", 4)
    arrived = swap(jnp.stack([own, opposite]), "expert", 2)
    return jnp.stack([own, arrived[0], opposite, arrived[1]])


def spread_plane(rest):
    return jnp.concatenate(ring_gather(rest, in_plane), axis=0)


def project_kernel(
    local, gain, w_query, w_key, w_value, inputs, *refs
):
    sources, (normed, normed_others, query, pair, others, near, held) = refs[:-7], refs[-7:]
    tokens = inputs.shape[0]

    @pl.when(pl.program_id(0) == 0)
    def _():
        rows = jnp.concatenate([inputs[...]] + [source[...] for source in sources], axis=0).astype(f32)
        scale = lax.rsqrt(jnp.mean(rows * rows, axis=-1, keepdims=True) + 1e-06)
        held[...] = (rows * scale * gain[...].astype(f32)).astype(bf16)
        normed[...] = held[:tokens]
        normed_others[...] = held[tokens:]

    query[...] = mm(held[:tokens], w_query[...]).astype(bf16)
    keys = mm(held[...], w_key[...]).astype(bf16)
    values = mm(held[...], w_value[...]).astype(bf16)
    pair[:local] = keys[:local]
    pair[local:] = values[:local]
    short = tokens - local
    near[:short] = keys[local:tokens]
    near[short:] = values[local:tokens]
    for r in range((held.shape[0] - tokens) // local):
        low = tokens + r * local
        others[2 * r * local : (2 * r + 1) * local] = keys[low : low + local]
        others[(2 * r + 1) * local : (2 * r + 2) * local] = values[low : low + local]


def project(inputs, sources, gain, w_query, w_key, w_value, local):
    tokens, width = inputs.shape
    away = sum(source.shape[0] for source in sources)
    short = tokens - local
    step = 256
    whole = lambda count: pl.BlockSpec((count, width), lambda i: (0, 0))
    cut = lambda count: pl.BlockSpec((count, step), lambda i: (0, i))
    return pl.pallas_call(
        partial(project_kernel, local),
        grid=(width // step,),
        in_specs=[whole(1), cut(width), cut(width), cut(width), whole(tokens)]
        + [whole(source.shape[0]) for source in sources],
        out_specs=[whole(tokens), whole(away), cut(tokens), cut(2 * local), cut(2 * away), cut(2 * short)],
        out_shape=[
            jax.ShapeDtypeStruct((size, width), bf16)
            for size in (tokens, away, tokens, 2 * local, 2 * away, 2 * short)
        ],
        scratch_shapes=[pltpu.VMEM((tokens + away, width), bf16)],
        compiler_params=params(),
        cost_estimate=cost(12),
        name="project",
    )(gain.reshape(1, width), w_query, w_key, w_value, inputs, *sources)


def key_value_views(pair, others, count, rows):
    views = [(pair, slice(0, rows), pair, slice(rows, 2 * rows))]
    for r in range(count - 1):
        at = 2 * r * rows
        views.append((others, slice(at, at + rows), others, slice(at + rows, at + 2 * rows)))
    return views


def own_lanes(head, dim, shape, axis):
    place = lax.broadcasted_iota(jnp.int32, shape, axis)
    return (place >= head * dim) & (place < (head + 1) * dim)


def forward_kernel(
    count,
    rows,
    dim,
    facts,
    query,
    pair,
    others,
    near,
    far_bias,
    near_bias,
    mixed,
    far_attend,
    near_attend,
    window,
    scores,
):
    place, far_len, near_len = facts[0], facts[1], facts[2]
    scale = 1.0 / math.sqrt(dim)
    views = key_value_views(pair, others, count, rows)
    short = near.shape[0] // 2
    band, reach = window.shape[1:]
    low = (query[...].astype(f32) * scale).astype(bf16)
    starts = [(place ^ r) * rows for r in range(count)]
    spot = lax.broadcasted_iota(jnp.int32, (1, rows), 1)
    kept = [start + spot < far_len for start in starts]
    near_kept = lax.broadcasted_iota(jnp.int32, (1, short), 1) < near_len
    line = 2 * (pl.program_id(0) % 4)
    mine = [jnp.where(own_lanes(head, dim, low.shape, 1), low, jnp.zeros_like(low)) for head in range(2)]
    far_mine = jnp.concatenate([part[:rows] for part in mine], axis=0)
    near_parts = mm(jnp.concatenate([part[rows:] for part in mine], axis=0), near[:short], NT)
    near_parts = [near_parts[:short], near_parts[short:]]
    for r in range(count):
        part = mm(far_mine, views[r][0][views[r][1]], NT)
        for head in range(2):
            scores[head, :, r * rows : (r + 1) * rows] = part[head * rows : (head + 1) * rows]
    for head in range(2):
        table = jnp.broadcast_to(far_bias[pl.ds(line + head, 1)], (band, reach))
        window[head] = pltpu.roll(table, reach - (band - 1), 1, stride=1, stride_axis=0)
    for head in range(2):
        table = jnp.broadcast_to(near_bias[pl.ds(line + head, 1)], (short, 2 * short))
        bias = pltpu.roll(table, short + 1, 1, stride=1, stride_axis=0)[:, :short]
        part = jnp.where(near_kept, near_parts[head] + bias, -1e30)
        part = jnp.exp(part - jnp.max(part, axis=-1, keepdims=True))
        near_attend[head] = (part * (1.0 / jnp.sum(part, axis=-1, keepdims=True))).astype(bf16)
        for at in range(0, rows, 32):
            shift = band * (rows // band - 1 - at // band)
            lines = slice(at % band, at % band + 32)
            parts = []
            for r in range(count):
                begin = pl.multiple_of(starts[r] + shift, 128)
                part = scores[head, at : at + 32, r * rows : (r + 1) * rows]
                part = part + window[head, lines, pl.ds(begin, rows)]
                parts.append(jnp.where(kept[r], part, -1e30))
            highest = parts[0]
            for part in parts[1:]:
                highest = jnp.maximum(highest, part)
            highest = jnp.max(highest, axis=-1, keepdims=True)
            parts = [jnp.exp(part - highest) for part in parts]
            whole = parts[0]
            for part in parts[1:]:
                whole = whole + part
            inverse = 1.0 / jnp.sum(whole, axis=-1, keepdims=True)
            for r in range(count):
                far_attend[head, at : at + 32, r * rows : (r + 1) * rows] = (parts[r] * inverse).astype(bf16)
    out = jnp.zeros((2 * rows, 2 * dim), f32)
    for r in range(count):
        attend = far_attend[:, :, r * rows : (r + 1) * rows].reshape(2 * rows, rows)
        out = out + mm(attend, views[r][2][views[r][3]])
    near_out = mm(near_attend[...].reshape(2 * short, short), near[short:])
    second = own_lanes(1, dim, (rows, 2 * dim), 1)
    mixed[:rows] = jnp.where(second, out[rows:], out[:rows]).astype(bf16)
    second = own_lanes(1, dim, (short, 2 * dim), 1)
    mixed[rows:] = jnp.where(second, near_out[short:], near_out[:short]).astype(bf16)


def attention_specs(count, rows, short, reach, tokens):
    cut = lambda size: pl.BlockSpec((size, 128), lambda i, *_: (0, i))
    parts = [cut(2 * rows), cut(2 * (count - 1) * rows)]
    table = lambda size: pl.BlockSpec((8, size), lambda i, *_: (i // 4, 0))
    weights = lambda size, span: pl.BlockSpec((2, size, span), lambda i, *_: (i, 0, 0))
    return (
        cut(tokens),
        parts,
        cut(2 * short),
        [table(reach), table(2 * short)],
        [weights(rows, count * rows), weights(short, short)],
    )


def attend_forward(facts, query, parts, near, far_bias, near_bias, count, rows, dim):
    tokens, width = query.shape
    heads = width // dim
    short = near.shape[0] // 2
    reach = far_bias.shape[-1]
    cut, part_specs, near_spec, tables, weights = attention_specs(count, rows, short, reach, tokens)
    return pl.pallas_call(
        partial(forward_kernel, count, rows, dim),
        grid_spec=pltpu.PrefetchScalarGridSpec(
            num_scalar_prefetch=1,
            grid=(heads // 2,),
            in_specs=[cut] + part_specs + [near_spec] + tables,
            out_specs=[cut] + weights,
            scratch_shapes=[pltpu.VMEM((2, 128, reach), f32), pltpu.VMEM((2, rows, count * rows), f32)],
        ),
        out_shape=[
            jax.ShapeDtypeStruct((tokens, width), bf16),
            jax.ShapeDtypeStruct((heads, rows, count * rows), bf16),
            jax.ShapeDtypeStruct((heads, short, short), bf16),
        ],
        compiler_params=params(),
        cost_estimate=cost(17),
        name="attend_forward",
    )(facts, query, *parts, near, far_bias, near_bias)


def backward_kernel(
    count,
    rows,
    dim,
    facts,
    query,
    grad,
    pair,
    others,
    near,
    far_attend,
    near_attend,
    far_hot,
    near_hot,
    grad_query,
    grad_pair,
    grad_others,
    grad_near,
    bias_grad,
    window,
    near_window,
    products,
    scores,
    near_scores,
):
    place = facts[0]
    scale = 1.0 / math.sqrt(dim)
    views = key_value_views(pair, others, count, rows)
    grad_views = key_value_views(grad_pair, grad_others, count, rows)
    short = near.shape[0] // 2
    band = window.shape[1]
    starts = [(place ^ r) * rows for r in range(count)]

    @pl.when(pl.program_id(0) == 0)
    def _():
        near_window[...] = jnp.zeros_like(near_window)

    def reversal(size):
        up = lax.broadcasted_iota(jnp.int32, (size, size), 0)
        across = lax.broadcasted_iota(jnp.int32, (size, size), 1)
        return (up + across == size - 1).astype(bf16)

    far_turn = reversal(band)
    near_turn = far_turn if short == band else reversal(short)
    low, grad_low = query[...], grad[...]
    turned = jnp.transpose(low.astype(f32) * scale, (1, 0)).astype(bf16)
    grad_turned = jnp.transpose(grad_low.astype(f32), (1, 0)).astype(bf16)
    mine, grad_mine, grad_heads = [], [], []
    for head in range(2):
        lines = own_lanes(head, dim, turned.shape, 0)
        mine.append(jnp.where(lines, turned, jnp.zeros_like(turned)))
        grad_mine.append(jnp.where(lines, grad_turned, jnp.zeros_like(turned)))
        lanes = own_lanes(head, dim, low.shape, 1)
        grad_heads.append(jnp.where(lanes, grad_low, jnp.zeros_like(grad_low)))
    far_grads = jnp.concatenate([part[:rows] for part in grad_heads], axis=0)
    near_parts = mm(jnp.concatenate([part[rows:] for part in grad_heads], axis=0), near[short:], NT)
    for r in range(count):
        part = mm(far_grads, views[r][2][views[r][3]], NT)
        for head in range(2):
            products[head, :, r * rows : (r + 1) * rows] = part[head * rows : (head + 1) * rows]
    window[...] = jnp.zeros_like(window)
    for head in range(2):
        wide = near_attend[head].astype(f32)
        part = near_parts[head * short : (head + 1) * short]
        part = wide * (part - jnp.sum(wide * part, axis=-1, keepdims=True))
        near_scores[head] = part.astype(bf16)
        for at in range(0, rows, 32):
            attend = far_attend[head, at : at + 32].astype(f32)
            part = products[head, at : at + 32]
            inner = jnp.sum(attend * part, axis=-1, keepdims=True)
            scores[head, at : at + 32] = (attend * (part - inner)).astype(bf16)
    out = jnp.zeros((2 * rows, 2 * dim), f32)
    for r in range(count):
        part = scores[:, :, r * rows : (r + 1) * rows].reshape(2 * rows, rows)
        out = out + mm(part, views[r][0][views[r][1]])
        for head in range(2):
            for h in range(rows // band):
                begin = pl.multiple_of(starts[r] + band * (rows // band - 1 - h), 128)
                lines = slice(head * rows + h * band, head * rows + (h + 1) * band)
                window[head, :, pl.ds(begin, rows)] += mm(far_turn, part[lines])
    near_out = mm(near_scores[...].reshape(2 * short, short), near[:short])
    second = own_lanes(1, dim, (rows, 2 * dim), 1)
    grad_query[:rows] = (jnp.where(second, out[rows:], out[:rows]) * scale).astype(bf16)
    second = own_lanes(1, dim, (short, 2 * dim), 1)
    grad_query[rows:] = (jnp.where(second, near_out[short:], near_out[:short]) * scale).astype(bf16)
    def by_bucket(lines, hot):
        row = lax.broadcasted_iota(jnp.int32, (16, lines.shape[1]), 0)
        high = lines.astype(bf16).astype(f32)
        rest = lines - high
        middle = rest.astype(bf16).astype(f32)
        stack = jnp.where(row == 0, high, jnp.where(row == 1, middle, jnp.where(row == 2, rest - middle, 0.0)))
        return jnp.sum(mm(stack.astype(bf16), hot[...]), axis=0, keepdims=True)

    for head in range(2):
        rolled = pltpu.roll(window[head], 0, 1, stride=1, stride_axis=0)
        sums = by_bucket(jnp.sum(rolled, axis=0, keepdims=True), far_hot)
        near_window[head, :, :short] = mm(near_turn, near_scores[head])
        rolled = pltpu.roll(near_window[head], 0, 1, stride=1, stride_axis=0)
        sums = sums + by_bucket(jnp.sum(rolled, axis=0, keepdims=True), near_hot)
        bias_grad[0, head : head + 1, :] = sums
    for r in range(count):
        lanes = slice(r * rows, (r + 1) * rows)
        keys = mm(mine[0][:, :rows], scores[0, :, lanes]) + mm(mine[1][:, :rows], scores[1, :, lanes])
        values = mm(grad_mine[0][:, :rows], far_attend[0, :, lanes]) + mm(
            grad_mine[1][:, :rows], far_attend[1, :, lanes]
        )
        view = grad_views[r]
        view[0][view[1]] = jnp.transpose(keys, (1, 0)).astype(bf16)
        view[2][view[3]] = jnp.transpose(values, (1, 0)).astype(bf16)
    keys = mm(mine[0][:, rows:], near_scores[0]) + mm(mine[1][:, rows:], near_scores[1])
    values = mm(grad_mine[0][:, rows:], near_attend[0]) + mm(grad_mine[1][:, rows:], near_attend[1])
    grad_near[:short] = jnp.transpose(keys, (1, 0)).astype(bf16)
    grad_near[short:] = jnp.transpose(values, (1, 0)).astype(bf16)


def attend_backward(facts, query, grad, parts, near, weights, hots, count, rows, dim):
    tokens, width = query.shape
    pairs = width // dim // 2
    short = near.shape[0] // 2
    reach, buckets = hots[0].shape
    cut, part_specs, near_spec, _, weight_specs = attention_specs(count, rows, short, reach, tokens)
    return pl.pallas_call(
        partial(backward_kernel, count, rows, dim),
        grid_spec=pltpu.PrefetchScalarGridSpec(
            num_scalar_prefetch=1,
            grid=(pairs,),
            in_specs=[cut, cut]
            + part_specs
            + [near_spec]
            + weight_specs
            + [pl.BlockSpec(hot.shape, lambda i, *_: (0, 0)) for hot in hots],
            out_specs=[cut]
            + part_specs
            + [near_spec, pl.BlockSpec((1, 2, buckets), lambda i, *_: (i, 0, 0))],
            scratch_shapes=[
                pltpu.VMEM((2, 128, reach), f32),
                pltpu.VMEM((2, short, 2 * short), f32),
                pltpu.VMEM((2, rows, count * rows), f32),
                pltpu.VMEM((2, rows, count * rows), bf16),
                pltpu.VMEM((2, short, short), bf16),
            ],
        ),
        out_shape=[
            jax.ShapeDtypeStruct((size, width), bf16)
            for size in (tokens, 2 * rows, 2 * (count - 1) * rows, 2 * short)
        ]
        + [jax.ShapeDtypeStruct((pairs, 2, buckets), f32)],
        compiler_params=params(),
        cost_estimate=cost(25),
        name="attend_backward",
    )(facts, query, grad, *parts, near, *weights, *hots)


def normed_grads_kernel(local, count, query, pair, others, near, w_query, w_key, w_value, *outs):
    own, own_short, away = outs
    short = near.shape[0] // 2

    @pl.when(pl.program_id(0) == 0)
    def _():
        for out in outs:
            out[...] = jnp.zeros_like(out)

    full = mm(query[...], w_query[...], NT)
    own[...] += full[:local] + mm(pair[:local], w_key[...], NT) + mm(pair[local:], w_value[...], NT)
    own_short[...] += full[local:] + mm(near[:short], w_key[...], NT) + mm(near[short:], w_value[...], NT)
    for r in range(count - 1):
        at = 2 * r * local
        away[r * local : (r + 1) * local] += mm(others[at : at + local], w_key[...], NT) + mm(
            others[at + local : at + 2 * local], w_value[...], NT
        )


def normed_grads(grads, w_query, w_key, w_value, local, count):
    width = w_query.shape[0]
    short = grads[3].shape[0] // 2
    cut = lambda size: pl.BlockSpec((size, width // 2), lambda i: (0, i))
    sizes = (local, short, (count - 1) * local)
    return pl.pallas_call(
        partial(normed_grads_kernel, local, count),
        grid=(2,),
        in_specs=[cut(array.shape[0]) for array in grads] + [cut(width)] * 3,
        out_specs=[pl.BlockSpec((size, width), lambda i: (0, 0)) for size in sizes],
        out_shape=[jax.ShapeDtypeStruct((size, width), f32) for size in sizes],
        compiler_params=params(),
        cost_estimate=cost(13),
        name="normed_grads",
    )(*grads, w_query, w_key, w_value)


def pick_kernel(facts, *refs):
    for i in range(3):
        refs[3][i] = refs[i][0]


def pick_weights(facts, *weights):
    _, units, width = weights[0].shape
    tile = units // 4
    return pl.pallas_call(
        pick_kernel,
        grid_spec=pltpu.PrefetchScalarGridSpec(
            num_scalar_prefetch=1,
            grid=(4,),
            in_specs=[pl.BlockSpec((1, tile, width), lambda i, f: (f[6], i, 0))] * 3,
            out_specs=pl.BlockSpec((3, tile, width), lambda i, f: (0, i, 0)),
        ),
        out_shape=jax.ShapeDtypeStruct((3, units, width), bf16),
        compiler_params=params(),
        cost_estimate=cost(5),
        name="pick_weights",
    )(facts, *weights)


def expert_kernel(chunks, capacity, padded, lanes_used, facts, slots_in, grads_in, *refs):
    sources, rest = refs[: 3 * chunks], refs[3 * chunks :]
    outs, rest = rest[: 3 * chunks + 2], rest[3 * chunks + 2 :]
    rows_buffer, grads_buffer, held, middles, out_buffer, grad_buffer, in_sems, out_sems = rest
    rows = rows_buffer.shape[0]
    units = sources[0].shape[1]
    wide = held.shape[1] // chunks
    groups = rows // padded
    spare = 16 - (padded - capacity)

    arrivals = [
        pltpu.make_async_copy(slots_in, rows_buffer, in_sems.at[0]),
        pltpu.make_async_copy(grads_in, grads_buffer, in_sems.at[1]),
    ]
    weights = []
    for k in range(3):
        for c in range(chunks):
            i = 3 * c + k
            index = facts[4] if c == 0 else k
            place = held.at[k, pl.ds(c * wide, units)]
            weights.append(pltpu.make_async_copy(sources[i].at[index], place, in_sems.at[2 + i]))
    arrivals[0].start()
    for copy in weights[: 2 * chunks]:
        copy.start()
    arrivals[1].start()
    for copy in weights[2 * chunks :]:
        copy.start()
    if wide > units:
        for k in range(3):
            for c in range(chunks):
                held[k, c * wide + units : (c + 1) * wide] = jnp.zeros((wide - units, held.shape[2]), bf16)

    arrivals[0].wait()
    lanes = lax.broadcasted_iota(jnp.int32, (padded, 128), 1)
    match = lax.broadcasted_iota(jnp.int32, (padded, 128), 0) == lanes
    columns = []
    for g in range(groups):
        tail = rows_buffer[pl.ds((g + 1) * padded - 16, 16), :128].astype(f32)
        line = tail[spare : spare + 1] + tail[spare + 1 : spare + 2]
        columns.append(jnp.sum(jnp.where(match, line, 0.0), axis=-1, keepdims=True))
    gate_column = jnp.concatenate(columns, axis=0)

    slots = rows_buffer[...]
    for copy in weights[:chunks]:
        copy.wait()
    gate_pre = mm(slots, held[0], NT)
    for copy in weights[chunks : 2 * chunks]:
        copy.wait()
    up_pre = mm(slots, held[1], NT)
    arrivals[1].wait()
    for copy in weights[2 * chunks :]:
        copy.wait()
    grads = grads_buffer[...]
    grad_hidden = mm(grads, held[2], NT) * gate_column
    slope = math.sqrt(2.0 / math.pi)
    square = gate_pre * gate_pre
    curve = jnp.tanh(slope * gate_pre * (1.0 + 0.044715 * square))
    side = 0.5 * (1.0 + curve)
    bent = gate_pre * side
    hidden = bent * up_pre
    bent_slope = side + 0.5 * slope * gate_pre * (1.0 - curve * curve) * (
        1.0 + 3.0 * 0.044715 * square
    )
    gate_low = (grad_hidden * up_pre * bent_slope).astype(bf16)
    up_low = (grad_hidden * bent).astype(bf16)
    departures = []

    def depart(buffer, target):
        copy = pltpu.make_async_copy(buffer, target, out_sems.at[len(departures)])
        copy.start()
        departures.append(copy)

    for k, value in enumerate(((hidden * gate_column).astype(bf16), gate_low, up_low)):
        for c in range(chunks):
            middles[3 * c + k] = value[:, c * wide : c * wide + units]
            depart(middles.at[3 * c + k], outs[3 * c + k])
    out = mm(hidden.astype(bf16), held[2])
    out_buffer[...] = out.astype(bf16)
    depart(out_buffer, outs[3 * chunks])
    grad_out = mm(gate_low, held[0]) + mm(up_low, held[1])
    grad_buffer[...] = grad_out.astype(bf16)

    grad_gate = jnp.sum(out * grads.astype(f32), axis=-1, keepdims=True)
    lanes = lax.broadcasted_iota(jnp.int32, (padded, lanes_used), 1)
    up = lax.broadcasted_iota(jnp.int32, (padded, lanes_used), 0)
    match = up + facts[5] * padded == lanes
    row = lax.broadcasted_iota(jnp.int32, (16, lanes_used), 0)
    for g in range(groups):
        values = jnp.where(match, grad_gate[g * padded : (g + 1) * padded], 0.0)
        line = jnp.sum(values, axis=0, keepdims=True)
        high = line.astype(bf16).astype(f32)
        tail = grad_out[(g + 1) * padded - 16 : (g + 1) * padded, :lanes_used]
        tail = jnp.where(row == spare, high, jnp.where(row == spare + 1, line - high, tail))
        grad_buffer[pl.ds((g + 1) * padded - 16, 16), :lanes_used] = tail.astype(bf16)
    depart(grad_buffer, outs[3 * chunks + 1])
    for copy in departures:
        copy.wait()


def expert_pass(facts, slots, grads, own, other, capacity, padded, lanes_used):
    rows, width = slots.shape
    units = own[0].shape[1]
    wide = (units + 127) // 128 * 128
    chunks = 1 if other is None else 2
    sources = list(own) + ([] if other is None else [other] * 3)
    anywhere = pl.BlockSpec(memory_space=pl.ANY)
    outs = pl.pallas_call(
        partial(expert_kernel, chunks, capacity, padded, lanes_used),
        grid_spec=pltpu.PrefetchScalarGridSpec(
            num_scalar_prefetch=1,
            grid=(1,),
            in_specs=[anywhere] * (2 + 3 * chunks),
            out_specs=[anywhere] * (3 * chunks + 2),
            scratch_shapes=[pltpu.VMEM((rows, width), bf16)] * 2
            + [pltpu.VMEM((3, chunks * wide, width), bf16), pltpu.VMEM((3 * chunks, rows, units), bf16)]
            + [pltpu.VMEM((rows, width), bf16)] * 2
            + [pltpu.SemaphoreType.DMA((2 + 3 * chunks,)), pltpu.SemaphoreType.DMA((3 * chunks + 2,))],
        ),
        out_shape=[jax.ShapeDtypeStruct((rows, units), bf16)] * (3 * chunks)
        + [jax.ShapeDtypeStruct((rows, width), bf16)] * 2,
        compiler_params=params(),
        cost_estimate=cost(15),
        name="expert_pass",
    )(facts, slots, grads, *sources)
    middles = [outs[3 * c : 3 * c + 3] for c in range(chunks)]
    return middles, outs[3 * chunks], outs[3 * chunks + 1]


def weight_body(count, packed, extra, facts, *refs):
    kinds = [refs[k * count : (k + 1) * count] for k in range(5)]
    outs = refs[5 * count + extra :]
    targets = outs[1:4] if packed else outs[:3]
    held, sems = refs[-6:-1], refs[-1]
    step = pl.program_id(0)
    slot = step % 2

    def fetch(index, side):
        for r in range(count):

            @pl.when(index == r)
            def _():
                for k in range(5):
                    pltpu.make_async_copy(kinds[k][r], held[k].at[side], sems.at[side, k]).start()

    @pl.when(step == 0)
    def _():
        fetch(step, slot)

    @pl.when(step + 1 < count)
    def _():
        fetch(step + 1, 1 - slot)

    for k in range(5):
        pltpu.make_async_copy(kinds[k][0], held[k].at[slot], sems.at[slot, k]).wait()

    @pl.when(step == 0)
    def _():
        for target in targets:
            target[...] = jnp.zeros_like(target)

    rows, grads = held[0][slot], held[1][slot]
    lefts = ((held[3], rows), (held[4], rows), (held[2], grads))
    for target, (left, right) in zip(targets, lefts):
        target[0] += mm(left[slot], right, TN)

    if packed:

        @pl.when(step == count - 1)
        def _():
            for i in range(3):
                outs[0][i] = targets[i][0].astype(bf16)


def weight_pass(facts, slots, grads, middles, before, local, packed):
    count = len(slots)
    rows, width = slots[0].shape
    units = middles[0][0].shape[1]
    anywhere = pl.BlockSpec(memory_space=pl.ANY)
    if packed:
        out_specs = [pl.BlockSpec((3, units, width), lambda i, f: (0, 0, 0))]
        out_shape = [jax.ShapeDtypeStruct((3, units, width), bf16)]
        totals = [pltpu.VMEM((1, units, width), f32)] * 3
    else:
        out_specs = [pl.BlockSpec((1, units, width), lambda i, f: (f[4], 0, 0))] * 3
        out_shape = [jax.ShapeDtypeStruct((local, units, width), f32)] * 3
        totals = []
    kinds = [list(slots), list(grads)] + [[middle[k] for middle in middles] for k in range(3)]
    body = partial(weight_body, count, packed, len(before))
    return pl.pallas_call(
        body,
        grid_spec=pltpu.PrefetchScalarGridSpec(
            num_scalar_prefetch=1,
            grid=(count,),
            in_specs=[anywhere] * (5 * count + len(before)),
            out_specs=out_specs,
            scratch_shapes=totals
            + [pltpu.VMEM((2, rows, width), bf16)] * 2
            + [pltpu.VMEM((2, rows, units), bf16)] * 3
            + [pltpu.SemaphoreType.DMA((2, 5))],
        ),
        out_shape=out_shape,
        input_output_aliases={1 + 5 * count + i: i for i in range(len(before))},
        compiler_params=params(),
        cost_estimate=cost(16),
        name="weight_pass",
    )(facts, *[array for kind in kinds for array in kind], *before)


def fill_kernel(facts, source, *refs):
    for i in range(3):
        refs[-3 + i][0] = source[i].astype(f32)


def weight_fill(facts, source, before):
    _, units, width = source.shape
    tile = units // 4
    anywhere = pl.BlockSpec(memory_space=pl.ANY)
    return pl.pallas_call(
        fill_kernel,
        grid_spec=pltpu.PrefetchScalarGridSpec(
            num_scalar_prefetch=1,
            grid=(4,),
            in_specs=[pl.BlockSpec((3, tile, width), lambda i, f: (0, i, 0))] + [anywhere] * 3,
            out_specs=[pl.BlockSpec((1, tile, width), lambda i, f: (f[6], i, 0))] * 3,
        ),
        out_shape=[jax.ShapeDtypeStruct(array.shape, f32) for array in before],
        input_output_aliases={2 + i: i for i in range(3)},
        compiler_params=params(),
        cost_estimate=cost(6.5),
        name="weight_fill",
    )(facts, source, *before)


def place_kernel(capacity, padded, block, local, turns, routes, rows, slots_out, wide_out, rows_out):
    experts_axis = block // padded
    tokens = rows.shape[0]
    experts = experts_axis * local
    number = lax.broadcasted_iota(jnp.int32, (experts, tokens), 0)
    picks = [number == routes[k : k + 1] for k in range(routes.shape[0])]
    named = picks[0]
    for pick in picks[1:]:
        named = named | pick
    earlier = lax.broadcasted_iota(jnp.int32, (tokens, tokens), 0) < lax.broadcasted_iota(
        jnp.int32, (tokens, tokens), 1
    )
    before = mm(named.astype(bf16), earlier.astype(bf16))
    places = []
    for k, pick in enumerate(picks):
        route = routes[k : k + 1]
        position = jnp.sum(jnp.where(pick, before, 0.0), axis=0, keepdims=True).astype(jnp.int32)
        owner = route // local
        turn = jnp.where(owner % 2 == 0, turns[:, 0:1], turns[:, 1:2])
        which = (route % local) ^ turn
        slot = which * block + owner * padded + position
        slots_out[k : k + 1] = jnp.where(position < capacity, slot, -1)
        slot = (owner * local + which) * padded + position
        places.append(jnp.where(position < capacity, slot, -1))
        wide_out[k : k + 1] = places[k]
    spots = lax.broadcasted_iota(jnp.int32, (local * block, tokens), 0)
    hot = spots == places[0]
    for slot in places[1:]:
        hot = hot | (spots == slot)
    rows_out[...] = mm(hot.astype(bf16), rows[...]).astype(bf16)


def place_rows(turns, routes, rows, capacity, padded, block, local):
    tops, tokens = routes.shape
    width = rows.shape[1]
    return pl.pallas_call(
        partial(place_kernel, capacity, padded, block, local),
        out_shape=[
            jax.ShapeDtypeStruct((tops, tokens), jnp.int32),
            jax.ShapeDtypeStruct((tops, tokens), jnp.int32),
            jax.ShapeDtypeStruct((local * block, width), bf16),
        ],
        compiler_params=pltpu.CompilerParams(vmem_limit_bytes=VMEM_BYTES),
        cost_estimate=cost(3.9),
        name="place_rows",
    )(turns, routes, rows)


def route_kernel(
    capacity, padded, mixed, w_proj, inputs, gain, router, routes, slots, resid, moe, probs, gates, *outs
):
    local, block = len(outs), outs[0].shape[0]
    tokens = inputs.shape[0]
    sums = inputs[...].astype(f32) + mm(mixed[...], w_proj[...])
    resid[...] = sums
    scale = lax.rsqrt(jnp.mean(sums * sums, axis=-1, keepdims=True) + 1e-06)
    low = (sums * scale * gain[...].astype(f32)).astype(bf16)
    moe[...] = low
    logits = mm(router[...], low, NT)
    grown = jnp.exp(logits - jnp.max(logits, axis=0, keepdims=True))
    share = grown / jnp.sum(grown, axis=0, keepdims=True)
    probs[...] = share
    number = lax.broadcasted_iota(jnp.int32, share.shape, 0)
    spots = lax.broadcasted_iota(jnp.int32, (local * block, tokens), 0)
    row = lax.broadcasted_iota(jnp.int32, (16, tokens), 0)
    hot = None
    lines = jnp.zeros((16, local * block), f32)
    for k in range(routes.shape[0]):
        gate = jnp.sum(jnp.where(number == routes[k : k + 1], share, 0.0), axis=0, keepdims=True)
        gates[k : k + 1] = gate
        high = gate.astype(bf16).astype(f32)
        both = jnp.where(row == 0, high, jnp.where(row == 1, gate - high, 0.0)).astype(bf16)
        mine = (spots == slots[k : k + 1]).astype(bf16)
        lines = lines + mm(both, mine, NT)
        hot = mine if hot is None else hot + mine
    filled = mm(hot, low).astype(bf16)
    spare = 16 - (padded - capacity)
    row = lax.broadcasted_iota(jnp.int32, (16, padded), 0)
    for j in range(local):
        outs[j][...] = filled[j * block : (j + 1) * block]
        for g in range(block // padded):
            at = j * block + g * padded
            tail = filled[at + padded - 16 : at + padded, :padded].astype(f32)
            line = lines[:, at : at + padded]
            tail = jnp.where(row == spare, line[0:1], jnp.where(row == spare + 1, line[1:2], tail))
            outs[j][pl.ds((g + 1) * padded - 16, 16), :padded] = tail.astype(bf16)


def route_rows(mixed, w_proj, inputs, gain, router, routes, slots, capacity, padded, block, local):
    tokens, width = inputs.shape
    tops = routes.shape[0]
    return pl.pallas_call(
        partial(route_kernel, capacity, padded),
        out_shape=[
            jax.ShapeDtypeStruct((tokens, width), f32),
            jax.ShapeDtypeStruct((tokens, width), bf16),
            jax.ShapeDtypeStruct((router.shape[0], tokens), f32),
            jax.ShapeDtypeStruct((tops, tokens), f32),
        ]
        + [jax.ShapeDtypeStruct((block, width), bf16)] * local,
        compiler_params=pltpu.CompilerParams(vmem_limit_bytes=VMEM_BYTES),
        cost_estimate=cost(6.4),
        name="route_rows",
    )(mixed, w_proj, inputs, gain.reshape(1, width), router, routes, slots)


def merge_kernel(
    capacity, padded, count, cotangent, resid, probs, moe, router, gain, w_proj, routes, slots, columns, *refs
):
    local = len(refs) - 5
    grads = refs[:local]
    grad_resid, grad_mixed, gain_grad, router_grad, branch_out = refs[local:]
    block = grads[0].shape[0]
    tokens = cotangent.shape[0]
    tops = routes.shape[0]
    spare = 16 - (padded - capacity)
    pieces = []
    for j in range(local):
        for g in range(block // padded):
            tail = grads[j][pl.ds((g + 1) * padded - 16, 16), : count * padded].astype(f32)
            line = tail[spare : spare + 1] + tail[spare + 1 : spare + 2]
            folded = line[:, :padded]
            for r in range(1, count):
                folded = folded + line[:, r * padded : (r + 1) * padded]
            pieces.append(folded)
    line = jnp.concatenate(pieces, axis=1)
    row = lax.broadcasted_iota(jnp.int32, (16, line.shape[1]), 0)
    high = line.astype(bf16).astype(f32)
    rest = line - high
    middle = rest.astype(bf16).astype(f32)
    stack = jnp.where(row == 0, high, jnp.where(row == 1, middle, jnp.where(row == 2, rest - middle, 0.0)))
    stack = stack.astype(bf16)
    share = probs[...]
    number = lax.broadcasted_iota(jnp.int32, share.shape, 0)
    spots = lax.broadcasted_iota(jnp.int32, (local * block, tokens), 0)
    grad_probs = jnp.zeros_like(share)
    for k in range(tops):
        picked = jnp.sum(mm(stack, (spots == slots[k : k + 1]).astype(bf16)), axis=0, keepdims=True)
        grad_probs = grad_probs + jnp.where(number == routes[k : k + 1], picked, 0.0)
    grad_logits = share * (grad_probs - jnp.sum(share * grad_probs, axis=0, keepdims=True))
    grad_logits = grad_logits.astype(bf16)
    router_grad[...] = mm(grad_logits, moe[...])
    grad_moe = mm(grad_logits, router[...], TN)
    spots = lax.broadcasted_iota(jnp.int32, (tokens, block), 1)
    for j in range(local):
        hot = None
        for k in range(tops):
            mine = spots + j * block == columns[:, k : k + 1]
            hot = mine if hot is None else hot | mine
        grad_moe = grad_moe + mm(hot.astype(bf16), grads[j][...])
    rows = resid[...]
    scale = lax.rsqrt(jnp.mean(rows * rows, axis=-1, keepdims=True) + 1e-06)
    normed = rows * scale
    gain_grad[...] = jnp.sum(grad_moe * normed, axis=0, keepdims=True)
    lifted = grad_moe * gain[...].astype(f32)
    spread = jnp.mean(lifted * normed, axis=-1, keepdims=True)
    back = cotangent[...].astype(f32) + scale * (lifted - normed * spread)
    grad_resid[...] = back
    branch = back.astype(bf16)
    grad_mixed[...] = mm(branch, w_proj[...], NT).astype(bf16)
    branch_out[...] = branch


def merge_rows(
    cotangent, resid, probs, moe, router, gain, w_proj, routes, slots, grads, capacity, padded, count
):
    tokens, width = cotangent.shape
    return pl.pallas_call(
        partial(merge_kernel, capacity, padded, count),
        out_shape=[
            jax.ShapeDtypeStruct((tokens, width), f32),
            jax.ShapeDtypeStruct((tokens, width), bf16),
            jax.ShapeDtypeStruct((1, width), f32),
            jax.ShapeDtypeStruct((router.shape[0], width), f32),
            jax.ShapeDtypeStruct((tokens, width), bf16),
        ],
        compiler_params=pltpu.CompilerParams(vmem_limit_bytes=VMEM_BYTES),
        cost_estimate=cost(7.4),
        name="merge_rows",
    )(
        cotangent, resid, probs, moe, router, gain.reshape(1, width), w_proj, routes, slots,
        jnp.transpose(slots), *grads,
    )


def blocks_kernel(
    local,
    facts,
    normed,
    normed_others,
    mixed,
    grad_query,
    grad_pair,
    grad_others,
    grad_near,
    branch,
    bias_grad,
    gain_grad,
    router_grad,
    near,
    far,
    near_right,
    far_right,
):
    step = pl.program_id(0)
    number = facts[3]
    group = step ^ (number // 8)
    share = (near.shape[1] - 8) // 4
    short = grad_near.shape[0] // 2
    own, own_short = normed[:local], normed[local:]

    def keyed(which):
        part = mm(own, grad_pair[which * local : (which + 1) * local], TN)
        part = part + mm(own_short, grad_near[which * short : (which + 1) * short], TN)
        for r in range(normed_others.shape[0] // local):
            at = (2 * r + which) * local
            part = part + mm(normed_others[r * local : (r + 1) * local], grad_others[at : at + local], TN)
        return part

    made = [mm(normed[...], grad_query[...], TN), keyed(0), keyed(1), mm(mixed[...], branch[...], TN)]
    made = [part.astype(bf16) for part in made]
    pairs, _, buckets = bias_grad.shape
    line = [bias_grad[p, h : h + 1, :] for p in range(pairs) for h in range(2)]
    line.append(jnp.zeros((1, 2 * near.shape[2] - 2 * pairs * buckets), f32))
    tail = jnp.zeros((24 - 2 - router_grad.shape[0], 2 * near.shape[2]), f32)
    small = jnp.concatenate(
        [jnp.concatenate(line, axis=1), gain_grad[...], router_grad[...], tail], axis=0
    )
    for s in range(8):
        spot = s ^ (number % 8)
        lines = [part[s * share : (s + 1) * share] for part in made]
        extra = jnp.zeros((8, 2 * near.shape[2]), f32)
        if s < 3:
            extra = jnp.where(group == 0, small[s * 8 : s * 8 + 8], extra)
        whole = jnp.concatenate(lines + [extra.astype(bf16)], axis=0)

        @pl.when(step < 2)
        def _():
            near[spot] = whole[:, : near.shape[2]]
            near_right[spot] = whole[:, near.shape[2] :]

        @pl.when(step >= 2)
        def _():
            far[spot] = whole[:, : near.shape[2]]
            far_right[spot] = whole[:, near.shape[2] :]


def weight_blocks(facts, lefts, rights, branch, bias_grad, gain_grad, router_grad, local):
    tokens, width = lefts[0].shape
    rows = 4 * width // 32 + 8
    cut = lambda count: pl.BlockSpec((count, width // 4), lambda i, f: (0, i ^ (f[3] // 8)))
    full = lambda count: pl.BlockSpec((count, width), lambda i, f: (0, 0))
    out = lambda which: pl.BlockSpec((8, rows, width // 2), which)
    return pl.pallas_call(
        partial(blocks_kernel, local),
        grid_spec=pltpu.PrefetchScalarGridSpec(
            num_scalar_prefetch=1,
            grid=(4,),
            in_specs=[cut(left.shape[0]) for left in lefts]
            + [full(right.shape[0]) for right in rights]
            + [
                full(tokens),
                pl.BlockSpec(bias_grad.shape, lambda i, f: (0, 0, 0)),
                full(1),
                full(router_grad.shape[0]),
            ],
            out_specs=[
                out(lambda i, f: (jnp.minimum(i, 1), 0, 0)),
                out(lambda i, f: (jnp.maximum(i - 2, 0), 0, 0)),
            ]
            * 2,
        ),
        out_shape=[jax.ShapeDtypeStruct((16, rows, width // 2), bf16)] * 4,
        compiler_params=params(),
        cost_estimate=cost(17),
        name="weight_blocks",
    )(facts, *lefts, *rights, branch, bias_grad, gain_grad, router_grad)


def unpack_kernel(facts, near, far, w_query, w_key, w_value, gain, gain_before, *refs):
    query, key, value, proj, top, router, gain_grad = refs[-7:]
    count = router.shape[0]
    step = pl.program_id(0)
    number = facts[3]
    group = step ^ (number // 8)
    share = (near.shape[1] - 8) // 4

    def spread(source):
        for s in range(8):
            block = source[s ^ (number % 8)].astype(f32)
            for which, out in enumerate((query, key, value, proj)):
                out[s * share : (s + 1) * share] = block[which * share : (which + 1) * share]
            if s < 3:

                @pl.when(group == 0)
                def _():
                    tail = block[4 * share :]
                    if s == 0:
                        top[...] = tail
                    low, high = max(s * 8, 2), min(s * 8 + 8, 2 + count)
                    router[low - 2 : high - 2] = tail[low - s * 8 : high - s * 8]

    @pl.when(step < 2)
    def _():
        spread(near)

    @pl.when(step >= 2)
    def _():
        spread(far)

    sums = query[...] * w_query[...].astype(f32)
    sums = sums + key[...] * w_key[...].astype(f32)
    sums = sums + value[...] * w_value[...].astype(f32)
    column = jnp.sum(sums, axis=-1, keepdims=True)
    size = column.shape[0]
    match = lax.broadcasted_iota(jnp.int32, (size, size), 0) == lax.broadcasted_iota(
        jnp.int32, (size, size), 1
    )
    line = jnp.sum(jnp.where(match, column, 0.0), axis=0, keepdims=True)
    gain_grad[...] = gain_before[...] + line / gain[...].astype(f32)


def unpack_blocks(facts, near, far, w_query, w_key, w_value, gain, gain_before, before, half, count):
    width = w_query.shape[0]
    wide = width // 2
    rows = near.shape[1]
    step = width // 4
    line = pl.BlockSpec((1, step), lambda i, f: (0, i ^ (f[3] // 8)))
    block = pl.BlockSpec((step, wide), lambda i, f: (i ^ (f[3] // 8), half))
    return pl.pallas_call(
        unpack_kernel,
        grid_spec=pltpu.PrefetchScalarGridSpec(
            num_scalar_prefetch=1,
            grid=(4,),
            in_specs=[
                pl.BlockSpec((8, rows, wide), lambda i, f: (jnp.minimum(i, 1), 0, 0)),
                pl.BlockSpec((8, rows, wide), lambda i, f: (jnp.maximum(i - 2, 0), 0, 0)),
                block,
                block,
                block,
                line,
                line,
            ]
            + [pl.BlockSpec(memory_space=pl.ANY)] * len(before),
            out_specs=[block] * 4 + [pl.BlockSpec((size, wide), lambda i, f: (0, half)) for size in (8, count)] + [line],
        ),
        out_shape=[jax.ShapeDtypeStruct((width, width), f32)] * 4
        + [jax.ShapeDtypeStruct((size, width), f32) for size in (8, count, 1)],
        input_output_aliases={8 + i: i for i in range(len(before))},
        compiler_params=params(),
        cost_estimate=cost(8),
        name="unpack_blocks",
    )(facts, near, far, w_query, w_key, w_value, gain.reshape(1, width), gain_before, *before)


def per_device(
    inputs,
    attn_gain,
    w_query,
    w_key,
    w_value,
    w_proj,
    rel_bias,
    moe_gain,
    w_router,
    w_gate,
    w_up,
    w_down,
    routes,
    long_buckets,
    short_buckets,
    long_lens,
    short_lens,
    cotangent,
):
    experts_axis = lax.axis_size("expert")
    tensor_axis = lax.axis_size("tensor")
    place = lax.axis_index("tensor")
    tok_count, width = inputs.shape
    top_count = routes.shape[1]
    short_len = (short_buckets.shape[0] + 1) // 2
    long_span = (long_buckets.shape[0] + 1) // 2
    long_local = tok_count - short_len
    bucket_count, heads = rel_bias.shape
    head_dim = width // heads
    experts = w_router.shape[1]
    local = experts // experts_axis
    capacity = (5 * tok_count * top_count + 4 * experts - 1) // (4 * experts)
    padded = (capacity + 2 + 15) // 16 * 16
    block = experts_axis * padded
    rel_table = rel_bias.astype(f32)
    here = lax.axis_index("expert")
    number = (here % 2) * 16 + place * 4 + here // 2
    paired = tensor_axis == 4 and local == 2
    routes_rows = jnp.transpose(routes)
    router = jnp.transpose(w_router)
    gate_turned = jnp.swapaxes(w_gate, 1, 2)
    up_turned = jnp.swapaxes(w_up, 1, 2)
    if paired:
        turns = jnp.stack([place % 2, place // 2]).astype(jnp.int32)
        which = jnp.where(here % 2 == 0, turns[0], turns[1])
        part_of = jnp.where(here % 2 == 0, turns[1], turns[0])
        shares = 2
    else:
        turns = jnp.zeros((2,), jnp.int32)
        which, part_of, shares = jnp.int32(0), place, tensor_axis
    facts = [place, long_lens[0], short_lens[0], number, which, part_of, 1 - which]
    facts = jnp.stack([jnp.asarray(fact, jnp.int32) for fact in facts])

    def trade(rows, other):
        pairs = []
        for e in range(experts_axis):
            mask = (2 if e % 2 == 0 else 1) if other else (1 if e % 2 == 0 else 2)
            pairs += [(e * tensor_axis + t, e * tensor_axis + (t ^ mask)) for t in range(tensor_axis)]
        return lax.ppermute(rows, ("expert", "tensor"), pairs)

    long_rows = inputs[:long_local]
    sources = [swap(long_rows, "tensor", r) for r in range(1, tensor_axis)]
    slots, wide_slots, grad_slots_in = place_rows(
        turns.reshape(1, 2), routes_rows, cotangent, capacity, padded, block, local
    )
    normed_low, normed_others, query, pair, others, near = project(
        inputs, sources, attn_gain, w_query, w_key, w_value, long_local
    )

    def by_expert(rows):
        split = rows.reshape(experts_axis, local, padded, width)
        return [split[:, j].reshape(block, width) for j in range(local)]

    def by_device(parts):
        split = [part.reshape(experts_axis, 1, padded, width) for part in parts]
        return jnp.concatenate(split, axis=1).reshape(local * block, width)

    grad_whole = over_experts(grad_slots_in)
    parts = (pair, others)
    if paired:
        other = pick_weights(facts, gate_turned, up_turned, w_down)
        other = trade(after(other, sources), False)

    reach = long_span + long_local
    first = long_span - long_local - long_local * place
    long_table = jnp.pad(long_buckets, (0, 1), constant_values=-1)
    long_hot = table_hot(lax.dynamic_slice_in_dim(long_table, first, reach, 0), bucket_count)
    short_hot = table_hot(jnp.pad(short_buckets, (0, 1), constant_values=-1), bucket_count)
    spread = lambda hot: jnp.einsum(
        "cb,bh->hc", hot, rel_table, precision=precise, preferred_element_type=f32
    )
    mixed, far_attend, near_attend = attend_forward(
        facts, query, parts, near, spread(long_hot), spread(short_hot),
        tensor_axis, long_local, head_dim,
    )
    resid, moe_low, probs, gates, *slots_in = route_rows(
        mixed, w_proj, inputs, moe_gain, router, routes_rows, slots, capacity, padded, block, local
    )

    own = (gate_turned, up_turned, w_down)
    lanes_used = shares * padded
    if paired:

        run = lambda rows, grads: expert_pass(
            facts, rows, grads, own, other, capacity, padded, lanes_used
        )
        grad_arrived = by_expert(after(grad_whole, slots_in))
        grads_b = trade(grad_arrived[1], False)
        grads_d = trade(grads_b, True)
        rows_b = over_experts(slots_in[1])
        rows_a = over_experts(after(slots_in[0], rows_b))
        rows_b = trade(after(rows_b, grads_b, grads_d), False)
        rows_d = trade(rows_b, True)
        grads_c = trade(after(grad_arrived[0], rows_d), True)
        pass_b = run(rows_b, grads_b)
        pass_d = run(after(rows_d, pass_b[1]), grads_d)
        rows_c = trade(after(rows_a, rows_d), True)
        pass_a = run(after(rows_a, pass_d[1], rows_c), grad_arrived[0])
        traded = add_low(pass_b[2], after(trade(pass_d[2], True), pass_a[1]))
        traded = trade(traded, False)
        pass_c = run(after(rows_c, pass_a[1]), grads_c)
        traded = after(traded, pass_c[1])
        traded_back = over_experts(traded)
        kept = add_low(pass_a[2], trade(after(pass_c[2], traded), True))
        grad_slots = [over_experts(after(kept, traded_back)), traded_back]

        passes = [pass_a, pass_c, pass_b, pass_d]
        slot_blocks = [rows_a, rows_c, rows_b, rows_d]
        grad_blocks = [grad_arrived[0], grads_c, grads_b, grads_d]
        (sent,) = weight_pass(
            facts, slot_blocks, grad_blocks, [after_all(made[0][1], pass_c[1]) for made in passes], (), local, True
        )
        weight_grads = weight_pass(
            facts, slot_blocks, grad_blocks, [after_all(made[0][0], sent) for made in passes], (), local, False
        )
        outs_d = trade(after(pass_d[1], traded), True)
        outs_c = trade(after(pass_c[1], kept, outs_d), True)
        outs_traded = trade(add_low(pass_b[1], outs_d), False)
        outs_kept = add_low(pass_a[1], outs_c)
        grad_slots[0] = after(grad_slots[0], weight_grads, outs_c, outs_traded)
        held_back = outs_traded
        sent = trade(after(sent, outs_traded), False)
        outs_back = over_experts(after(by_device([outs_kept, outs_traded]), grad_slots[0]))
    else:
        grad_blocks = [gather_parts(rows) for rows in by_expert(grad_whole)]
        slot_blocks = [gather_parts(over_experts(slots_in[j])) for j in range(local)]
        weight_grads, passes = (), []
        for j in range(local):
            facts_j = facts.at[4].set(j)
            passes.append(
                [
                    expert_pass(facts_j, rows, grads, own, None, capacity, padded, lanes_used)
                    for rows, grads in zip(slot_blocks[j], grad_blocks[j])
                ]
            )
            weight_grads = weight_pass(
                facts_j, slot_blocks[j], grad_blocks[j], [made[0][0] for made in passes[j]], weight_grads, local, False
            )
        send_back = lambda which: [
            over_experts(sum_parts([made[which] for made in passes[j]]).astype(bf16)) for j in range(local)
        ]
        grad_slots = send_back(2)
        outs_back = by_device(send_back(1))
        held_back = sent = grad_slots[0]

    grad_resid, grad_mixed, moe_gain_grad, router_grad, branch = merge_rows(
        cotangent, resid, probs, moe_low, router, moe_gain, w_proj, routes_rows, slots, grad_slots,
        capacity, padded, shares,
    )
    grad_mixed = after(grad_mixed, held_back)
    quick = experts_axis == 8 and tensor_axis == 4
    hots = (long_hot.astype(bf16), short_hot.astype(bf16))
    *attn_grads, bias_grad = attend_backward(
        facts, query, grad_mixed, parts, near, (far_attend, near_attend), hots, tensor_axis, long_local, head_dim
    )
    if quick:
        bias_grad = after(bias_grad, sent)
        made = weight_blocks(
            facts, (normed_low, normed_others, mixed), attn_grads, branch, bias_grad, moe_gain_grad, router_grad,
            long_local,
        )
        sums = [add_low(made[half], swap(made[half + 1], "expert", 1)) for half in (0, 2)]
        attn_grads = after_all(attn_grads, sums, outs_back)
    own_grads, near_grads, away = normed_grads(attn_grads, w_query, w_key, w_value, long_local, tensor_axis)
    if quick:
        sums = [ring_sum(plane_parts(part), in_plane).astype(bf16) for part in sums]
        away = after(away, sums)
    pieces = [own_grads] + [
        away[r * long_local : (r + 1) * long_local].astype(bf16) for r in range(tensor_axis - 1)
    ]
    if tensor_axis == 4:
        pieces = pieces[:3] + [pieces[3][: long_local // 2], pieces[3][long_local // 2 :]]
    summed = sum_parts(pieces)
    if quick:
        owns = [sum_depth(part) for part in sums]
        sums = [spread_depth(own) for own in owns]
        sent, outs_back, summed = after_all((sent, outs_back, summed), sums[0], owns[1])
        sums[1] = after(sums[1], summed)
    if paired:
        weight_grads = weight_fill(facts, sent, weight_grads)
    slot_places = jnp.arange(local * block, dtype=jnp.int32)
    outputs = resid
    for k in range(top_count):
        chosen = mm((wide_slots[k][:, None] == slot_places).astype(bf16), outs_back)
        outputs = outputs + gates[k][:, None] * chosen
    outputs = outputs.astype(bf16)
    grad_normed = jnp.concatenate([summed, near_grads], axis=0)
    inputs_wide = inputs.astype(f32)
    scale = lax.rsqrt(jnp.mean(inputs_wide * inputs_wide, axis=-1, keepdims=True) + 1e-06)
    normed = inputs_wide * scale
    lifted = grad_normed * attn_gain.astype(f32)
    inputs_grad = grad_resid + scale * (
        lifted - normed * jnp.mean(lifted * normed, axis=-1, keepdims=True)
    )
    if quick:
        unpack = partial(unpack_blocks, facts)
        weights = (w_query, w_key, w_value, attn_gain)
        one, two = sums
        by_x, by_y = in_plane(one, 0), in_plane(one, 1)
        half_x, half_y = after_all((by_x[:2], by_y[2:]), outputs, weight_grads, two)
        one = jnp.concatenate([one, by_x, by_y, in_plane(half_x, 1), in_plane(half_y, 0)], axis=0)
        first = unpack(one, swap(one, "expert", 1), *weights, jnp.zeros((1, width), f32), (), 0, experts)
        by_x, by_y = in_plane(two, 0), in_plane(two, 1)
        rest = after_all((in_plane(by_x[:2], 1), in_plane(by_y[2:], 0)), first[6], inputs_grad)
        two = jnp.concatenate([two, by_x, by_y] + rest, axis=0)
        second = unpack(two, swap(two, "expert", 1), *weights, first[6], first[:6], 1, experts)
        query_grad, key_grad, value_grad, proj_grad = second[:4]
        attn_gain_grad = second[6][0]
        small, router_sum = second[4], second[5]
    else:
        key_others = [slice(2 * r * long_local, (2 * r + 1) * long_local) for r in range(tensor_axis - 1)]
        value_others = [slice((2 * r + 1) * long_local, (2 * r + 2) * long_local) for r in range(tensor_axis - 1)]

        def keyed(index, spots):
            short = slice(index * short_len, (index + 1) * short_len)
            rows = slice(index * long_local, (index + 1) * long_local)
            lefts = jnp.concatenate([normed_low, normed_others], axis=0)
            rights = jnp.concatenate(
                [attn_grads[1][rows], attn_grads[3][short]] + [attn_grads[2][spot] for spot in spots], axis=0
            )
            return mm(lefts, rights, TN)

        rel_row = jnp.pad(bias_grad.reshape(1, -1), ((0, 0), (0, width - bias_grad.size)))
        small = jnp.concatenate([rel_row, moe_gain_grad, router_grad], axis=0)
        query_grad, key_grad, value_grad, proj_grad, small = lax.psum(
            (
                mm(normed_low, attn_grads[0], TN),
                keyed(0, key_others),
                keyed(1, value_others),
                mm(mixed, branch, TN),
                small,
            ),
            ("expert", "tensor"),
        )
        attn_gain_grad = jnp.sum(
            query_grad * w_query.astype(f32) + key_grad * w_key.astype(f32) + value_grad * w_value.astype(f32),
            axis=1,
        ) / attn_gain.astype(f32)
        router_sum = small[2:]
    rel_grad = jnp.transpose(small[0, : heads * bucket_count].reshape(heads, bucket_count))
    return (
        outputs,
        inputs_grad,
        attn_gain_grad,
        query_grad,
        key_grad,
        value_grad,
        proj_grad,
        rel_grad,
        small[1],
        jnp.transpose(router_sum),
        jnp.swapaxes(weight_grads[0], 1, 2),
        jnp.swapaxes(weight_grads[1], 1, 2),
        weight_grads[2],
    )


def solution(mesh):
    return jax.shard_map(
        per_device,
        mesh=mesh,
        in_specs=(
            P(("expert", "tensor"), None),
            P(),
            P(),
            P(),
            P(),
            P(),
            P(),
            P(),
            P(),
            P("expert", None, "tensor"),
            P("expert", None, "tensor"),
            P("expert", "tensor", None),
            P(("expert", "tensor"), None),
            P(),
            P(),
            P("expert"),
            P(("expert", "tensor")),
            P(("expert", "tensor"), None),
        ),
        out_specs=(
            P(("expert", "tensor"), None),
            P(("expert", "tensor"), None),
            P(),
            P(),
            P(),
            P(),
            P(),
            P(),
            P(),
            P(),
            P("expert", None, "tensor"),
            P("expert", None, "tensor"),
            P("expert", "tensor", None),
        ),
        check_vma=False,
    )
```
